128 devices in a mesh: tm: 16 (over y, z_hi, core), space: 8 (over z_lo, x).
Axes of the slice: x: 4, y: 4, z: 4 (z_hi: 2, z_lo: 2; z = z_hi * 2 + z_lo), core: 2. Of those that a mesh axis runs over, the one named last changes fastest.
Arguments:
- slab_starts: float32 [16, 2, 16, 128, 256], P('tm', None, 'space'), may hold values from 0 to 0.5
- slab_nodes: float32 [16, 2, 2, 16, 128, 256], P('tm', None, None, 'space'), may hold values from 0 to 0.5
- first_slab: int32 [1], replicated, may hold values from 0 to 15
- converged: int32 [2], replicated, may hold values 0 or 1
Outputs:
- new_starts: float32 [16, 2, 16, 128, 256], P('tm', None, 'space')
- new_nodes: float32 [16, 2, 2, 16, 128, 256], P('tm', None, None, 'space')
The draws below stay inside these ranges and needn't reach their ends.
All inputs are finite; a program needn't handle non-finite values.
Results may differ from the reference program's by a relative error of at most 0.00002.
Values sent between devices are 32-bit elements; how exact they have to be, the bound alone decides.
No kernel may reach another device: no remote copies, remote signals or barrier semaphores. Data moves between devices by JAX's collectives and lax.ppermute only.
A program may use at most 64 MiB of HBM per device.

```python
import jax
import jax.numpy as jnp
from jax import lax

CY = 128
CZ = 256
ITERS = 2
SLABS = 16
NX = 16


def plant(result, own_key, least, top_value):
    longest = result.shape.index(max(result.shape))
    spots = []
    for shift in (0, 1):
        where = [jax.random.randint(jax.random.fold_in(own_key, axis), (), 0, length) for axis, length in enumerate(result.shape)]
        where[longest] = (where[longest] + shift) % result.shape[longest]
        spots.append(tuple(where))
    return result.at[spots[0]].set(least).at[spots[1]].set(top_value)


def block_scale(key, extent, shards, low, largest):
    def one(axis_at, parts):
        steps = jax.random.uniform(jax.random.fold_in(jax.random.fold_in(key, 6), axis_at), (parts,), jnp.float32, low / len(shards), largest / len(shards))
        return jnp.repeat(jnp.exp(steps), extent[axis_at] // parts).reshape((-1,) + (1,) * (len(extent) - axis_at - 1))

    level = one(*shards[0])
    for cut in shards[1:]:
        level = level * one(*cut)
    return level


def setup_inputs(seed: int = 0) -> dict:
    splits = jax.random.split(jax.random.key(seed), 5)
    slab_starts = jnp.clip(0.5 * jax.random.uniform(splits[0], (SLABS, 2, NX, CY, CZ), jnp.float32) ** block_scale(splits[0], (SLABS, 2, NX, CY, CZ), ((0, 16), (2, 8)), -0.2, 0.2), 0.0, 0.5)
    slab_nodes = jnp.clip(0.5 * jax.random.uniform(splits[1], (SLABS, 2, 2, NX, CY, CZ), jnp.float32) ** block_scale(splits[1], (SLABS, 2, 2, NX, CY, CZ), ((0, 16), (3, 8)), -0.2, 0.2), 0.0, 0.5)
    first_slab = jax.random.randint(splits[2], (1,), 0, SLABS).astype(jnp.int32)
    converged = plant((jax.random.randint(splits[3], (ITERS,), 0, 2) < 1).astype(jnp.int32), jax.random.fold_in(splits[3], 1), 0, 1)
    return {"slab_starts": slab_starts, "slab_nodes": slab_nodes, "first_slab": first_slab, "converged": converged}


slab_step = 0.5
spread_p = 0.2
spread_v = 0.1
feed_rate = 0.04
kill_rate = 0.06
weight_end = 5.0 / 24.0
weight_mid = 1.0 / 3.0
weight_far = 1.0 / 24.0


def tendency(field):
    padded = jnp.pad(field, ((0, 0), (1, 1), (1, 1), (1, 1)))
    interior = padded[:, 1:-1, 1:-1, 1:-1]
    beside = padded[:, 2:, 1:-1, 1:-1] + padded[:, :-2, 1:-1, 1:-1]
    beside = beside + padded[:, 1:-1, 2:, 1:-1] + padded[:, 1:-1, :-2, 1:-1]
    beside = beside + padded[:, 1:-1, 1:-1, 2:] + padded[:, 1:-1, 1:-1, :-2]
    laplace_term = beside - 6.0 * interior
    depleted = interior[0]
    catalyst = interior[1]
    reaction = (1.0 - depleted) * catalyst * catalyst
    rate_p = spread_p * laplace_term[0] + reaction - feed_rate * depleted
    rate_v = spread_v * laplace_term[1] + reaction - (feed_rate + kill_rate) * catalyst
    return jnp.stack([rate_p, rate_v])


def sweep(pair):
    start_value, old_nodes = pair
    rate_start = tendency(start_value)
    rate_one = tendency(old_nodes[0])
    rate_two = tendency(old_nodes[1])
    node_one = start_value + slab_step * (weight_end * rate_start + weight_mid * rate_one - weight_far * rate_two)
    rate_new = tendency(node_one)
    node_two = node_one + 0.5 * slab_step * (rate_new - rate_one) + slab_step * (-weight_far * rate_start + weight_mid * rate_one + weight_end * rate_two)
    correction = node_two - (start_value + slab_step * rate_start)
    return node_one, node_two, correction


def reference(slab_starts, slab_nodes, first_slab, converged):
    leader = first_slab[0].astype(jnp.int32)
    for iteration in range(ITERS):
        conv_flag = converged[iteration]
        node_one, node_two, correction = lax.map(sweep, (slab_starts, slab_nodes))
        current = lax.dynamic_index_in_dim(slab_starts, leader, 0, keepdims=False)
        updated = slab_starts
        for position in range(1, SLABS + 1):
            source = jnp.mod(leader + position - 1, SLABS).astype(jnp.int32)
            proposal = current + slab_step * tendency(current) + lax.dynamic_index_in_dim(correction, source, 0, keepdims=False)
            if position < SLABS:
                target = jnp.mod(leader + position, SLABS).astype(jnp.int32)
                updated = lax.dynamic_update_index_in_dim(updated, proposal, target, 0)
                current = proposal
            else:
                newest = proposal
        stacked = jnp.stack([node_one, node_two], axis=1)
        old_first = lax.dynamic_index_in_dim(updated, leader, 0, keepdims=False)
        first_value = jnp.where(conv_flag > 0, newest, old_first)
        updated = lax.dynamic_update_index_in_dim(updated, first_value, leader, 0)
        old_pair = lax.dynamic_index_in_dim(stacked, leader, 0, keepdims=False)
        first_pair = jnp.where(conv_flag > 0, jnp.stack([newest, newest]), old_pair)
        stacked = lax.dynamic_update_index_in_dim(stacked, first_pair, leader, 0)
        slab_starts = updated
        slab_nodes = stacked
        leader = jnp.mod(leader + conv_flag, SLABS).astype(jnp.int32)
    return slab_starts, slab_nodes
```

```python
import functools

import jax
import jax.numpy as jnp
from jax import lax
from jax.experimental import pallas as pl
from jax.experimental.pallas import tpu as pltpu
from jax.sharding import PartitionSpec as P

SLABS = 16
NX = 16
TILES_Y = 8
TILES_Z = 16
EDGE = 16
RIM = 8
BLOCK = 6
H = 0.5
AXES = ("tm", "space")
F32 = jnp.float32
VMEM_LIMIT = 48 * 1024 * 1024
PLANE = (8, 128)


def device_of(i, j):
    i, j = i % TILES_Y, j % TILES_Z
    zb, x = (0, i) if i < 4 else (1, 7 - i)
    cj = j // 2
    core = (j % 2) ^ (cj % 2)
    za, y = (0, cj) if cj < 4 else (1, 7 - cj)
    zl = za ^ zb
    return (y * 4 + za * 2 + core) * 8 + zl * 4 + x


def own_tile():
    tm, space = lax.axis_index("tm"), lax.axis_index("space")
    y, za, core = tm // 4, (tm // 2) % 2, tm % 2
    zl, x = space // 4, space % 4
    zb = za ^ zl
    ti = jnp.where(zb == 0, x, 7 - x)
    cj = jnp.where(za == 0, y, 7 - y)
    return ti, 2 * cj + (core ^ (cj % 2))


def roll(v, by, axis):
    by %= v.shape[axis]
    return v if by == 0 else pltpu.roll(v, by, axis)


def lanes():
    return lax.broadcasted_iota(jnp.int32, PLANE, 1)


def rows():
    return lax.broadcasted_iota(jnp.int32, PLANE, 0)


def spread_kernel(start_ref, one_ref, two_ref, out_ref, padded):
    lane = lanes()
    column, part = lane % 32, lane // 32
    zero = jnp.zeros(PLANE, F32)
    for half in range(2):
        padded[half, 0:RIM] = zero
        padded[half, RIM + 128 : RIM + 136] = zero
    for array, ref in enumerate((start_ref, one_ref, two_ref)):
        for half in range(2):
            at = (0,) * (len(ref.shape) - 2) + (slice(None), slice(128 * half, 128 * half + 128))
            padded[half, RIM : RIM + 128] = ref[at]

        def tile_row(ti):
            rolled = {}

            def piece(q, half, tj):
                by = (32 * q - EDGE * tj + RIM) % 128
                if (q, half, by) not in rolled:
                    block = padded[half, pl.ds(EDGE * ti + q, 8, stride=4)]
                    rolled[q, half, by] = roll(block, by, 1)
                return rolled[q, half, by]

            for tj in range(TILES_Z):
                value = None
                for q in range(4):
                    if tj == 7:
                        v = jnp.where(column < 24, piece(q, 0, tj), piece(q, 1, tj))
                    elif tj == 8:
                        v = jnp.where(column < 8, piece(q, 0, tj), piece(q, 1, tj))
                    else:
                        v = piece(q, tj // 8, tj)
                    value = v if q == 0 else jnp.where(part == q, v, value)
                if tj == 0:
                    value = jnp.where(column < 8, 0.0, value)
                if tj == 15:
                    value = jnp.where(column < 24, value, 0.0)
                out_ref[device_of(ti, tj), array, 0, 0] = value

        for ti in range(TILES_Y):
            tile_row(ti)


def spread(starts, nodes):
    plane = (1, 1, 128, 256)
    return pl.pallas_call(
        spread_kernel,
        grid=(2, 2),
        in_specs=[
            pl.BlockSpec(plane, lambda f, x: (f, x, 0, 0)),
            pl.BlockSpec((1,) + plane, lambda f, x: (0, f, x, 0, 0)),
            pl.BlockSpec((1,) + plane, lambda f, x: (1, f, x, 0, 0)),
        ],
        out_specs=pl.BlockSpec((128, 3, 1, 1, 8, 128), lambda f, x: (0, 0, f, x, 0, 0)),
        out_shape=jax.ShapeDtypeStruct((128, 3, 2, 2, 8, 128), F32),
        scratch_shapes=[pltpu.VMEM((2, 144, 128), F32)],
        compiler_params=pltpu.CompilerParams(vmem_limit_bytes=VMEM_LIMIT),
        name="spread",
    )(starts, nodes, nodes)


def collect_kernel(in_ref, starts_ref, nodes_ref, planes):
    lane, row = lanes(), rows()
    block = lane // 16
    for array in range(3):
        for ti in range(0, TILES_Y, 2):
            for half in range(2):
                halves = []
                for i in (ti, ti + 1):
                    whole = [None] * 8
                    for t in range(8):
                        v = in_ref[device_of(i, 8 * half + t), array]
                        for k in range(8):
                            moved = roll(v, 16 * (t - k), 1)
                            whole[k] = moved if t == 0 else jnp.where(block == t, moved, whole[k])
                    halves.append(whole)
                for q in range(4):
                    for xp in range(2):
                        low, high = halves[0][2 * q + xp], halves[1][2 * q + xp]
                        fields = (
                            jnp.where(row < 4, low, roll(high, 4, 0)),
                            jnp.where(row < 4, roll(low, 4, 0), high),
                        )
                        for f in range(2):
                            planes[f, xp, half, pl.ds(EDGE * ti + q, 8, stride=4)] = fields[f]
        for f in range(2):
            for xp in range(2):
                for half in range(2):
                    where = (slice(None), slice(128 * half, 128 * half + 128))
                    if array == 0:
                        starts_ref[(f, xp) + where] = planes[f, xp, half]
                    else:
                        nodes_ref[(array - 1, f, xp) + where] = planes[f, xp, half]


def collect(tiles):
    return pl.pallas_call(
        collect_kernel,
        out_shape=(
            jax.ShapeDtypeStruct((2, 2, 128, 256), F32),
            jax.ShapeDtypeStruct((2, 2, 2, 128, 256), F32),
        ),
        in_specs=[pl.BlockSpec(memory_space=pltpu.VMEM)],
        out_specs=(pl.BlockSpec(memory_space=pltpu.VMEM),) * 2,
        scratch_shapes=[pltpu.VMEM((2, 2, 2, 128, 128), F32)],
        compiler_params=pltpu.CompilerParams(vmem_limit_bytes=VMEM_LIMIT),
        name="collect",
    )(tiles)


class Tile:
    def __init__(self, scalars):
        lane, row = lanes(), rows()
        self.lane, self.row = lane, row
        self.not_last, self.not_first = lane < 96, lane >= 32
        y = EDGE * scalars[3] - RIM + 4 * row + lane // 32
        z = EDGE * scalars[4] - RIM + lane % 32
        self.inside = (y >= 0) & (y < 128) & (z >= 0) & (z < 256)

    def around(self, v):
        up, down = roll(v, -32, 1), roll(v, 32, 1)
        up = jnp.where(self.not_last, up, roll(up, -1, 0))
        down = jnp.where(self.not_first, down, roll(down, 1, 0))
        return (roll(v, -1, 1) + roll(v, 1, 1)) + (up + down)

    def tendency(self, load, x):
        mid = [load(f, x) for f in range(2)]
        total = []
        for f in range(2):
            s = self.around(mid[f])
            if x > 0:
                s = s + load(f, x - 1)
            if x < NX - 1:
                s = s + load(f, x + 1)
            total.append(s)
        p, v = mid
        reaction = (1.0 - p) * (v * v)
        rate_p = 0.2 * total[0] + (reaction - 1.24 * p)
        rate_v = 0.1 * total[1] + (reaction - 0.7 * v)
        return (jnp.where(self.inside, rate_p, 0.0), jnp.where(self.inside, rate_v, 0.0)), mid


def sweep_kernel(first, scalars, in_ref, out_ref, one, two, ahead, rate):
    tile = Tile(scalars)

    def old(array):
        return lambda f, x: in_ref[0, x // 2, array, f, x % 2]

    for x in range(NX):
        f0, y0 = tile.tendency(old(0), x)
        f1, _ = tile.tendency(old(1), x)
        f2, _ = tile.tendency(old(2), x)
        for f in range(2):
            one[f, x] = y0[f] + (5 * H / 24) * f0[f] + ((H / 3) * f1[f] - (H / 24) * f2[f])
            out_ref[0, 0, f, x] = (H / 6) * (f1[f] + f2[f]) - (5 * H / 6) * f0[f]
            ahead[f, x] = y0[f] + H * f0[f]
    for x in range(NX):
        r1, _ = tile.tendency(lambda f, x: one[f, x], x)
        for f in range(2):
            correction = out_ref[0, 0, f, x] + (H / 2) * r1[f]
            out_ref[0, 0, f, x] = correction
            two[f, x] = ahead[f, x] + correction
            rate[f, x] = r1[f]
    for x in range(NX):
        r2, _ = tile.tendency(lambda f, x: two[f, x], x)
        for f in range(2):
            r1 = rate[f, x]
            out_ref[0, 1, f, x] = (H / 3) * r1 - (H / 24) * r2[f]
            out_ref[0, 2, f, x] = (H / 6) * (r1 + r2[f])


def sweep(scalars, tiles, first, count):
    def slab(i, s):
        return (lax.rem(s[0] + (first + i), SLABS), 0, 0, 0, 0, 0, 0)

    planes = pltpu.VMEM((2, NX, 8, 128), F32)
    return pl.pallas_call(
        functools.partial(sweep_kernel, first),
        grid_spec=pltpu.PrefetchScalarGridSpec(
            num_scalar_prefetch=1,
            grid=(count,),
            in_specs=[pl.BlockSpec((1, 8, 3, 2, 2, 8, 128), slab)],
            out_specs=pl.BlockSpec((1, 3, 2, NX, 8, 128), lambda i, s: (i, 0, 0, 0, 0, 0)),
            scratch_shapes=[planes] * 4,
        ),
        out_shape=jax.ShapeDtypeStruct((count, 3, 2, NX, 8, 128), F32),
        compiler_params=pltpu.CompilerParams(vmem_limit_bytes=VMEM_LIMIT),
        cost_estimate=pl.CostEstimate(flops=count * 5 * 32 * 1024 * 40, bytes_accessed=count * 1200000, transcendentals=0),
        name=f"sweep_{first}",
    )(scalars, tiles)


def core_pack(tile, load, pair):
    left = tile.lane % 32 < 16
    packed = [jnp.where(left, roll(load(f, 2 * pair), -8, 1), roll(load(f, 2 * pair + 1), 8, 1)) for f in range(2)]
    return jnp.where(tile.row < 4, roll(packed[0], -2, 0), roll(packed[1], 2, 0))


def chain_steps(tile, scalars, first, count, sweeps, z, late, corr, one, two, ahead, packs):
    take_first = scalars[1] > 0

    def step(p, at, final=False):
        now, other = p % 2, (p + 1) % 2
        reset = (p == 0) | ((p == 1) & take_first)
        for x in range(NX):
            fl, l = tile.tendency(lambda f, x: late[other, f, x], x)
            f0, y0 = tile.tendency(lambda f, x: z[now, f, x], x)
            for f in range(2):
                late[now, f, x] = jnp.where(reset, y0[f], l[f] + H * fl[f] + corr[f, x])
                g = y0[f] + H * f0[f]
                ahead[f, x] = g
                if final:
                    one[f, x] = y0[f] + (H / 2) * f0[f]
                    two[f, x] = (-H / 2) * f0[f]
                else:
                    z[other, f, x] = g + sweeps[at, 0, f, x]
                    one[f, x] = y0[f] + (5 * H / 24) * f0[f] + sweeps[at, 1, f, x]
                    two[f, x] = sweeps[at, 2, f, x] - (5 * H / 6) * f0[f]
        for x in range(NX):
            f1, _ = tile.tendency(lambda f, x: one[f, x], x)
            for f in range(2):
                c = two[f, x] + (H / 2) * f1[f]
                corr[f, x] = c
                two[f, x] = ahead[f, x] + c
        for pair in range(8):
            packs[at, pair, 0] = core_pack(tile, lambda f, x: late[now, f, x], pair)
            packs[at, pair, 1] = core_pack(tile, lambda f, x: one[f, x], pair)
            packs[at, pair, 2] = core_pack(tile, lambda f, x: two[f, x], pair)

    def looped(at, carry):
        step(first + at, at)
        return carry

    lax.fori_loop(0, count, looped, 0)
    return step


def send_out(tile, end, z, late, corr, state_ref, low_ref, high_ref):
    now, before = end % 2, (end + 1) % 2
    loads = (lambda f, x: z[now, f, x], lambda f, x: late[before, f, x], lambda f, x: corr[f, x])
    row = tile.row
    for k, load in enumerate(loads):
        for f in range(2):
            for x in range(NX):
                state_ref[k, f, x] = load(f, x)
        for m in range(4):
            a, b = core_pack(tile, load, 2 * m), core_pack(tile, load, 2 * m + 1)
            low = jnp.where(row < 2, a, jnp.where(row < 4, roll(a, -2, 0), jnp.where(row < 6, roll(b, 4, 0), roll(b, 2, 0))))
            high = jnp.where(row < 2, roll(a, -2, 0), jnp.where(row < 4, roll(a, -4, 0), jnp.where(row < 6, roll(b, 2, 0), b)))
            low_ref[4 * k + m] = low
            high_ref[4 * k + m] = high


def take_in(tile, start, z, late, corr, state_ref, got):
    row, column = tile.row, tile.lane % 32
    now, before = start % 2, (start + 1) % 2
    own = (row >= 2) & (row < 6)

    def place(v, at, to):
        return roll(v, to - at, 0)

    def tall(dj, k, f, pair):
        at, where = 4 * (pair % 2) + 2 * f, 4 * k + pair // 2
        top = place(got[-1, dj][where], at, 0)
        bottom = place(got[1, dj][where], at, 6)
        if dj == 0:
            return jnp.where(row < 2, top, bottom)
        low = place(got[0, dj][where], at, 2)
        high = place(got[0, dj][12 + where], at, 4)
        return jnp.where(row < 2, top, jnp.where(row < 4, low, jnp.where(row < 6, high, bottom)))

    for k in range(3):
        for f in range(2):
            for pair in range(8):
                left, mid, right = (tall(dj, k, f, pair) for dj in (-1, 0, 1))
                for xp in range(2):
                    x = 2 * pair + xp
                    centre = jnp.where(own, state_ref[k, f, x], roll(mid, 8 - 16 * xp, 1))
                    v = jnp.where(
                        column < 8,
                        roll(left, -8 - 16 * xp, 1),
                        jnp.where(column < 24, centre, roll(right, 24 - 16 * xp, 1)),
                    )
                    v = jnp.where(tile.inside, v, 0.0)
                    if k == 0:
                        z[now, f, x] = v
                    elif k == 1:
                        late[before, f, x] = v
                    else:
                        corr[f, x] = v


AROUND = [(di, dj) for di in (-1, 0, 1) for dj in (-1, 0, 1) if (di, dj) != (0, 0)]


def chain_kernel(first, count, scalars, sweeps, *refs):
    tile = Tile(scalars)
    last = first + count >= SLABS
    z, late, corr, one, two, ahead = refs[-6:]
    refs = refs[:-6]
    if first == 0:
        start_ref, refs = refs[0], refs[1:]
        for f in range(2):
            for x in range(NX):
                z[0, f, x] = start_ref[0, x // 2, 0, f, x % 2]
    else:
        got = dict(zip(AROUND, refs[1:9], strict=True))
        take_in(tile, first, z, late, corr, refs[0], got)
        refs = refs[9:]
    work = (z, late, corr, one, two, ahead)
    if not last:
        packs, state_ref, low_ref, high_ref = refs
        chain_steps(tile, scalars, first, count, sweeps, *work, packs)
        send_out(tile, first + count, z, late, corr, state_ref, low_ref, high_ref)
        return
    earlier, (out_ref, packs) = refs[:-2], refs[-2:]
    step = chain_steps(tile, scalars, first, count, sweeps, *work, packs)
    step(SLABS, count, final=True)
    end = SLABS % 2
    for x in range(NX):
        fl, l = tile.tendency(lambda f, x: late[end, f, x], x)
        for f in range(2):
            one[f, x] = l[f] + H * fl[f] + corr[f, x]
    leader, conv_one, conv_two = scalars[0], scalars[1] > 0, scalars[2] > 0

    def put(p, source):
        slab = lax.rem(leader + p, SLABS)
        for pair in range(8):
            for array in range(3):
                out_ref[slab * 8 + pair, array] = source(pair, array)

    for b, ref in enumerate(earlier):
        def move(i, carry, b=b, ref=ref):
            put(b * BLOCK + i, lambda pair, array: ref[i, pair, array])
            return carry

        lax.fori_loop(0, BLOCK, move, 0)

    def move_last(i, carry):
        put(first + i, lambda pair, array: packs[i, pair, array])
        return carry

    lax.fori_loop(0, count, move_last, 0)

    @pl.when(conv_one)
    def _():
        put(0, lambda pair, array: packs[count, pair, array])

    @pl.when(conv_two & conv_one)
    def _():
        put(1, lambda pair, array: core_pack(tile, lambda f, x: one[f, x], pair))

    @pl.when(conv_two & jnp.logical_not(conv_one))
    def _():
        put(0, lambda pair, array: packs[count, pair, 0])


def chain(scalars, first, count, sweeps, inputs, in_specs):
    last = first + count >= SLABS
    vmem = pl.BlockSpec(memory_space=pltpu.VMEM)
    if last:
        out_shape = jax.ShapeDtypeStruct((128, 3, 8, 128), F32)
        out_specs = vmem
        scratch = [pltpu.VMEM((count + 1, 8, 3, 8, 128), F32)]
    else:
        out_shape = (
            jax.ShapeDtypeStruct((count, 8, 3, 8, 128), F32),
            jax.ShapeDtypeStruct((3, 2, NX, 8, 128), F32),
            jax.ShapeDtypeStruct((12, 8, 128), F32),
            jax.ShapeDtypeStruct((12, 8, 128), F32),
        )
        out_specs = (vmem,) * 4
        scratch = []
    planes, double = pltpu.VMEM((2, NX, 8, 128), F32), pltpu.VMEM((2, 2, NX, 8, 128), F32)
    return pl.pallas_call(
        functools.partial(chain_kernel, first, count),
        grid_spec=pltpu.PrefetchScalarGridSpec(
            num_scalar_prefetch=1,
            grid=(1,),
            in_specs=[vmem] + in_specs,
            out_specs=out_specs,
            scratch_shapes=scratch + [double, double, planes, planes, planes, planes],
        ),
        out_shape=out_shape,
        compiler_params=pltpu.CompilerParams(vmem_limit_bytes=VMEM_LIMIT),
        name=f"chain_{first}",
    )(scalars, sweeps, *inputs)


def exchange(low, high):
    both = jnp.concatenate([low, high])
    got = []
    for di, dj in AROUND:
        payload = both if di == 0 else (high if di < 0 else low)
        pairs = [(device_of(i + di, j + dj), device_of(i, j)) for i in range(TILES_Y) for j in range(TILES_Z)]
        got.append(lax.ppermute(payload, AXES, pairs))
    return got


def body(slab_starts, slab_nodes, first_slab, converged):
    ti, tj = own_tile()
    scalars = jnp.stack([first_slab[0], converged[0], converged[1], ti.astype(jnp.int32), tj.astype(jnp.int32)])
    vmem = pl.BlockSpec(memory_space=pltpu.VMEM)
    chunks = spread(slab_starts[0], slab_nodes[0])
    tiles = lax.all_to_all(chunks.reshape(128, 96, 128), AXES, 0, 0, tiled=True)
    tiles = tiles.reshape(SLABS, 8, 3, 2, 2, 8, 128)

    sweeps = sweep(scalars, tiles, 0, BLOCK)
    start_spec = pl.BlockSpec((1, 8, 1, 2, 2, 8, 128), lambda i, s: (lax.rem(s[0], SLABS), 0, 0, 0, 0, 0, 0))
    packs_a, state, low, high = chain(scalars, 0, BLOCK, sweeps, [tiles], [start_spec])
    got = exchange(low, high)
    sweeps = sweep(scalars, tiles, BLOCK, BLOCK)
    last_sweeps = sweep(scalars, tiles, 2 * BLOCK, SLABS - 2 * BLOCK)
    packs_b, state, low, high = chain(scalars, BLOCK, BLOCK, sweeps, [state, *got], [vmem] * 9)
    got = exchange(low, high)
    out = chain(
        scalars, 2 * BLOCK, SLABS - 2 * BLOCK, last_sweeps, [state, *got, packs_a, packs_b], [vmem] * 11
    )
    out = lax.all_to_all(out.reshape(128, 24, 128), AXES, 0, 0, tiled=True)
    starts, nodes = collect(out.reshape(128, 3, 8, 128))
    return starts[None], nodes[None]


def solution(mesh):
    slab_spec = P("tm", None, "space", None, None)
    node_spec = P("tm", None, None, "space", None, None)
    return jax.shard_map(
        body,
        mesh=mesh,
        in_specs=(slab_spec, node_spec, P(), P()),
        out_specs=(slab_spec, node_spec),
        check_vma=False,
    )
```

```python
import functools

import jax
import jax.numpy as jnp
from jax import lax
from jax.experimental import pallas as pl
from jax.experimental.pallas import tpu as pltpu
from jax.sharding import PartitionSpec as P

SLABS = 16
TILES_Y = 8
TILES_Z = 16
EDGE = 16
RIM = 8
BLOCK = 6
H = 0.5
AXES = ("tm", "space")
F32 = jnp.float32
VMEM_LIMIT = 40 * 1024 * 1024
SHAPE = (8, 128)
SLAB_ROWS = 192
AROUND = [(di, dj) for di in (-1, 0, 1) for dj in (-1, 0, 1) if (di, dj) != (0, 0)]


def device_of(i, j):
    i, j = i % TILES_Y, j % TILES_Z
    zb, x = (0, i) if i < 4 else (1, 7 - i)
    cj = j // 2
    core = (j % 2) ^ (cj % 2)
    za, y = (0, cj) if cj < 4 else (1, 7 - cj)
    zl = za ^ zb
    return (y * 4 + za * 2 + core) * 8 + zl * 4 + x


def own_tile():
    tm, space = lax.axis_index("tm"), lax.axis_index("space")
    y, za, core = tm // 4, (tm // 2) % 2, tm % 2
    zl, x = space // 4, space % 4
    zb = za ^ zl
    ti = jnp.where(zb == 0, x, 7 - x)
    cj = jnp.where(za == 0, y, 7 - y)
    return ti, 2 * cj + (core ^ (cj % 2))


def roll(v, by, axis=1):
    by %= v.shape[axis]
    return v if by == 0 else pltpu.roll(v, by, axis)


def lanes():
    return lax.broadcasted_iota(jnp.int32, SHAPE, 1)


def rows():
    return lax.broadcasted_iota(jnp.int32, SHAPE, 0)


def swap_bits(arrays, pairs):
    arrays, lane = list(arrays), lanes()
    for index_bit, lane_bit in pairs:
        step, low = 1 << lane_bit, (lane >> lane_bit) % 2 == 0
        for a in range(len(arrays)):
            b = a | (1 << index_bit)
            if a != b:
                u, v = arrays[a], arrays[b]
                arrays[a] = jnp.where(low, u, roll(v, step))
                arrays[b] = jnp.where(low, roll(u, -step), v)
    return arrays


def turn_pairs(v):
    v = roll(v, 4, 0)
    return jnp.where(rows() // 2 % 2 == 0, roll(v, -2, 0), roll(v, 2, 0))


def spread_kernel(starts_ref, nodes_ref, out_ref, planes):
    for array in range(3):
        for f in range(2):
            for xp in range(2):
                for half in range(2):
                    z = slice(128 * half, 128 * half + 128)
                    planes[f, xp, half] = starts_ref[f, xp, :, z] if array == 0 else nodes_ref[array - 1, f, xp, :, z]
        for f in range(2):
            for half in range(2):
                for upper in range(2):
                    loads = [
                        planes[f, xp, half, pl.ds(64 * upper + ys, 8, stride=8)] for ys in range(8) for xp in range(2)
                    ]
                    for k, v in enumerate(swap_bits(loads, [(3, 6), (2, 5), (1, 4), (0, 3)])):
                        tj, rz = 8 * half + k // 2, k % 2
                        device = device_of(7 if upper else 0, tj)
                        at = device * 24 + array * 4 + f * 2 + rz
                        out_ref[pl.ds(at, 8, stride=12)] = turn_pairs(v) if upper else v


def spread(starts, nodes):
    vmem = pl.BlockSpec(memory_space=pltpu.VMEM)
    return pl.pallas_call(
        spread_kernel,
        in_specs=[vmem, vmem],
        out_specs=vmem,
        out_shape=jax.ShapeDtypeStruct((128 * 24, 128), F32),
        scratch_shapes=[pltpu.VMEM((2, 2, 2, 128, 128), F32)],
        compiler_params=pltpu.CompilerParams(vmem_limit_bytes=VMEM_LIMIT),
        name="spread",
    )(starts, nodes)


def collect_kernel(in_ref, starts_ref, nodes_ref, planes):
    for array in range(3):
        for f in range(2):
            for xp in range(2):
                for half in range(2):
                    for upper in range(2):
                        loads = []
                        for t in range(8):
                            device = device_of(7 if upper else 0, 8 * half + t)
                            v = in_ref[pl.ds(device * 24 + array * 4 + f * 2 + xp, 8, stride=12)]
                            loads.append(turn_pairs(v) if upper else v)
                        for ys, v in enumerate(swap_bits(loads, [(2, 6), (1, 5), (0, 4)])):
                            planes[f, xp, half, pl.ds(64 * upper + ys, 8, stride=8)] = v
                    z = slice(128 * half, 128 * half + 128)
                    if array == 0:
                        starts_ref[f, xp, :, z] = planes[f, xp, half]
                    else:
                        nodes_ref[array - 1, f, xp, :, z] = planes[f, xp, half]


def collect(tiles):
    vmem = pl.BlockSpec(memory_space=pltpu.VMEM)
    return pl.pallas_call(
        collect_kernel,
        out_shape=(
            jax.ShapeDtypeStruct((2, 2, 128, 256), F32),
            jax.ShapeDtypeStruct((2, 2, 2, 128, 256), F32),
        ),
        in_specs=[vmem],
        out_specs=(vmem, vmem),
        scratch_shapes=[pltpu.VMEM((2, 2, 2, 128, 128), F32)],
        compiler_params=pltpu.CompilerParams(vmem_limit_bytes=VMEM_LIMIT),
        name="collect",
    )(tiles)


def deal_kernel(scalars, in_ref, low_ref, high_ref, left_ref, right_ref):
    for u in range(6):
        for ry, y_ref in enumerate((low_ref, high_ref)):
            for rz, z_ref in enumerate((left_ref, right_ref)):
                v = in_ref[pl.ds(ry * 12 + 2 * u + rz, 8, stride=24)]
                y_ref[rz, 0, u] = v
                z_ref[ry, 0, u] = v


def slab_at(first):
    return lambda i, s: (lax.rem(s[0] + (first + i), SLABS), 0)


def halves_spec():
    return pl.BlockSpec((2, 1, 6, 8, 128), lambda i, s: (0, i, 0, 0, 0))


def deal(scalars, tiles, first, count):
    return pl.pallas_call(
        deal_kernel,
        grid_spec=pltpu.PrefetchScalarGridSpec(
            num_scalar_prefetch=1,
            grid=(count,),
            in_specs=[pl.BlockSpec((SLAB_ROWS, 128), slab_at(first))],
            out_specs=(halves_spec(),) * 4,
        ),
        out_shape=(jax.ShapeDtypeStruct((2, count, 6, 8, 128), F32),) * 4,
        compiler_params=pltpu.CompilerParams(vmem_limit_bytes=VMEM_LIMIT),
        cost_estimate=pl.CostEstimate(flops=0, bytes_accessed=count * 300000, transcendentals=0),
        name=f"deal_{first}",
    )(scalars, tiles)


def exchange(low, high, left, right):
    got = []
    for di, dj in AROUND:
        if dj == 0:
            payload = high if di < 0 else low
        elif di == 0:
            payload = right if dj < 0 else left
        else:
            payload = (high if di < 0 else low)[1 if dj < 0 else 0]
        pairs = [(device_of(i + di, j + dj), device_of(i, j)) for i in range(TILES_Y) for j in range(TILES_Z)]
        got.append(lax.ppermute(payload, AXES, pairs))
    return got


def assemble(tile, u, low, high, got):
    pieces = []
    for rp in range(4):
        for cp in range(4):
            di, ry = ((-1, 1), (0, 0), (0, 1), (1, 0))[rp]
            dj, rz = ((-1, 1), (0, 0), (0, 1), (1, 0))[cp]
            if (di, dj) == (0, 0):
                pieces.append((high if ry else low)[rz, 0, u])
            elif dj == 0:
                pieces.append(got[di, dj][rz, 0, u])
            elif di == 0:
                pieces.append(got[di, dj][ry, 0, u])
            else:
                pieces.append(got[di, dj][0, u])
    whole = swap_bits(pieces, [(3, 6), (2, 5), (1, 4), (0, 3)])
    return [jnp.where(tile.inside, v, 0.0) for v in whole]


def quarters(arrays):
    lane = lanes()
    merged = []
    for k in range(8):
        merged.append(jnp.where(lane < 64, roll(arrays[k], -40), roll(arrays[k + 8], 24)))
    merged = [
        jnp.where((lane >> 4) % 2 == 0, merged[k], roll(merged[k + 2], 16)) for k in (0, 1, 4, 5)
    ]
    merged = swap_bits(merged, [(1, 5), (0, 3)])
    return [[merged[2 * ry + rz] for rz in range(2)] for ry in range(2)]


def core_rows(arrays):
    lane = lanes()
    merged = [jnp.where(lane < 64, roll(arrays[k], -40), roll(arrays[k + 4], 24)) for k in range(4)]
    merged = [jnp.where((lane >> 4) % 2 == 0, merged[k], roll(merged[k + 1], 16)) for k in (0, 2)]
    return swap_bits(merged, [(0, 5)])


class Tile:
    def __init__(self, scalars):
        lane, row = lanes(), rows()
        y = EDGE * scalars[3] - RIM + 8 * (lane // 32)
        z = EDGE * scalars[4] - RIM + lane % 32
        self.inside = (y >= 0) & (y < 128) & (z >= 0) & (z < 256)
        self.below_top, self.above_bottom = row < 7, row > 0

    def around(self, load, f, xp, ys):
        mid = load(f, xp, ys)
        total = roll(mid, -1) + roll(mid, 1)
        total = total + (load(f, xp, ys + 1) if ys < 7 else roll(load(f, xp, 0), -32))
        total = total + (load(f, xp, ys - 1) if ys > 0 else roll(load(f, xp, 7), 32))
        other = load(f, 1 - xp, ys)
        if xp == 0:
            far = jnp.where(self.above_bottom, roll(other, 1, 0), 0.0)
        else:
            far = jnp.where(self.below_top, roll(other, -1, 0), 0.0)
        return total + (other + far), mid

    def tendency(self, load, xp, ys):
        around_p, p = self.around(load, 0, xp, ys)
        around_v, v = self.around(load, 1, xp, ys)
        reaction = (1.0 - p) * (v * v)
        rate_p = 0.2 * around_p + (reaction - 1.24 * p)
        rate_v = 0.1 * around_v + (reaction - 0.7 * v)
        return (jnp.where(self.inside, rate_p, 0.0), jnp.where(self.inside, rate_v, 0.0)), (p, v)


CELLS = [(xp, ys) for ys in range(8) for xp in range(2)]
FIELD = (2, 2, 8, 8, 128)


def reader(ref, *at):
    return lambda f, xp, ys: ref[at + (f, xp, ys)]


def sweep_kernel(scalars, low, high, *refs):
    got, (out_ref, start_ref, old, one, two, ahead, rate) = dict(zip(AROUND, refs[:8], strict=True)), refs[8:]
    tile = Tile(scalars)
    for array in range(3):
        for f in range(2):
            for (xp, ys), v in zip(CELLS, assemble(tile, 2 * array + f, low, high, got), strict=True):
                old[array, f, xp, ys] = v

    @pl.when(pl.program_id(0) == 0)
    def _():
        start_ref[...] = old[0]

    for xp, ys in CELLS:
        f0, y0 = tile.tendency(reader(old, 0), xp, ys)
        f1, _ = tile.tendency(reader(old, 1), xp, ys)
        f2, _ = tile.tendency(reader(old, 2), xp, ys)
        for f in range(2):
            one[f, xp, ys] = y0[f] + (5 * H / 24) * f0[f] + ((H / 3) * f1[f] - (H / 24) * f2[f])
            out_ref[0, 0, f, xp, ys] = (H / 6) * (f1[f] + f2[f]) - (5 * H / 6) * f0[f]
            ahead[f, xp, ys] = y0[f] + H * f0[f]
    for xp, ys in CELLS:
        r1, _ = tile.tendency(reader(one), xp, ys)
        for f in range(2):
            correction = out_ref[0, 0, f, xp, ys] + (H / 2) * r1[f]
            out_ref[0, 0, f, xp, ys] = correction
            two[f, xp, ys] = ahead[f, xp, ys] + correction
            rate[f, xp, ys] = r1[f]
    for xp, ys in CELLS:
        r2, _ = tile.tendency(reader(two), xp, ys)
        for f in range(2):
            r1 = rate[f, xp, ys]
            out_ref[0, 1, f, xp, ys] = (H / 3) * r1 - (H / 24) * r2[f]
            out_ref[0, 2, f, xp, ys] = (H / 6) * (r1 + r2[f])


def sweep(scalars, low, high, got, first, count):
    corner = pl.BlockSpec((1, 6, 8, 128), lambda i, s: (i, 0, 0, 0))
    specs = [halves_spec(), halves_spec()]
    specs += [corner if di and dj else halves_spec() for di, dj in AROUND]
    field = pltpu.VMEM(FIELD, F32)
    return pl.pallas_call(
        sweep_kernel,
        grid_spec=pltpu.PrefetchScalarGridSpec(
            num_scalar_prefetch=1,
            grid=(count,),
            in_specs=specs,
            out_specs=(
                pl.BlockSpec((1, 3) + FIELD, lambda i, s: (i,) + (0,) * 6),
                pl.BlockSpec(FIELD, lambda i, s: (0,) * 5),
            ),
            scratch_shapes=[pltpu.VMEM((3,) + FIELD, F32)] + [field] * 4,
        ),
        out_shape=(jax.ShapeDtypeStruct((count, 3) + FIELD, F32), jax.ShapeDtypeStruct(FIELD, F32)),
        compiler_params=pltpu.CompilerParams(vmem_limit_bytes=VMEM_LIMIT),
        cost_estimate=pl.CostEstimate(flops=count * 5 * 32 * 1024 * 40, bytes_accessed=count * 1200000, transcendentals=0),
        name=f"sweep_{first}",
    )(scalars, low, high, *got)


def write_pack(ref, at, array, load):
    for f in range(2):
        for xp in range(2):
            for ry, v in enumerate(core_rows([load(f, xp, ys) for ys in range(8)])):
                ref[at, ry * 12 + array * 4 + f * 2 + xp] = v


def chain_kernel(first, count, scalars, sweeps, *refs):
    tile = Tile(scalars)
    last = first + count >= SLABS
    z, late, corr, one, two, ahead = refs[-6:]
    refs = refs[:-6]
    take_first = scalars[1] > 0
    if first == 0:
        start_ref, refs = refs[0], refs[1:]
        z[0] = start_ref[...]
    else:
        got = dict(zip(AROUND, refs[2:10], strict=True))
        for k in range(3):
            for f in range(2):
                for (xp, ys), v in zip(CELLS, assemble(tile, 2 * k + f, refs[0], refs[1], got), strict=True):
                    if k == 0:
                        z[first % 2, f, xp, ys] = v
                    elif k == 1:
                        late[(first + 1) % 2, f, xp, ys] = v
                    else:
                        corr[f, xp, ys] = v
        refs = refs[10:]
    packs = refs[-1] if last else refs[0]

    def step(p, at, final=False):
        now, other = p % 2, (p + 1) % 2
        reset = (p == 0) | ((p == 1) & take_first)
        for xp, ys in CELLS:
            fl, l = tile.tendency(reader(late, other), xp, ys)
            f0, y0 = tile.tendency(reader(z, now), xp, ys)
            for f in range(2):
                late[now, f, xp, ys] = jnp.where(reset, y0[f], l[f] + H * fl[f] + corr[f, xp, ys])
                g = y0[f] + H * f0[f]
                ahead[f, xp, ys] = g
                if final:
                    one[f, xp, ys] = y0[f] + (H / 2) * f0[f]
                    two[f, xp, ys] = (-H / 2) * f0[f]
                else:
                    z[other, f, xp, ys] = g + sweeps[at, 0, f, xp, ys]
                    one[f, xp, ys] = y0[f] + (5 * H / 24) * f0[f] + sweeps[at, 1, f, xp, ys]
                    two[f, xp, ys] = sweeps[at, 2, f, xp, ys] - (5 * H / 6) * f0[f]
        for xp, ys in CELLS:
            f1, _ = tile.tendency(reader(one), xp, ys)
            for f in range(2):
                c = two[f, xp, ys] + (H / 2) * f1[f]
                corr[f, xp, ys] = c
                two[f, xp, ys] = ahead[f, xp, ys] + c
        write_pack(packs, at, 0, reader(late, now))
        write_pack(packs, at, 1, reader(one))
        write_pack(packs, at, 2, reader(two))

    def looped(at, carry):
        step(first + at, at)
        return carry

    lax.fori_loop(0, count, looped, 0)

    if not last:
        end = first + count
        _, low_ref, high_ref, left_ref, right_ref = refs
        for k, load in enumerate((reader(z, end % 2), reader(late, (end + 1) % 2), reader(corr))):
            for f in range(2):
                parts = quarters([load(f, xp, ys) for xp, ys in CELLS])
                for ry, y_ref in enumerate((low_ref, high_ref)):
                    for rz, z_ref in enumerate((left_ref, right_ref)):
                        y_ref[rz, 0, 2 * k + f] = parts[ry][rz]
                        z_ref[ry, 0, 2 * k + f] = parts[ry][rz]
        return

    step(SLABS, count, final=True)
    end = SLABS % 2
    for xp, ys in CELLS:
        fl, l = tile.tendency(reader(late, end), xp, ys)
        for f in range(2):
            one[f, xp, ys] = l[f] + H * fl[f] + corr[f, xp, ys]
    write_pack(packs, count + 1, 0, reader(one))
    leader, conv_one, conv_two = scalars[0], scalars[1] > 0, scalars[2] > 0
    out_ref = refs[-2]

    def put(p, ref, i, newest=False):
        base = lax.rem(leader + p, SLABS) * SLAB_ROWS
        for ry in range(2):
            for array in range(3):
                for k in range(4):
                    r = ry * 12 + array * 4 + k
                    out_ref[pl.ds(base + r, 8, stride=24)] = ref[i, ry * 12 + k] if newest else ref[i, r]

    for b, ref in enumerate((*refs[:-2], packs)):

        def move(i, carry, b=b, ref=ref):
            put(b * BLOCK + i, ref, i)
            return carry

        lax.fori_loop(0, count if ref is packs else BLOCK, move, 0)

    @pl.when(conv_one)
    def _():
        put(0, packs, count)

    @pl.when(conv_two & conv_one)
    def _():
        put(1, packs, count + 1, newest=True)

    @pl.when(conv_two & jnp.logical_not(conv_one))
    def _():
        put(0, packs, count, newest=True)


def chain(scalars, first, count, sweeps, inputs):
    last = first + count >= SLABS
    vmem = pl.BlockSpec(memory_space=pltpu.VMEM)
    if last:
        out_shape = jax.ShapeDtypeStruct((SLABS * SLAB_ROWS, 128), F32)
        scratch = [pltpu.VMEM((count + 2, 24, 8, 128), F32)]
    else:
        out_shape = (jax.ShapeDtypeStruct((count, 24, 8, 128), F32),)
        out_shape += (jax.ShapeDtypeStruct((2, 1, 6, 8, 128), F32),) * 4
        scratch = []
    field, double = pltpu.VMEM(FIELD, F32), pltpu.VMEM((2,) + FIELD, F32)
    return pl.pallas_call(
        functools.partial(chain_kernel, first, count),
        grid_spec=pltpu.PrefetchScalarGridSpec(
            num_scalar_prefetch=1,
            grid=(1,),
            in_specs=[vmem] * (1 + len(inputs)),
            out_specs=vmem if last else (vmem,) * 5,
            scratch_shapes=scratch + [double, double, field, field, field, field],
        ),
        out_shape=out_shape,
        compiler_params=pltpu.CompilerParams(vmem_limit_bytes=VMEM_LIMIT),
        cost_estimate=pl.CostEstimate(flops=count * 3 * 32 * 1024 * 40, bytes_accessed=count * 500000, transcendentals=0),
        name=f"chain_{first}",
    )(scalars, sweeps, *inputs)


def body(slab_starts, slab_nodes, first_slab, converged):
    ti, tj = own_tile()
    scalars = jnp.stack([first_slab[0], converged[0], converged[1], ti.astype(jnp.int32), tj.astype(jnp.int32)])
    chunks = spread(slab_starts[0], slab_nodes[0])
    tiles = lax.all_to_all(chunks.reshape(128, 24, 128), AXES, 0, 0, tiled=True).reshape(SLABS * SLAB_ROWS, 128)

    blocks = [(0, BLOCK), (BLOCK, BLOCK), (2 * BLOCK, SLABS - 2 * BLOCK)]
    dealt = [deal(scalars, tiles, *block) for block in blocks]
    got = exchange(*dealt[0])
    sweeps, start = sweep(scalars, dealt[0][0], dealt[0][1], got, *blocks[0])
    inputs = [start]
    packs = []
    for b, block in enumerate(blocks[:-1]):
        follow = blocks[b + 1]
        quarter_tiles, _ = lax.optimization_barrier((dealt[b + 1], got))
        beside = exchange(*quarter_tiles)
        pack, *state = chain(scalars, *block, sweeps, inputs)
        packs.append(pack)
        got = exchange(*state)
        sweeps, _ = sweep(scalars, quarter_tiles[0], quarter_tiles[1], beside, *follow)
        inputs = [state[0], state[1], *got]
    out = chain(scalars, *blocks[-1], sweeps, inputs + packs)
    out = lax.all_to_all(out.reshape(128, 24, 128), AXES, 0, 0, tiled=True)
    starts, nodes = collect(out.reshape(128 * 24, 128))
    return starts[None], nodes[None]


def solution(mesh):
    slab_spec = P("tm", None, "space", None, None)
    node_spec = P("tm", None, None, "space", None, None)
    return jax.shard_map(
        body,
        mesh=mesh,
        in_specs=(slab_spec, node_spec, P(), P()),
        out_specs=(slab_spec, node_spec),
        check_vma=False,
    )
```

```python
import functools

import jax
import jax.numpy as jnp
from jax import lax
from jax.experimental import pallas as pl
from jax.experimental.pallas import tpu as pltpu
from jax.sharding import PartitionSpec as P

SLABS = 16
TILES_Y = 8
TILES_Z = 16
EDGE = 16
RIM = 8
BLOCK = 6
H = 0.5
AXES = ("tm", "space")
F32 = jnp.float32
VMEM_LIMIT = 40 * 1024 * 1024
SHAPE = (8, 128)
SLAB_ROWS = 192


def device_of(i, j):
    i, j = i % TILES_Y, j % TILES_Z
    zb, x = (0, i) if i < 4 else (1, 7 - i)
    cj = j // 2
    core = (j % 2) ^ (cj % 2)
    za, y = (0, cj) if cj < 4 else (1, 7 - cj)
    zl = za ^ zb
    return (y * 4 + za * 2 + core) * 8 + zl * 4 + x


def own_tile():
    tm, space = lax.axis_index("tm"), lax.axis_index("space")
    y, za, core = tm // 4, (tm // 2) % 2, tm % 2
    zl, x = space // 4, space % 4
    zb = za ^ zl
    ti = jnp.where(zb == 0, x, 7 - x)
    cj = jnp.where(za == 0, y, 7 - y)
    return ti, 2 * cj + (core ^ (cj % 2))


def roll(v, by, axis=1):
    by %= v.shape[axis]
    return v if by == 0 else pltpu.roll(v, by, axis)


def lanes():
    return lax.broadcasted_iota(jnp.int32, SHAPE, 1)


def rows():
    return lax.broadcasted_iota(jnp.int32, SHAPE, 0)


def swap_bits(arrays, pairs):
    arrays, lane = list(arrays), lanes()
    for index_bit, lane_bit in pairs:
        step, low = 1 << lane_bit, (lane >> lane_bit) % 2 == 0
        for a in range(len(arrays)):
            b = a | (1 << index_bit)
            if a != b:
                u, v = arrays[a], arrays[b]
                arrays[a] = jnp.where(low, u, roll(v, step))
                arrays[b] = jnp.where(low, roll(u, -step), v)
    return arrays


def turn_pairs(v):
    v = roll(v, 4, 0)
    return jnp.where(rows() // 2 % 2 == 0, roll(v, -2, 0), roll(v, 2, 0))


def spread_kernel(starts_ref, nodes_ref, out_ref, planes):
    for array in range(3):
        source = starts_ref if array == 0 else nodes_ref.at[array - 1]
        for f in range(2):
            for xp in range(2):
                for half in range(2):
                    planes[2 * array + f, xp, half] = source[f, xp, :, 128 * half : 128 * half + 128]

    def unit(u, carry):
        row = u // 2 * 4 + u % 2 * 2
        for half in range(2):
            for upper in range(2):
                loads = [
                    planes[u, xp, half, pl.ds(64 * upper + ys, 8, stride=8)] for ys in range(8) for xp in range(2)
                ]
                for k, v in enumerate(swap_bits(loads, [(3, 6), (2, 5), (1, 4), (0, 3)])):
                    tj, rz = 8 * half + k // 2, k % 2
                    device = device_of(7 if upper else 0, tj)
                    out_ref[pl.ds(device * 24 + rz + row, 8, stride=12)] = turn_pairs(v) if upper else v
        return carry

    lax.fori_loop(0, 6, unit, 0)


def spread(starts, nodes):
    vmem = pl.BlockSpec(memory_space=pltpu.VMEM)
    return pl.pallas_call(
        spread_kernel,
        in_specs=[vmem, vmem],
        out_specs=vmem,
        out_shape=jax.ShapeDtypeStruct((128 * 24, 128), F32),
        scratch_shapes=[pltpu.VMEM((6, 2, 2, 128, 128), F32)],
        compiler_params=pltpu.CompilerParams(vmem_limit_bytes=VMEM_LIMIT),
        name="spread",
    )(starts, nodes)


def collect_kernel(in_ref, starts_ref, nodes_ref, planes):
    def unit(u, carry):
        for half in range(2):
            for upper in range(2):
                loads = []
                for t in range(8):
                    device = device_of(7 if upper else 0, 8 * half + t)
                    v = in_ref[pl.ds(device * 24 + u, 8, stride=12)]
                    loads.append(turn_pairs(v) if upper else v)
                for ys, v in enumerate(swap_bits(loads, [(2, 6), (1, 5), (0, 4)])):
                    planes[u, half, pl.ds(64 * upper + ys, 8, stride=8)] = v
        return carry

    lax.fori_loop(0, 12, unit, 0)
    for array in range(3):
        target = starts_ref if array == 0 else nodes_ref.at[array - 1]
        for f in range(2):
            for xp in range(2):
                for half in range(2):
                    target[f, xp, :, 128 * half : 128 * half + 128] = planes[array * 4 + f * 2 + xp, half]


def collect(tiles):
    vmem = pl.BlockSpec(memory_space=pltpu.VMEM)
    return pl.pallas_call(
        collect_kernel,
        out_shape=(
            jax.ShapeDtypeStruct((2, 2, 128, 256), F32),
            jax.ShapeDtypeStruct((2, 2, 2, 128, 256), F32),
        ),
        in_specs=[vmem],
        out_specs=(vmem, vmem),
        scratch_shapes=[pltpu.VMEM((12, 2, 128, 128), F32)],
        compiler_params=pltpu.CompilerParams(vmem_limit_bytes=VMEM_LIMIT),
        name="collect",
    )(tiles)


def deal_kernel(scalars, in_ref, low_ref, high_ref):
    def position(p, carry):
        base = lax.rem(scalars[0] + p, SLABS) * SLAB_ROWS
        for u in range(6):
            for ry, ref in enumerate((low_ref, high_ref)):
                for rz in range(2):
                    ref[rz, p, u] = in_ref[pl.ds(base + ry * 12 + 2 * u + rz, 8, stride=24)]
        return carry

    lax.fori_loop(0, SLABS, position, 0)


VMEM = pl.BlockSpec(memory_space=pltpu.VMEM)
SMEM = pl.BlockSpec(memory_space=pltpu.SMEM)


def deal(scalars, tiles):
    return pl.pallas_call(
        deal_kernel,
        in_specs=[SMEM, VMEM],
        out_specs=(VMEM,) * 2,
        out_shape=(jax.ShapeDtypeStruct((2, SLABS, 6, 8, 128), F32),) * 2,
        compiler_params=pltpu.CompilerParams(vmem_limit_bytes=VMEM_LIMIT),
        cost_estimate=pl.CostEstimate(flops=0, bytes_accessed=3000000, transcendentals=0),
        name="deal",
    )(scalars, tiles)


def from_neighbour(payload, di, dj):
    pairs = [(device_of(i + di, j + dj), device_of(i, j)) for i in range(TILES_Y) for j in range(TILES_Z)]
    return lax.ppermute(payload, AXES, pairs)


def exchange(low, high):
    up, down = from_neighbour(high, -1, 0), from_neighbour(low, 1, 0)
    column = [jnp.stack([up[rz], low[rz], high[rz], down[rz]]) for rz in range(2)]
    left, right = from_neighbour(column[1], 0, -1), from_neighbour(column[0], 0, 1)
    return low, high, up, down, left, right


def assemble(tile, p, u, low, high, up, down, left, right):
    pieces = []
    for row, ref in enumerate((up, low, high, down)):
        pieces += [left[row, p, u], ref[0, p, u], ref[1, p, u], right[row, p, u]]
    whole = swap_bits(pieces, [(3, 6), (2, 5), (1, 4), (0, 3)])
    return [jnp.where(tile.inside, v, 0.0) for v in whole]


def quarters(arrays):
    lane = lanes()
    merged = []
    for k in range(8):
        merged.append(jnp.where(lane < 64, roll(arrays[k], -40), roll(arrays[k + 8], 24)))
    merged = [
        jnp.where((lane >> 4) % 2 == 0, merged[k], roll(merged[k + 2], 16)) for k in (0, 1, 4, 5)
    ]
    merged = swap_bits(merged, [(1, 5), (0, 3)])
    return [[merged[2 * ry + rz] for rz in range(2)] for ry in range(2)]


def core_rows(arrays):
    lane = lanes()
    merged = [jnp.where(lane < 64, roll(arrays[k], -40), roll(arrays[k + 4], 24)) for k in range(4)]
    merged = [jnp.where((lane >> 4) % 2 == 0, merged[k], roll(merged[k + 1], 16)) for k in (0, 2)]
    return swap_bits(merged, [(0, 5)])


class Tile:
    def __init__(self, scalars):
        lane, row = lanes(), rows()
        y = EDGE * scalars[3] - RIM + 8 * (lane // 32)
        z = EDGE * scalars[4] - RIM + lane % 32
        self.inside = (y >= 0) & (y < 128) & (z >= 0) & (z < 256)
        self.below_top, self.above_bottom = row < 7, row > 0

    def around(self, load, f, xp, ys):
        mid = load(f, xp, ys)
        total = roll(mid, -1) + roll(mid, 1)
        total = total + (load(f, xp, ys + 1) if ys < 7 else roll(load(f, xp, 0), -32))
        total = total + (load(f, xp, ys - 1) if ys > 0 else roll(load(f, xp, 7), 32))
        other = load(f, 1 - xp, ys)
        if xp == 0:
            far = jnp.where(self.above_bottom, roll(other, 1, 0), 0.0)
        else:
            far = jnp.where(self.below_top, roll(other, -1, 0), 0.0)
        return total + (other + far), mid

    def tendency(self, load, xp, ys):
        around_p, p = self.around(load, 0, xp, ys)
        around_v, v = self.around(load, 1, xp, ys)
        reaction = (1.0 - p) * (v * v)
        rate_p = 0.2 * around_p + (reaction - 1.24 * p)
        rate_v = 0.1 * around_v + (reaction - 0.7 * v)
        return (jnp.where(self.inside, rate_p, 0.0), jnp.where(self.inside, rate_v, 0.0)), (p, v)


CELLS = [(xp, ys) for ys in range(8) for xp in range(2)]
FIELD = (2, 2, 8, 8, 128)


def reader(ref, *at):
    return lambda f, xp, ys: ref[at + (f, xp, ys)]


def sweep_kernel(first, count, scalars, *refs):
    halo, (out_ref, start_ref, old, one, two, ahead, rate, base) = refs[:6], refs[6:]
    tile = Tile(scalars)

    def position(at, carry):
        for array in range(3):
            both = [assemble(tile, first + at, 2 * array + f, *halo) for f in range(2)]
            for f in range(2):
                for (xp, ys), v in zip(CELLS, both[f], strict=True):
                    old[array, f, xp, ys] = v

        if first == 0:

            @pl.when(at == 0)
            def _():
                start_ref[...] = old[0]

        for xp, ys in CELLS:
            f0, y0 = tile.tendency(reader(old, 0), xp, ys)
            f1, _ = tile.tendency(reader(old, 1), xp, ys)
            f2, _ = tile.tendency(reader(old, 2), xp, ys)
            for f in range(2):
                one[f, xp, ys] = y0[f] + (5 * H / 24) * f0[f] + ((H / 3) * f1[f] - (H / 24) * f2[f])
                base[f, xp, ys] = (H / 6) * (f1[f] + f2[f]) - (5 * H / 6) * f0[f]
                ahead[f, xp, ys] = y0[f] + H * f0[f]
        for xp, ys in CELLS:
            r1, _ = tile.tendency(reader(one), xp, ys)
            for f in range(2):
                correction = base[f, xp, ys] + (H / 2) * r1[f]
                base[f, xp, ys] = correction
                two[f, xp, ys] = ahead[f, xp, ys] + correction
                rate[f, xp, ys] = r1[f]
        for xp, ys in CELLS:
            r2, _ = tile.tendency(reader(two), xp, ys)
            for f in range(2):
                r1 = rate[f, xp, ys]
                one[f, xp, ys] = (H / 3) * r1 - (H / 24) * r2[f]
                ahead[f, xp, ys] = (H / 6) * (r1 + r2[f])
        out_ref[at, 0] = base[...]
        out_ref[at, 1] = one[...]
        out_ref[at, 2] = ahead[...]
        return carry

    lax.fori_loop(0, count, position, 0)


def sweep(scalars, halo, first, count):
    field = pltpu.VMEM(FIELD, F32)
    return pl.pallas_call(
        functools.partial(sweep_kernel, first, count),
        in_specs=[SMEM] + [VMEM] * 6,
        out_specs=(VMEM,) * 2,
        scratch_shapes=[pltpu.VMEM((3,) + FIELD, F32)] + [field] * 5,
        out_shape=(jax.ShapeDtypeStruct((count, 3) + FIELD, F32), jax.ShapeDtypeStruct(FIELD, F32)),
        compiler_params=pltpu.CompilerParams(vmem_limit_bytes=VMEM_LIMIT),
        cost_estimate=pl.CostEstimate(flops=count * 5 * 32 * 1024 * 40, bytes_accessed=count * 1200000, transcendentals=0),
        name=f"sweep_{first}",
    )(scalars, *halo)


def write_packs(ref, at, loads):
    values = {}
    for array, load in enumerate(loads):
        for f in range(2):
            for xp in range(2):
                for ry, v in enumerate(core_rows([load(f, xp, ys) for ys in range(8)])):
                    values[ry * 12 + array * 4 + f * 2 + xp] = v
    for r, v in values.items():
        ref[at, r] = v


def pack_kernel(in_ref, out_ref):
    def position(i, carry):
        write_packs(out_ref, i, [reader(in_ref, i, array) for array in range(3)])
        return carry

    lax.fori_loop(0, out_ref.shape[0], position, 0)


def pack(raw):
    count = raw.shape[0]
    return pl.pallas_call(
        pack_kernel,
        in_specs=[VMEM],
        out_specs=VMEM,
        out_shape=jax.ShapeDtypeStruct((count, 24, 8, 128), F32),
        compiler_params=pltpu.CompilerParams(vmem_limit_bytes=VMEM_LIMIT),
        cost_estimate=pl.CostEstimate(flops=count * 1000000, bytes_accessed=count * 500000, transcendentals=0),
        name="pack",
    )(raw)


def chain_kernel(first, count, scalars, sweeps, *refs):
    tile = Tile(scalars)
    last = first + count >= SLABS
    z, late, corr, one, two, ahead, next_z, next_late = refs[-8:]
    refs = refs[:-8]
    take_first = scalars[1] > 0
    if first == 0:
        start_ref, refs = refs[0], refs[1:]
        z[...] = start_ref[...]
    else:
        for k, ref in enumerate((z, late, corr)):
            both = [assemble(tile, 0, 2 * k + f, *refs[:6]) for f in range(2)]
            for f in range(2):
                for (xp, ys), v in zip(CELLS, both[f], strict=True):
                    ref[f, xp, ys] = v
        refs = refs[6:]
    raw = refs[-1] if last else refs[0]

    def step(at, final=False):
        p = first + at
        reset = (p == 0) | ((p == 1) & take_first)
        for xp, ys in CELLS:
            fl, l = tile.tendency(reader(late), xp, ys)
            f0, y0 = tile.tendency(reader(z), xp, ys)
            for f in range(2):
                next_late[f, xp, ys] = jnp.where(reset, y0[f], l[f] + H * fl[f] + corr[f, xp, ys])
                g = y0[f] + H * f0[f]
                ahead[f, xp, ys] = g
                if final:
                    one[f, xp, ys] = y0[f] + (H / 2) * f0[f]
                    two[f, xp, ys] = (-H / 2) * f0[f]
                else:
                    next_z[f, xp, ys] = g + sweeps[at, 0, f, xp, ys]
                    one[f, xp, ys] = y0[f] + (5 * H / 24) * f0[f] + sweeps[at, 1, f, xp, ys]
                    two[f, xp, ys] = sweeps[at, 2, f, xp, ys] - (5 * H / 6) * f0[f]
        for xp, ys in CELLS:
            f1, _ = tile.tendency(reader(one), xp, ys)
            for f in range(2):
                c = two[f, xp, ys] + (H / 2) * f1[f]
                corr[f, xp, ys] = c
                two[f, xp, ys] = ahead[f, xp, ys] + c
        late[...] = next_late[...]
        if not final:
            z[...] = next_z[...]
        raw[at, 0] = next_late[...]
        raw[at, 1] = one[...]
        raw[at, 2] = two[...]

    def looped(at, carry):
        step(at)
        return carry

    lax.fori_loop(0, count, looped, 0)

    if not last:
        _, low_ref, high_ref = refs
        for k, ref in enumerate((z, late, corr)):
            both = [quarters([ref[f, xp, ys] for xp, ys in CELLS]) for f in range(2)]
            for f in range(2):
                for ry, half_ref in enumerate((low_ref, high_ref)):
                    for rz in range(2):
                        half_ref[rz, 0, 2 * k + f] = both[f][ry][rz]
        return

    step(count, final=True)
    for xp, ys in CELLS:
        fl, l = tile.tendency(reader(late), xp, ys)
        for f in range(2):
            raw[count + 1, 0, f, xp, ys] = l[f] + H * fl[f] + corr[f, xp, ys]
    leader, conv_one, conv_two = scalars[0], scalars[1] > 0, scalars[2] > 0
    *earlier, out_ref, packs, _ = refs

    def pack_at(i, carry):
        write_packs(packs, i, [reader(raw, i, array) for array in range(3)])
        return carry

    lax.fori_loop(0, count + 2, pack_at, 0)

    def put(p, ref, i, newest=False):
        base = lax.rem(leader + p, SLABS) * SLAB_ROWS
        for ry in range(2):
            for array in range(3):
                for k in range(4):
                    r = ry * 12 + array * 4 + k
                    out_ref[pl.ds(base + r, 8, stride=24)] = ref[i, ry * 12 + k] if newest else ref[i, r]

    for b, ref in enumerate((*earlier, packs)):

        def move(i, carry, b=b, ref=ref):
            put(b * BLOCK + i, ref, i)
            return carry

        lax.fori_loop(0, count if ref is packs else BLOCK, move, 0)

    @pl.when(conv_one)
    def _():
        put(0, packs, count)

    @pl.when(conv_two & conv_one)
    def _():
        put(1, packs, count + 1, newest=True)

    @pl.when(conv_two & jnp.logical_not(conv_one))
    def _():
        put(0, packs, count, newest=True)


def chain(scalars, first, count, sweeps, inputs):
    last = first + count >= SLABS
    if last:
        out_shape = jax.ShapeDtypeStruct((SLABS * SLAB_ROWS, 128), F32)
        scratch = [pltpu.VMEM((count + 2, 24, 8, 128), F32), pltpu.VMEM((count + 2, 3) + FIELD, F32)]
    else:
        out_shape = (jax.ShapeDtypeStruct((count, 3) + FIELD, F32),)
        out_shape += (jax.ShapeDtypeStruct((2, 1, 6, 8, 128), F32),) * 2
        scratch = []
    return pl.pallas_call(
        functools.partial(chain_kernel, first, count),
        in_specs=[SMEM] + [VMEM] * (1 + len(inputs)),
        out_specs=VMEM if last else (VMEM,) * 3,
        scratch_shapes=scratch + [pltpu.VMEM(FIELD, F32)] * 8,
        out_shape=out_shape,
        compiler_params=pltpu.CompilerParams(vmem_limit_bytes=VMEM_LIMIT),
        cost_estimate=pl.CostEstimate(flops=count * 3 * 32 * 1024 * 40, bytes_accessed=count * 500000, transcendentals=0),
        name=f"chain_{first}",
    )(scalars, sweeps, *inputs)


def body(slab_starts, slab_nodes, first_slab, converged):
    ti, tj = own_tile()
    scalars = jnp.stack([first_slab[0], converged[0], converged[1], ti.astype(jnp.int32), tj.astype(jnp.int32)])
    chunks = spread(slab_starts[0], slab_nodes[0])
    tiles = lax.all_to_all(chunks.reshape(128, 24, 128), AXES, 0, 0, tiled=True).reshape(SLABS * SLAB_ROWS, 128)

    blocks = [(0, BLOCK), (BLOCK, BLOCK), (2 * BLOCK, SLABS - 2 * BLOCK)]
    halo = exchange(*deal(scalars, tiles))
    sweeps = [sweep(scalars, halo, *block) for block in blocks]
    inputs = [sweeps[0][1]]
    packs = []
    for block, (swept, _) in zip(blocks[:-1], sweeps, strict=False):
        raw, *state = chain(scalars, *block, swept, inputs)
        packs.append(pack(raw))
        inputs = exchange(*state)
    out = chain(scalars, *blocks[-1], sweeps[-1][0], [*inputs, *packs])
    out = lax.all_to_all(out.reshape(128, 24, 128), AXES, 0, 0, tiled=True)
    starts, nodes = collect(out.reshape(128 * 24, 128))
    return starts[None], nodes[None]


def solution(mesh):
    slab_spec = P("tm", None, "space", None, None)
    node_spec = P("tm", None, None, "space", None, None)
    return jax.shard_map(
        body,
        mesh=mesh,
        in_specs=(slab_spec, node_spec, P(), P()),
        out_specs=(slab_spec, node_spec),
        check_vma=False,
    )
```

```python
import functools

import jax
import jax.numpy as jnp
from jax import lax
from jax.experimental import pallas as pl
from jax.experimental.pallas import tpu as pltpu
from jax.sharding import PartitionSpec as P

SLABS = 16
TILES_Y = 8
TILES_Z = 16
EDGE = 16
RIM = 8
BLOCKS = ((0, 6), (6, 6), (12, 4))
H = 0.5
AXES = ("tm", "space")
F32 = jnp.float32
VMEM_LIMIT = 40 * 1024 * 1024
SHAPE = (8, 128)
VMEM = pl.BlockSpec(memory_space=pltpu.VMEM)
SMEM = pl.BlockSpec(memory_space=pltpu.SMEM)
ANY = pl.BlockSpec(memory_space=pl.ANY)
SLAB_ROWS = 192


def device_of(i, j):
    i, j = i % TILES_Y, j % TILES_Z
    zb, x = (0, i) if i < 4 else (1, 7 - i)
    cj = j // 2
    core = (j % 2) ^ (cj % 2)
    za, y = (0, cj) if cj < 4 else (1, 7 - cj)
    zl = za ^ zb
    return (y * 4 + za * 2 + core) * 8 + zl * 4 + x


def own_tile():
    tm, space = lax.axis_index("tm"), lax.axis_index("space")
    y, za, core = tm // 4, (tm // 2) % 2, tm % 2
    zl, x = space // 4, space % 4
    zb = za ^ zl
    ti = jnp.where(zb == 0, x, 7 - x)
    cj = jnp.where(za == 0, y, 7 - y)
    return ti, 2 * cj + (core ^ (cj % 2))


def roll(v, by, axis=1):
    by %= v.shape[axis]
    return v if by == 0 else pltpu.roll(v, by, axis)


def lanes():
    return lax.broadcasted_iota(jnp.int32, SHAPE, 1)


def rows():
    return lax.broadcasted_iota(jnp.int32, SHAPE, 0)


def swap_bits(arrays, pairs):
    arrays, lane = list(arrays), lanes()
    for index_bit, lane_bit in pairs:
        step, low = 1 << lane_bit, (lane >> lane_bit) % 2 == 0
        for a in range(len(arrays)):
            b = a | (1 << index_bit)
            if a != b:
                u, v = arrays[a], arrays[b]
                arrays[a] = jnp.where(low, u, roll(v, step))
                arrays[b] = jnp.where(low, roll(u, -step), v)
    return arrays


def turn_pairs(v):
    v = roll(v, 4, 0)
    return jnp.where(rows() // 2 % 2 == 0, roll(v, -2, 0), roll(v, 2, 0))


def spread_kernel(starts_ref, nodes_ref, out_ref, planes, arrived):
    def copies(u):
        source = starts_ref if u < 2 else nodes_ref.at[u // 2 - 1]
        return [
            pltpu.make_async_copy(
                source.at[u % 2, xp, :, pl.ds(128 * half, 128)], planes.at[u, xp, half], arrived.at[4 * u + 2 * xp + half]
            )
            for xp in range(2)
            for half in range(2)
        ]

    for u in range(6):
        for copy in copies(u):
            copy.start()

    def unit(u):
        row = u // 2 * 4 + u % 2 * 2
        for half in range(2):
            for upper in range(2):
                loads = [
                    planes[u, xp, half, pl.ds(64 * upper + ys, 8, stride=8)] for ys in range(8) for xp in range(2)
                ]
                for k, v in enumerate(swap_bits(loads, [(3, 6), (2, 5), (1, 4), (0, 3)])):
                    tj, rz = 8 * half + k // 2, k % 2
                    device = device_of(7 if upper else 0, tj)
                    out_ref[pl.ds(device * 24 + rz + row, 8, stride=12)] = turn_pairs(v) if upper else v

    for copy in copies(0) + copies(1):
        copy.wait()

    def pair(k, carry):
        for n in (1, 2):

            @pl.when(k == n)
            def _(n=n):
                for copy in copies(2 * n) + copies(2 * n + 1):
                    copy.wait()

        lax.fori_loop(2 * k, 2 * k + 2, lambda u, c: (unit(u), c)[1], 0)
        return carry

    lax.fori_loop(0, 3, pair, 0)


def spread(starts, nodes):
    return pl.pallas_call(
        spread_kernel,
        in_specs=[ANY, ANY],
        out_specs=VMEM,
        out_shape=jax.ShapeDtypeStruct((128 * 24, 128), F32),
        scratch_shapes=[pltpu.VMEM((6, 2, 2, 128, 128), F32), pltpu.SemaphoreType.DMA((24,))],
        compiler_params=pltpu.CompilerParams(vmem_limit_bytes=VMEM_LIMIT),
        name="spread",
    )(starts, nodes)


def collect_kernel(in_ref, starts_ref, nodes_ref, planes, left):
    def unit(u, carry):
        for half in range(2):
            for upper in range(2):
                loads = []
                for t in range(8):
                    device = device_of(7 if upper else 0, 8 * half + t)
                    v = in_ref[pl.ds(device * 24 + u, 8, stride=12)]
                    loads.append(turn_pairs(v) if upper else v)
                for ys, v in enumerate(swap_bits(loads, [(2, 6), (1, 5), (0, 4)])):
                    planes[u, half, pl.ds(64 * upper + ys, 8, stride=8)] = v
        return carry

    def copies(array):
        target = starts_ref if array == 0 else nodes_ref.at[array - 1]
        return [
            pltpu.make_async_copy(
                planes.at[4 * array + 2 * f + xp, half],
                target.at[f, xp, :, pl.ds(128 * half, 128)],
                left.at[8 * array + 4 * f + 2 * xp + half],
            )
            for f in range(2)
            for xp in range(2)
            for half in range(2)
        ]

    def array_at(k, carry):
        lax.fori_loop(4 * k, 4 * k + 4, unit, 0)
        for n in range(3):

            @pl.when(k == n)
            def _(n=n):
                for copy in copies(n):
                    copy.start()

        return carry

    lax.fori_loop(0, 3, array_at, 0)
    for n in range(3):
        for copy in copies(n):
            copy.wait()


def collect(tiles):
    return pl.pallas_call(
        collect_kernel,
        out_shape=(
            jax.ShapeDtypeStruct((2, 2, 128, 256), F32),
            jax.ShapeDtypeStruct((2, 2, 2, 128, 256), F32),
        ),
        in_specs=[VMEM],
        out_specs=(ANY, ANY),
        scratch_shapes=[pltpu.VMEM((12, 2, 128, 128), F32), pltpu.SemaphoreType.DMA((24,))],
        compiler_params=pltpu.CompilerParams(vmem_limit_bytes=VMEM_LIMIT),
        name="collect",
    )(tiles)


def deal_kernel(scalars, in_ref, *out_refs):
    for b, (first, count) in enumerate(BLOCKS):

        def position(i, carry, b=b, first=first):
            base = lax.rem(scalars[0] + (first + i), SLABS) * SLAB_ROWS
            for u in range(6):
                for ry in range(2):
                    for rz in range(2):
                        v = in_ref[pl.ds(base + ry * 12 + 2 * u + rz, 8, stride=24)]
                        out_refs[2 * b + ry][rz, i, u] = v
            return carry

        lax.fori_loop(0, count, position, 0)


def deal(scalars, tiles):
    outs = pl.pallas_call(
        deal_kernel,
        in_specs=[SMEM, VMEM],
        out_specs=(VMEM,) * (2 * len(BLOCKS)),
        out_shape=tuple(jax.ShapeDtypeStruct((2, n, 6, 8, 128), F32) for _, n in BLOCKS for _ in range(2)),
        compiler_params=pltpu.CompilerParams(vmem_limit_bytes=VMEM_LIMIT),
        cost_estimate=pl.CostEstimate(flops=0, bytes_accessed=3000000, transcendentals=0),
        name="deal",
    )(scalars, tiles)
    return [outs[2 * b : 2 * b + 2] for b in range(len(BLOCKS))]


def from_neighbour(payload, di, dj):
    pairs = [(device_of(i + di, j + dj), device_of(i, j)) for i in range(TILES_Y) for j in range(TILES_Z)]
    return lax.ppermute(payload, AXES, pairs)


def rows_beside(low, high):
    return from_neighbour(high, -1, 0), from_neighbour(low, 1, 0)


def columns_beside(columns):
    return from_neighbour(columns[1], 0, -1), from_neighbour(columns[0], 0, 1)


def columns_kernel(low, high, up, down, *refs):
    for rz, ref in enumerate(refs[-2:]):

        def position(i, carry, rz=rz, ref=ref):
            for u in range(6):
                arrays = [r[rz, i, u] for r in (up, low, high, down)]
                for k, v in enumerate(swap_bits(arrays, [(1, 6), (0, 5)])):
                    ref[k, i, u] = v
            return carry

        lax.fori_loop(0, ref.shape[1], position, 0)


def columns(low, high, up, down, after=(), held=()):
    n = low.shape[1]
    outs = pl.pallas_call(
        lambda *refs: columns_kernel(*refs[:4], *refs[-2:]),
        in_specs=[VMEM] * 4 + [ANY] * (len(after) + len(held)),
        out_specs=(ANY,) * len(held) + (VMEM,) * 2,
        out_shape=tuple(jax.ShapeDtypeStruct(h.shape, F32) for h in held)
        + (jax.ShapeDtypeStruct((4, n, 6, 8, 128), F32),) * 2,
        input_output_aliases={4 + len(after) + k: k for k in range(len(held))},
        compiler_params=pltpu.CompilerParams(vmem_limit_bytes=VMEM_LIMIT),
        cost_estimate=pl.CostEstimate(flops=0, bytes_accessed=n * 800000, transcendentals=0),
        name="columns",
    )(low, high, up, down, *after, *held)
    return outs[-2:], outs[:-2]


def assemble(tile, p, u, first_half, second_half, left, right):
    pieces = [ref[k, p, u] for k in range(4) for ref in (left, first_half, second_half, right)]
    whole = swap_bits(pieces, [(1, 4), (0, 3)])
    return [jnp.where(tile.inside, v, 0.0) for v in whole]


def quarters(arrays):
    lane = lanes()
    merged = []
    for k in range(8):
        merged.append(jnp.where(lane < 64, roll(arrays[k], -40), roll(arrays[k + 8], 24)))
    merged = [
        jnp.where((lane >> 4) % 2 == 0, merged[k], roll(merged[k + 2], 16)) for k in (0, 1, 4, 5)
    ]
    merged = swap_bits(merged, [(1, 5), (0, 3)])
    return [[merged[2 * ry + rz] for rz in range(2)] for ry in range(2)]


def core_rows(arrays):
    lane = lanes()
    merged = [jnp.where(lane < 64, roll(arrays[k], -40), roll(arrays[k + 4], 24)) for k in range(4)]
    merged = [jnp.where((lane >> 4) % 2 == 0, merged[k], roll(merged[k + 1], 16)) for k in (0, 2)]
    return swap_bits(merged, [(0, 5)])


class Tile:
    def __init__(self, scalars):
        lane, row = lanes(), rows()
        y = EDGE * scalars[3] - RIM + 8 * (lane // 32)
        z = EDGE * scalars[4] - RIM + lane % 32
        self.inside = (y >= 0) & (y < 128) & (z >= 0) & (z < 256)
        self.below_top, self.above_bottom = row < 7, row > 0

    def around(self, load, f, xp, ys):
        mid = load(f, xp, ys)
        total = roll(mid, -1) + roll(mid, 1)
        total = total + (load(f, xp, ys + 1) if ys < 7 else roll(load(f, xp, 0), -32))
        total = total + (load(f, xp, ys - 1) if ys > 0 else roll(load(f, xp, 7), 32))
        other = load(f, 1 - xp, ys)
        if xp == 0:
            far = jnp.where(self.above_bottom, roll(other, 1, 0), 0.0)
        else:
            far = jnp.where(self.below_top, roll(other, -1, 0), 0.0)
        return total + (other + far), mid

    def tendency(self, load, xp, ys):
        around_p, p = self.around(load, 0, xp, ys)
        around_v, v = self.around(load, 1, xp, ys)
        reaction = (1.0 - p) * (v * v)
        rate_p = 0.2 * around_p + (reaction - 1.24 * p)
        rate_v = 0.1 * around_v + (reaction - 0.7 * v)
        return (jnp.where(self.inside, rate_p, 0.0), jnp.where(self.inside, rate_v, 0.0)), (p, v)


CELLS = [(xp, ys) for ys in range(8) for xp in range(2)]
FIELD = (2, 2, 8, 8, 128)


def reader(ref, *at):
    return lambda f, xp, ys: ref[at + (f, xp, ys)]


def sweep_kernel(first, begin, count, scalars, *refs):
    halo, (out_ref, start_ref, old, one, two, ahead, rate, base) = refs[:4], refs[-8:]
    tile = Tile(scalars)

    def position(at, carry):
        for array in range(3):
            both = [assemble(tile, begin + at, 2 * array + f, *halo) for f in range(2)]
            for f in range(2):
                for (xp, ys), v in zip(CELLS, both[f], strict=True):
                    old[array, f, xp, ys] = v

        if first == begin == 0:

            @pl.when(at == 0)
            def _():
                start_ref[...] = old[0]

        for xp, ys in CELLS:
            f0, y0 = tile.tendency(reader(old, 0), xp, ys)
            f1, _ = tile.tendency(reader(old, 1), xp, ys)
            f2, _ = tile.tendency(reader(old, 2), xp, ys)
            for f in range(2):
                one[f, xp, ys] = y0[f] + (5 * H / 24) * f0[f] + ((H / 3) * f1[f] - (H / 24) * f2[f])
                base[f, xp, ys] = (H / 6) * (f1[f] + f2[f]) - (5 * H / 6) * f0[f]
                ahead[f, xp, ys] = y0[f] + H * f0[f]
        for xp, ys in CELLS:
            r1, _ = tile.tendency(reader(one), xp, ys)
            for f in range(2):
                correction = base[f, xp, ys] + (H / 2) * r1[f]
                base[f, xp, ys] = correction
                two[f, xp, ys] = ahead[f, xp, ys] + correction
                rate[f, xp, ys] = r1[f]
        for xp, ys in CELLS:
            r2, _ = tile.tendency(reader(two), xp, ys)
            for f in range(2):
                r1 = rate[f, xp, ys]
                one[f, xp, ys] = (H / 3) * r1 - (H / 24) * r2[f]
                ahead[f, xp, ys] = (H / 6) * (r1 + r2[f])
        out_ref[at, 0] = base[...]
        out_ref[at, 1] = one[...]
        out_ref[at, 2] = ahead[...]
        return carry

    lax.fori_loop(0, count, position, 0)


def sweep(scalars, halo, first, begin, count, after=()):
    field = pltpu.VMEM(FIELD, F32)
    return pl.pallas_call(
        functools.partial(sweep_kernel, first, begin, count),
        in_specs=[SMEM] + [VMEM] * 4 + [ANY] * len(after),
        out_specs=(VMEM,) * 2,
        scratch_shapes=[pltpu.VMEM((3,) + FIELD, F32)] + [field] * 5,
        out_shape=(jax.ShapeDtypeStruct((count, 3) + FIELD, F32), jax.ShapeDtypeStruct(FIELD, F32)),
        compiler_params=pltpu.CompilerParams(vmem_limit_bytes=VMEM_LIMIT),
        cost_estimate=pl.CostEstimate(flops=count * 5 * 32 * 1024 * 40, bytes_accessed=count * 1200000, transcendentals=0),
        name=f"sweep_{first + begin}",
    )(scalars, *halo, *after)


def write_packs(ref, at, loads):
    values = {}
    for array, load in enumerate(loads):
        for f in range(2):
            for xp in range(2):
                for ry, v in enumerate(core_rows([load(f, xp, ys) for ys in range(8)])):
                    values[ry * 12 + array * 4 + f * 2 + xp] = v
    for r, v in values.items():
        ref[at, r] = v


def pack_kernel(in_ref, *refs):
    out_ref = refs[-1]

    def position(i, carry):
        write_packs(out_ref, i, [reader(in_ref, i, array) for array in range(3)])
        return carry

    lax.fori_loop(0, out_ref.shape[0], position, 0)


def pack(raw, after=()):
    count = raw.shape[0]
    return pl.pallas_call(
        pack_kernel,
        in_specs=[VMEM] + [ANY] * len(after),
        out_specs=VMEM,
        out_shape=jax.ShapeDtypeStruct((count, 24, 8, 128), F32),
        compiler_params=pltpu.CompilerParams(vmem_limit_bytes=VMEM_LIMIT),
        cost_estimate=pl.CostEstimate(flops=count * 1000000, bytes_accessed=count * 500000, transcendentals=0),
        name="pack",
    )(raw, *after)


def chain_kernel(first, count, scalars, *refs):
    tile = Tile(scalars)
    last = first + count >= SLABS
    z, late, corr, one, two, ahead, next_z, next_late = refs[-8:]
    parts = 1 if first == 0 else 2
    swept, refs = refs[:parts], refs[parts:-8]
    take_first = scalars[1] > 0
    if first == 0:
        start_ref, refs = refs[0], refs[1:]
        z[...] = start_ref[...]
    else:
        for k, ref in enumerate((z, late, corr)):
            both = [assemble(tile, 0, 2 * k + f, *refs[:4]) for f in range(2)]
            for f in range(2):
                for (xp, ys), v in zip(CELLS, both[f], strict=True):
                    ref[f, xp, ys] = v
        refs = refs[4:]
    raw = refs[-1] if last else refs[0]

    def step(at, sweeps=None, j=None):
        final = sweeps is None
        p = first + at
        reset = (p == 0) | ((p == 1) & take_first)
        for xp, ys in CELLS:
            fl, l = tile.tendency(reader(late), xp, ys)
            f0, y0 = tile.tendency(reader(z), xp, ys)
            for f in range(2):
                next_late[f, xp, ys] = jnp.where(reset, y0[f], l[f] + H * fl[f] + corr[f, xp, ys])
                g = y0[f] + H * f0[f]
                ahead[f, xp, ys] = g
                if final:
                    one[f, xp, ys] = y0[f] + (H / 2) * f0[f]
                    two[f, xp, ys] = (-H / 2) * f0[f]
                else:
                    next_z[f, xp, ys] = g + sweeps[j, 0, f, xp, ys]
                    one[f, xp, ys] = y0[f] + (5 * H / 24) * f0[f] + sweeps[j, 1, f, xp, ys]
                    two[f, xp, ys] = sweeps[j, 2, f, xp, ys] - (5 * H / 6) * f0[f]
        for xp, ys in CELLS:
            f1, _ = tile.tendency(reader(one), xp, ys)
            for f in range(2):
                c = two[f, xp, ys] + (H / 2) * f1[f]
                corr[f, xp, ys] = c
                two[f, xp, ys] = ahead[f, xp, ys] + c
        late[...] = next_late[...]
        if not final:
            z[...] = next_z[...]
        raw[at, 0] = next_late[...]
        raw[at, 1] = one[...]
        raw[at, 2] = two[...]

    at = 0
    for ref in swept:

        def looped(j, carry, at=at, ref=ref):
            step(at + j, ref, j)
            return carry

        lax.fori_loop(0, ref.shape[0], looped, 0)
        at += ref.shape[0]

    if not last:
        _, low_ref, high_ref = refs
        for k, ref in enumerate((z, late, corr)):
            both = [quarters([ref[f, xp, ys] for xp, ys in CELLS]) for f in range(2)]
            for f in range(2):
                for ry, half_ref in enumerate((low_ref, high_ref)):
                    for rz in range(2):
                        half_ref[rz, 0, 2 * k + f] = both[f][ry][rz]
        return

    step(count)
    for xp, ys in CELLS:
        fl, l = tile.tendency(reader(late), xp, ys)
        for f in range(2):
            raw[count + 1, 0, f, xp, ys] = l[f] + H * fl[f] + corr[f, xp, ys]
    leader, conv_one, conv_two = scalars[0], scalars[1] > 0, scalars[2] > 0
    *earlier, out_ref, packs, _ = refs

    def pack_at(i, carry):
        write_packs(packs, i, [reader(raw, i, array) for array in range(3)])
        return carry

    lax.fori_loop(0, count + 2, pack_at, 0)

    def put(p, ref, i, newest=False):
        base = lax.rem(leader + p, SLABS) * SLAB_ROWS
        for ry in range(2):
            for array in range(3):
                for k in range(4):
                    r = ry * 12 + array * 4 + k
                    out_ref[pl.ds(base + r, 8, stride=24)] = ref[i, ry * 12 + k] if newest else ref[i, r]

    for b, ref in enumerate((*earlier, packs)):

        def move(i, carry, b=b, ref=ref):
            put(BLOCKS[b][0] + i, ref, i)
            return carry

        lax.fori_loop(0, BLOCKS[b][1], move, 0)

    @pl.when(conv_one)
    def _():
        put(0, packs, count)

    @pl.when(conv_two & conv_one)
    def _():
        put(1, packs, count + 1, newest=True)

    @pl.when(conv_two & jnp.logical_not(conv_one))
    def _():
        put(0, packs, count, newest=True)


def chain(scalars, first, count, inputs):
    last = first + count >= SLABS
    if last:
        out_shape = jax.ShapeDtypeStruct((SLABS * SLAB_ROWS, 128), F32)
        scratch = [pltpu.VMEM((count + 2, 24, 8, 128), F32), pltpu.VMEM((count + 2, 3) + FIELD, F32)]
    else:
        out_shape = (jax.ShapeDtypeStruct((count, 3) + FIELD, F32),)
        out_shape += (jax.ShapeDtypeStruct((2, 1, 6, 8, 128), F32),) * 2
        scratch = []
    return pl.pallas_call(
        functools.partial(chain_kernel, first, count),
        in_specs=[SMEM] + [VMEM] * len(inputs),
        out_specs=VMEM if last else (VMEM,) * 3,
        scratch_shapes=scratch + [pltpu.VMEM(FIELD, F32)] * 8,
        out_shape=out_shape,
        compiler_params=pltpu.CompilerParams(vmem_limit_bytes=VMEM_LIMIT),
        cost_estimate=pl.CostEstimate(flops=count * 3 * 32 * 1024 * 40, bytes_accessed=count * 500000, transcendentals=0),
        name=f"chain_{first}",
    )(scalars, *inputs)


def body(slab_starts, slab_nodes, first_slab, converged):
    ti, tj = own_tile()
    scalars = jnp.stack([first_slab[0], converged[0], converged[1], ti.astype(jnp.int32), tj.astype(jnp.int32)])
    chunks = spread(slab_starts[0], slab_nodes[0])
    tiles = lax.all_to_all(chunks.reshape(128, 24, 128), AXES, 0, 0, tiled=True).reshape(SLABS * SLAB_ROWS, 128)

    half_a, half_b, half_c = deal(scalars, tiles)

    rows = rows_beside(*half_a)
    columns_a, half_b = columns(*half_a, *rows, held=half_b)
    beside = columns_beside(columns_a)
    rows = rows_beside(*half_b)
    columns_b, half_c = columns(*half_b, *rows, after=beside, held=half_c)
    beside_b = columns_beside(columns_b)
    rows_c = rows_beside(*half_c)
    swept, start = sweep(scalars, [*columns_a, *beside], 0, 0, 6, after=columns_b)
    raw, *state = chain(scalars, *BLOCKS[0], [swept, start])

    rows = rows_beside(*state)
    columns_c, _ = columns(*half_c, *rows_c, after=state)
    beside_c = columns_beside(columns_c)
    halo_b = [*columns_b, *beside_b]
    swept, _ = sweep(scalars, halo_b, 6, 0, 3, after=columns_c)
    inside, _ = columns(*state, *rows, after=[swept])
    beside = columns_beside(inside)
    more, _ = sweep(scalars, halo_b, 6, 3, 3, after=inside)
    raw_b, *state = chain(scalars, *BLOCKS[1], [swept, more, *inside, *beside])

    rows = rows_beside(*state)
    halo_c = [*columns_c, *beside_c]
    packs_a = pack(raw, after=state)
    swept, _ = sweep(scalars, halo_c, 12, 0, 2, after=state)
    inside, _ = columns(*state, *rows, after=[swept, packs_a])
    beside = columns_beside(inside)
    more, _ = sweep(scalars, halo_c, 12, 2, 2, after=inside)
    packs_b = pack(raw_b, after=inside)
    out = chain(scalars, *BLOCKS[2], [swept, more, *inside, *beside, packs_a, packs_b])
    out = lax.all_to_all(out.reshape(128, 24, 128), AXES, 0, 0, tiled=True)
    starts, nodes = collect(out.reshape(128 * 24, 128))
    return starts[None], nodes[None]


def solution(mesh):
    slab_spec = P("tm", None, "space", None, None)
    node_spec = P("tm", None, None, "space", None, None)
    return jax.shard_map(
        body,
        mesh=mesh,
        in_specs=(slab_spec, node_spec, P(), P()),
        out_specs=(slab_spec, node_spec),
        check_vma=False,
    )
```

```python
import functools

import jax
import jax.numpy as jnp
from jax import lax
from jax.experimental import pallas as pl
from jax.experimental.pallas import tpu as pltpu
from jax.sharding import PartitionSpec as P

SLABS = 16
TILES_Y = 8
TILES_Z = 16
EDGE = 16
RIM = 8
BLOCKS = ((0, 6), (6, 6), (12, 4))
SETS = ((0, 6), (6, 10))
H = 0.5
AXES = ("tm", "space")
F32 = jnp.float32
VMEM_LIMIT = 40 * 1024 * 1024
SHAPE = (8, 128)
VMEM = pl.BlockSpec(memory_space=pltpu.VMEM)
SMEM = pl.BlockSpec(memory_space=pltpu.SMEM)
ANY = pl.BlockSpec(memory_space=pl.ANY)
HBM = pl.BlockSpec(memory_space=pltpu.HBM)
SLAB_ROWS = 192


def device_of(i, j):
    i, j = i % TILES_Y, j % TILES_Z
    zb, x = (0, i) if i < 4 else (1, 7 - i)
    cj = j // 2
    core = (j % 2) ^ (cj % 2)
    za, y = (0, cj) if cj < 4 else (1, 7 - cj)
    zl = za ^ zb
    return (y * 4 + za * 2 + core) * 8 + zl * 4 + x


def own_tile():
    tm, space = lax.axis_index("tm"), lax.axis_index("space")
    y, za, core = tm // 4, (tm // 2) % 2, tm % 2
    zl, x = space // 4, space % 4
    zb = za ^ zl
    ti = jnp.where(zb == 0, x, 7 - x)
    cj = jnp.where(za == 0, y, 7 - y)
    return ti, 2 * cj + (core ^ (cj % 2))


def roll(v, by, axis=1):
    by %= v.shape[axis]
    return v if by == 0 else pltpu.roll(v, by, axis)


def lanes():
    return lax.broadcasted_iota(jnp.int32, SHAPE, 1)


def rows():
    return lax.broadcasted_iota(jnp.int32, SHAPE, 0)


def swap_bits(arrays, pairs):
    arrays, lane = list(arrays), lanes()
    for index_bit, lane_bit in pairs:
        step, low = 1 << lane_bit, (lane >> lane_bit) % 2 == 0
        across = lane ^ step
        for a in range(len(arrays)):
            b = a | (1 << index_bit)
            if a != b:
                u, v = arrays[a], arrays[b]
                moved = jnp.where(low, v, u)
                moved = roll(moved, 64) if step == 64 else jnp.take_along_axis(moved, across, axis=1)
                arrays[a] = jnp.where(low, u, moved)
                arrays[b] = jnp.where(low, moved, v)
    return arrays


def turn_pairs(v):
    v = roll(v, 4, 0)
    return jnp.where(rows() // 2 % 2 == 0, roll(v, -2, 0), roll(v, 2, 0))


def spread_kernel(starts_ref, nodes_ref, out_ref, planes, arrived):
    def copies(u):
        source = starts_ref if u < 2 else nodes_ref.at[u // 2 - 1]
        return [
            pltpu.make_async_copy(
                source.at[u % 2, xp, :, pl.ds(128 * half, 128)], planes.at[u, xp, half], arrived.at[4 * u + 2 * xp + half]
            )
            for xp in range(2)
            for half in range(2)
        ]

    for u in range(6):
        for copy in copies(u):
            copy.start()

    def unit(u):
        row = u // 2 * 4 + u % 2 * 2
        for half in range(2):
            for upper in range(2):
                loads = [
                    planes[u, xp, half, pl.ds(64 * upper + ys, 8, stride=8)] for ys in range(8) for xp in range(2)
                ]
                for k, v in enumerate(swap_bits(loads, [(3, 6), (2, 5), (1, 4), (0, 3)])):
                    tj, rz = 8 * half + k // 2, k % 2
                    device = device_of(7 if upper else 0, tj)
                    out_ref[pl.ds(device * 24 + rz + row, 8, stride=12)] = turn_pairs(v) if upper else v

    for copy in copies(0) + copies(1):
        copy.wait()

    def pair(k, carry):
        for n in (1, 2):

            @pl.when(k == n)
            def _(n=n):
                for copy in copies(2 * n) + copies(2 * n + 1):
                    copy.wait()

        lax.fori_loop(2 * k, 2 * k + 2, lambda u, c: (unit(u), c)[1], 0)
        return carry

    lax.fori_loop(0, 3, pair, 0)


def spread(starts, nodes):
    return pl.pallas_call(
        spread_kernel,
        in_specs=[HBM, HBM],
        out_specs=VMEM,
        out_shape=jax.ShapeDtypeStruct((128 * 24, 128), F32),
        scratch_shapes=[pltpu.VMEM((6, 2, 2, 128, 128), F32), pltpu.SemaphoreType.DMA((24,))],
        compiler_params=pltpu.CompilerParams(vmem_limit_bytes=VMEM_LIMIT),
        name="spread",
    )(starts, nodes)


def collect_kernel(in_ref, starts_ref, nodes_ref, planes, left):
    def unit(u, carry):
        for half in range(2):
            for upper in range(2):
                loads = []
                for t in range(8):
                    device = device_of(7 if upper else 0, 8 * half + t)
                    v = in_ref[pl.ds(device * 24 + u, 8, stride=12)]
                    loads.append(turn_pairs(v) if upper else v)
                for ys, v in enumerate(swap_bits(loads, [(2, 6), (1, 5), (0, 4)])):
                    planes[u, half, pl.ds(64 * upper + ys, 8, stride=8)] = v
        return carry

    def copies(array):
        target = starts_ref if array == 0 else nodes_ref.at[array - 1]
        return [
            pltpu.make_async_copy(
                planes.at[4 * array + 2 * f + xp, half],
                target.at[f, xp, :, pl.ds(128 * half, 128)],
                left.at[8 * array + 4 * f + 2 * xp + half],
            )
            for f in range(2)
            for xp in range(2)
            for half in range(2)
        ]

    def array_at(k, carry):
        lax.fori_loop(4 * k, 4 * k + 4, unit, 0)
        for n in range(3):

            @pl.when(k == n)
            def _(n=n):
                for copy in copies(n):
                    copy.start()

        return carry

    lax.fori_loop(0, 3, array_at, 0)
    for n in range(3):
        for copy in copies(n):
            copy.wait()


def collect(tiles):
    return pl.pallas_call(
        collect_kernel,
        out_shape=(
            jax.ShapeDtypeStruct((2, 2, 128, 256), F32),
            jax.ShapeDtypeStruct((2, 2, 2, 128, 256), F32),
        ),
        in_specs=[VMEM],
        out_specs=(ANY, ANY),
        scratch_shapes=[pltpu.VMEM((12, 2, 128, 128), F32), pltpu.SemaphoreType.DMA((24,))],
        compiler_params=pltpu.CompilerParams(vmem_limit_bytes=VMEM_LIMIT),
        name="collect",
    )(tiles)


def deal_kernel(scalars, in_ref, *out_refs):
    for b, (first, count) in enumerate(SETS):

        def position(i, carry, b=b, first=first):
            base = lax.rem(scalars[0] + (first + i), SLABS) * SLAB_ROWS
            for u in range(6):
                for ry in range(2):
                    for rz in range(2):
                        v = in_ref[pl.ds(base + ry * 12 + 2 * u + rz, 8, stride=24)]
                        out_refs[2 * b + ry][rz, i, u] = v
            return carry

        lax.fori_loop(0, count, position, 0)


def deal(scalars, tiles):
    outs = pl.pallas_call(
        deal_kernel,
        in_specs=[SMEM, VMEM],
        out_specs=(VMEM,) * (2 * len(SETS)),
        out_shape=tuple(jax.ShapeDtypeStruct((2, n, 6, 8, 128), F32) for _, n in SETS for _ in range(2)),
        compiler_params=pltpu.CompilerParams(vmem_limit_bytes=VMEM_LIMIT),
        cost_estimate=pl.CostEstimate(flops=0, bytes_accessed=3000000, transcendentals=0),
        name="deal",
    )(scalars, tiles)
    return [outs[2 * b : 2 * b + 2] for b in range(len(SETS))]


def from_neighbour(payload, di, dj):
    pairs = [(device_of(i + di, j + dj), device_of(i, j)) for i in range(TILES_Y) for j in range(TILES_Z)]
    return lax.ppermute(payload, AXES, pairs)


def rows_beside(low, high):
    return from_neighbour(high, -1, 0), from_neighbour(low, 1, 0)


def columns_beside(columns):
    return from_neighbour(columns[1], 0, -1), from_neighbour(columns[0], 0, 1)


def columns_kernel(low, high, up, down, *refs):
    for rz, ref in enumerate(refs[-2:]):

        def position(i, carry, rz=rz, ref=ref):
            for u in range(6):
                arrays = [r[rz, i, u] for r in (up, low, high, down)]
                for k, v in enumerate(swap_bits(arrays, [(1, 6), (0, 5)])):
                    ref[k, i, u] = v
            return carry

        lax.fori_loop(0, ref.shape[1], position, 0)


def columns(low, high, up, down, after=(), held=()):
    n = low.shape[1]
    outs = pl.pallas_call(
        lambda *refs: columns_kernel(*refs[:4], *refs[-2:]),
        in_specs=[VMEM] * 4 + [ANY] * (len(after) + len(held)),
        out_specs=(ANY,) * len(held) + (VMEM,) * 2,
        out_shape=tuple(jax.ShapeDtypeStruct(h.shape, F32) for h in held)
        + (jax.ShapeDtypeStruct((4, n, 6, 8, 128), F32),) * 2,
        input_output_aliases={4 + len(after) + k: k for k in range(len(held))},
        compiler_params=pltpu.CompilerParams(vmem_limit_bytes=VMEM_LIMIT),
        cost_estimate=pl.CostEstimate(flops=0, bytes_accessed=n * 800000, transcendentals=0),
        name="columns",
    )(low, high, up, down, *after, *held)
    return outs[-2:], outs[:-2]


def assemble(tile, p, u, first_half, second_half, left, right):
    pieces = [ref[k, p, u] for k in range(4) for ref in (left, first_half, second_half, right)]
    whole = swap_bits(pieces, [(1, 4), (0, 3)])
    return [jnp.where(tile.inside, v, 0.0) for v in whole]


def quarters(arrays):
    lane = lanes()
    merged = []
    for k in range(8):
        merged.append(jnp.where(lane < 64, roll(arrays[k], -40), roll(arrays[k + 8], 24)))
    merged = [
        jnp.where((lane >> 4) % 2 == 0, merged[k], roll(merged[k + 2], 16)) for k in (0, 1, 4, 5)
    ]
    merged = swap_bits(merged, [(1, 5), (0, 3)])
    return [[merged[2 * ry + rz] for rz in range(2)] for ry in range(2)]


def core_rows(arrays):
    lane = lanes()
    merged = [jnp.where(lane < 64, roll(arrays[k], -40), roll(arrays[k + 4], 24)) for k in range(4)]
    merged = [jnp.where((lane >> 4) % 2 == 0, merged[k], roll(merged[k + 1], 16)) for k in (0, 2)]
    return swap_bits(merged, [(0, 5)])


class Tile:
    def __init__(self, scalars):
        lane, row = lanes(), rows()
        y = EDGE * scalars[3] - RIM + 8 * (lane // 32)
        z = EDGE * scalars[4] - RIM + lane % 32
        self.inside = (y >= 0) & (y < 128) & (z >= 0) & (z < 256)
        self.below_top, self.above_bottom = row < 7, row > 0

    def around(self, load, f, xp, ys):
        mid = load(f, xp, ys)
        total = roll(mid, -1) + roll(mid, 1)
        total = total + (load(f, xp, ys + 1) if ys < 7 else roll(load(f, xp, 0), -32))
        total = total + (load(f, xp, ys - 1) if ys > 0 else roll(load(f, xp, 7), 32))
        other = load(f, 1 - xp, ys)
        if xp == 0:
            far = jnp.where(self.above_bottom, roll(other, 1, 0), 0.0)
        else:
            far = jnp.where(self.below_top, roll(other, -1, 0), 0.0)
        return total + (other + far), mid

    def tendency(self, load, xp, ys):
        around_p, p = self.around(load, 0, xp, ys)
        around_v, v = self.around(load, 1, xp, ys)
        reaction = (1.0 - p) * (v * v)
        rate_p = 0.2 * around_p + (reaction - 1.24 * p)
        rate_v = 0.1 * around_v + (reaction - 0.7 * v)
        return (jnp.where(self.inside, rate_p, 0.0), jnp.where(self.inside, rate_v, 0.0)), (p, v)


CELLS = [(xp, ys) for ys in range(8) for xp in range(2)]
FIELD = (2, 2, 8, 8, 128)


def reader(ref, *at):
    return lambda f, xp, ys: ref[at + (f, xp, ys)]


def sweep_kernel(first, begin, count, scalars, *refs):
    halo, (out_ref, start_ref, old, one, two, ahead, rate, base) = refs[:4], refs[-8:]
    tile = Tile(scalars)

    def position(at, carry):
        for array in range(3):
            both = [assemble(tile, begin + at, 2 * array + f, *halo) for f in range(2)]
            for f in range(2):
                for (xp, ys), v in zip(CELLS, both[f], strict=True):
                    old[array, f, xp, ys] = v

        if first == begin == 0:

            @pl.when(at == 0)
            def _():
                start_ref[...] = old[0]

        for xp, ys in CELLS:
            f0, y0 = tile.tendency(reader(old, 0), xp, ys)
            f1, _ = tile.tendency(reader(old, 1), xp, ys)
            f2, _ = tile.tendency(reader(old, 2), xp, ys)
            for f in range(2):
                one[f, xp, ys] = y0[f] + (5 * H / 24) * f0[f] + ((H / 3) * f1[f] - (H / 24) * f2[f])
                base[f, xp, ys] = (H / 6) * (f1[f] + f2[f]) - (5 * H / 6) * f0[f]
                ahead[f, xp, ys] = y0[f] + H * f0[f]
        for xp, ys in CELLS:
            r1, _ = tile.tendency(reader(one), xp, ys)
            for f in range(2):
                correction = base[f, xp, ys] + (H / 2) * r1[f]
                base[f, xp, ys] = correction
                two[f, xp, ys] = ahead[f, xp, ys] + correction
                rate[f, xp, ys] = r1[f]
        for xp, ys in CELLS:
            r2, _ = tile.tendency(reader(two), xp, ys)
            for f in range(2):
                r1 = rate[f, xp, ys]
                one[f, xp, ys] = (H / 3) * r1 - (H / 24) * r2[f]
                ahead[f, xp, ys] = (H / 6) * (r1 + r2[f])
        out_ref[at, 0] = base[...]
        out_ref[at, 1] = one[...]
        out_ref[at, 2] = ahead[...]
        return carry

    lax.fori_loop(0, count, position, 0)


def sweep(scalars, halo, first, begin, count, after=()):
    field = pltpu.VMEM(FIELD, F32)
    return pl.pallas_call(
        functools.partial(sweep_kernel, first, begin, count),
        in_specs=[SMEM] + [VMEM] * 4 + [ANY] * len(after),
        out_specs=(VMEM,) * 2,
        scratch_shapes=[pltpu.VMEM((3,) + FIELD, F32)] + [field] * 5,
        out_shape=(jax.ShapeDtypeStruct((count, 3) + FIELD, F32), jax.ShapeDtypeStruct(FIELD, F32)),
        compiler_params=pltpu.CompilerParams(vmem_limit_bytes=VMEM_LIMIT),
        cost_estimate=pl.CostEstimate(flops=count * 5 * 32 * 1024 * 40, bytes_accessed=count * 1200000, transcendentals=0),
        name=f"sweep_{first + begin}",
    )(scalars, *halo, *after)


def write_packs(ref, at, loads):
    values = {}
    for array, load in enumerate(loads):
        for f in range(2):
            for xp in range(2):
                for ry, v in enumerate(core_rows([load(f, xp, ys) for ys in range(8)])):
                    values[ry * 12 + array * 4 + f * 2 + xp] = v
    for r, v in values.items():
        ref[at, r] = v


def pack_kernel(in_ref, *refs):
    out_ref = refs[-1]

    def position(i, carry):
        write_packs(out_ref, i, [reader(in_ref, i, array) for array in range(3)])
        return carry

    lax.fori_loop(0, out_ref.shape[0], position, 0)


def pack(raw, after=()):
    count = raw.shape[0]
    return pl.pallas_call(
        pack_kernel,
        in_specs=[VMEM] + [ANY] * len(after),
        out_specs=VMEM,
        out_shape=jax.ShapeDtypeStruct((count, 24, 8, 128), F32),
        compiler_params=pltpu.CompilerParams(vmem_limit_bytes=VMEM_LIMIT),
        cost_estimate=pl.CostEstimate(flops=count * 1000000, bytes_accessed=count * 500000, transcendentals=0),
        name="pack",
    )(raw, *after)


def chain_kernel(first, count, scalars, *refs):
    tile = Tile(scalars)
    last = first + count >= SLABS
    z, late, corr, one, two, ahead, next_z, next_late = refs[-8:]
    parts = 1 if first == 0 else 2
    swept, refs = refs[:parts], refs[parts:-8]
    take_first = scalars[1] > 0
    if first == 0:
        start_ref, refs = refs[0], refs[1:]
        z[...] = start_ref[...]
    else:
        for k, ref in enumerate((z, late, corr)):
            both = [assemble(tile, 0, 2 * k + f, *refs[:4]) for f in range(2)]
            for f in range(2):
                for (xp, ys), v in zip(CELLS, both[f], strict=True):
                    ref[f, xp, ys] = v
        refs = refs[4:]
    raw = refs[-1] if last else refs[0]

    def step(at, sweeps=None, j=None):
        final = sweeps is None
        p = first + at
        reset = (p == 0) | ((p == 1) & take_first)
        for xp, ys in CELLS:
            fl, l = tile.tendency(reader(late), xp, ys)
            f0, y0 = tile.tendency(reader(z), xp, ys)
            for f in range(2):
                next_late[f, xp, ys] = jnp.where(reset, y0[f], l[f] + H * fl[f] + corr[f, xp, ys])
                g = y0[f] + H * f0[f]
                ahead[f, xp, ys] = g
                if final:
                    one[f, xp, ys] = y0[f] + (H / 2) * f0[f]
                    two[f, xp, ys] = (-H / 2) * f0[f]
                else:
                    next_z[f, xp, ys] = g + sweeps[j, 0, f, xp, ys]
                    one[f, xp, ys] = y0[f] + (5 * H / 24) * f0[f] + sweeps[j, 1, f, xp, ys]
                    two[f, xp, ys] = sweeps[j, 2, f, xp, ys] - (5 * H / 6) * f0[f]
        for xp, ys in CELLS:
            f1, _ = tile.tendency(reader(one), xp, ys)
            for f in range(2):
                c = two[f, xp, ys] + (H / 2) * f1[f]
                corr[f, xp, ys] = c
                two[f, xp, ys] = ahead[f, xp, ys] + c
        late[...] = next_late[...]
        if not final:
            z[...] = next_z[...]
        raw[at, 0] = next_late[...]
        raw[at, 1] = one[...]
        raw[at, 2] = two[...]

    at = 0
    for ref in swept:

        def looped(j, carry, at=at, ref=ref):
            step(at + j, ref, j)
            return carry

        lax.fori_loop(0, ref.shape[0], looped, 0)
        at += ref.shape[0]

    if not last:
        _, low_ref, high_ref = refs
        for k, ref in enumerate((z, late, corr)):
            both = [quarters([ref[f, xp, ys] for xp, ys in CELLS]) for f in range(2)]
            for f in range(2):
                for ry, half_ref in enumerate((low_ref, high_ref)):
                    for rz in range(2):
                        half_ref[rz, 0, 2 * k + f] = both[f][ry][rz]
        return

    step(count)
    for xp, ys in CELLS:
        fl, l = tile.tendency(reader(late), xp, ys)
        for f in range(2):
            raw[count + 1, 0, f, xp, ys] = l[f] + H * fl[f] + corr[f, xp, ys]
    leader, conv_one, conv_two = scalars[0], scalars[1] > 0, scalars[2] > 0
    *earlier, out_ref, packs, _ = refs

    def pack_at(i, carry):
        write_packs(packs, i, [reader(raw, i, array) for array in range(3)])
        return carry

    lax.fori_loop(0, count + 2, pack_at, 0)

    def put(p, ref, i, newest=False):
        base = lax.rem(leader + p, SLABS) * SLAB_ROWS
        for ry in range(2):
            for array in range(3):
                for k in range(4):
                    r = ry * 12 + array * 4 + k
                    out_ref[pl.ds(base + r, 8, stride=24)] = ref[i, ry * 12 + k] if newest else ref[i, r]

    for b, ref in enumerate((*earlier, packs)):

        def move(i, carry, b=b, ref=ref):
            put(BLOCKS[b][0] + i, ref, i)
            return carry

        lax.fori_loop(0, BLOCKS[b][1], move, 0)

    @pl.when(conv_one)
    def _():
        put(0, packs, count)

    @pl.when(conv_two & conv_one)
    def _():
        put(1, packs, count + 1, newest=True)

    @pl.when(conv_two & jnp.logical_not(conv_one))
    def _():
        put(0, packs, count, newest=True)


def chain(scalars, first, count, inputs):
    last = first + count >= SLABS
    if last:
        out_shape = jax.ShapeDtypeStruct((SLABS * SLAB_ROWS, 128), F32)
        scratch = [pltpu.VMEM((count + 2, 24, 8, 128), F32), pltpu.VMEM((count + 2, 3) + FIELD, F32)]
    else:
        out_shape = (jax.ShapeDtypeStruct((count, 3) + FIELD, F32),)
        out_shape += (jax.ShapeDtypeStruct((2, 1, 6, 8, 128), F32),) * 2
        scratch = []
    return pl.pallas_call(
        functools.partial(chain_kernel, first, count),
        in_specs=[SMEM] + [VMEM] * len(inputs),
        out_specs=VMEM if last else (VMEM,) * 3,
        scratch_shapes=scratch + [pltpu.VMEM(FIELD, F32)] * 8,
        out_shape=out_shape,
        compiler_params=pltpu.CompilerParams(vmem_limit_bytes=VMEM_LIMIT),
        cost_estimate=pl.CostEstimate(flops=count * 3 * 32 * 1024 * 40, bytes_accessed=count * 500000, transcendentals=0),
        name=f"chain_{first}",
    )(scalars, *inputs)


def body(slab_starts, slab_nodes, first_slab, converged):
    ti, tj = own_tile()
    scalars = jnp.stack([first_slab[0], converged[0], converged[1], ti.astype(jnp.int32), tj.astype(jnp.int32)])
    chunks = spread(slab_starts[0], slab_nodes[0])
    tiles = lax.all_to_all(chunks.reshape(128, 24, 128), AXES, 0, 0, tiled=True).reshape(SLABS * SLAB_ROWS, 128)

    half_a, half_b = deal(scalars, tiles)

    rows = rows_beside(*half_a)
    columns_a, half_b = columns(*half_a, *rows, held=half_b)
    beside = columns_beside(columns_a)
    rows = rows_beside(*half_b)
    columns_b, _ = columns(*half_b, *rows, after=beside)
    halo = [*columns_b, *columns_beside(columns_b)]
    swept, start = sweep(scalars, [*columns_a, *beside], 0, 0, 6, after=columns_b)
    raw, *state = chain(scalars, *BLOCKS[0], [swept, start])

    rows = rows_beside(*state)
    swept, _ = sweep(scalars, halo, 6, 0, 3, after=state)
    inside, _ = columns(*state, *rows, after=[swept])
    beside = columns_beside(inside)
    more, _ = sweep(scalars, halo, 6, 3, 3, after=inside)
    raw_b, *state = chain(scalars, *BLOCKS[1], [swept, more, *inside, *beside])

    rows = rows_beside(*state)
    packs_a = pack(raw, after=state)
    swept, _ = sweep(scalars, halo, 6, 6, 2, after=state)
    inside, _ = columns(*state, *rows, after=[swept, packs_a])
    beside = columns_beside(inside)
    more, _ = sweep(scalars, halo, 6, 8, 2, after=inside)
    packs_b = pack(raw_b, after=inside)
    out = chain(scalars, *BLOCKS[2], [swept, more, *inside, *beside, packs_a, packs_b])
    out = lax.all_to_all(out.reshape(128, 24, 128), AXES, 0, 0, tiled=True)
    starts, nodes = collect(out.reshape(128 * 24, 128))
    return starts[None], nodes[None]


def solution(mesh):
    slab_spec = P("tm", None, "space", None, None)
    node_spec = P("tm", None, None, "space", None, None)
    return jax.shard_map(
        body,
        mesh=mesh,
        in_specs=(slab_spec, node_spec, P(), P()),
        out_specs=(slab_spec, node_spec),
        check_vma=False,
    )
```

```python
import functools

import jax
import jax.numpy as jnp
from jax import lax
from jax.experimental import pallas as pl
from jax.experimental.pallas import tpu as pltpu
from jax.sharding import PartitionSpec as P

SLABS = 16
TILES_Y = 8
TILES_Z = 16
EDGE = 16
RIM = 8
BLOCKS = ((0, 6), (6, 6), (12, 4))
SETS = ((0, 6), (6, 10))
H = 0.5
AXES = ("tm", "space")
F32 = jnp.float32
VMEM_LIMIT = 40 * 1024 * 1024
SHAPE = (8, 128)
VMEM = pl.BlockSpec(memory_space=pltpu.VMEM)
SMEM = pl.BlockSpec(memory_space=pltpu.SMEM)
ANY = pl.BlockSpec(memory_space=pl.ANY)
HBM = pl.BlockSpec(memory_space=pltpu.HBM)
SLAB_ROWS = 192


def device_of(i, j):
    i, j = i % TILES_Y, j % TILES_Z
    zb, x = (0, i) if i < 4 else (1, 7 - i)
    cj = j // 2
    core = (j % 2) ^ (cj % 2)
    za, y = (0, cj) if cj < 4 else (1, 7 - cj)
    zl = za ^ zb
    return (y * 4 + za * 2 + core) * 8 + zl * 4 + x


def own_tile():
    tm, space = lax.axis_index("tm"), lax.axis_index("space")
    y, za, core = tm // 4, (tm // 2) % 2, tm % 2
    zl, x = space // 4, space % 4
    zb = za ^ zl
    ti = jnp.where(zb == 0, x, 7 - x)
    cj = jnp.where(za == 0, y, 7 - y)
    return ti, 2 * cj + (core ^ (cj % 2))


def roll(v, by, axis=1):
    by %= v.shape[axis]
    return v if by == 0 else pltpu.roll(v, by, axis)


def lanes():
    return lax.broadcasted_iota(jnp.int32, SHAPE, 1)


def rows():
    return lax.broadcasted_iota(jnp.int32, SHAPE, 0)


def swap_bits(arrays, pairs):
    arrays, lane = list(arrays), lanes()
    for index_bit, lane_bit in pairs:
        step, low = 1 << lane_bit, (lane >> lane_bit) % 2 == 0
        across = lane ^ step
        for a in range(len(arrays)):
            b = a | (1 << index_bit)
            if a != b:
                u, v = arrays[a], arrays[b]
                moved = jnp.where(low, v, u)
                moved = roll(moved, 64) if step == 64 else jnp.take_along_axis(moved, across, axis=1)
                arrays[a] = jnp.where(low, u, moved)
                arrays[b] = jnp.where(low, moved, v)
    return arrays


def turn_blocks(arrays, width):
    n, block = len(arrays), lanes() // width
    arrays = [roll(arrays[-k % n], width * (-k % n)) for k in range(n)]
    step = 1
    while step < n:
        here = block // step % 2 == 0
        arrays = [jnp.where(here, arrays[k], arrays[(k - step) % n]) for k in range(n)]
        step *= 2
    return [roll(v, -width * k) for k, v in enumerate(arrays)]


def turn_pairs(v):
    v = roll(v, 4, 0)
    return jnp.where(rows() // 2 % 2 == 0, roll(v, -2, 0), roll(v, 2, 0))


def spread_kernel(starts_ref, nodes_ref, out_ref, planes, arrived):
    def copies(u):
        source = starts_ref if u < 2 else nodes_ref.at[u // 2 - 1]
        return [
            pltpu.make_async_copy(
                source.at[u % 2, xp, :, pl.ds(128 * half, 128)], planes.at[u, xp, half], arrived.at[4 * u + 2 * xp + half]
            )
            for xp in range(2)
            for half in range(2)
        ]

    for u in range(6):
        for copy in copies(u):
            copy.start()

    def unit(u):
        row = u // 2 * 4 + u % 2 * 2
        for half in range(2):
            found = []
            for upper in range(2):
                loads = [
                    planes[u, xp, half, pl.ds(64 * upper + ys, 8, stride=8)] for ys in range(8) for xp in range(2)
                ]
                for k, v in enumerate(turn_blocks(loads, 8)):
                    tj, rz = 8 * half + k // 2, k % 2
                    at = device_of(7 if upper else 0, tj) * 24 + rz
                    found.append((at, turn_pairs(v) if upper else v))
            for at, v in found:
                out_ref[pl.ds(at + row, 8, stride=12)] = v

    for copy in copies(0) + copies(1):
        copy.wait()

    def pair(k, carry):
        for n in (1, 2):

            @pl.when(k == n)
            def _(n=n):
                for copy in copies(2 * n) + copies(2 * n + 1):
                    copy.wait()

        lax.fori_loop(2 * k, 2 * k + 2, lambda u, c: (unit(u), c)[1], 0)
        return carry

    lax.fori_loop(0, 3, pair, 0)


def spread(starts, nodes):
    return pl.pallas_call(
        spread_kernel,
        in_specs=[HBM, HBM],
        out_specs=VMEM,
        out_shape=jax.ShapeDtypeStruct((128 * 24, 128), F32),
        scratch_shapes=[pltpu.VMEM((6, 2, 2, 128, 128), F32), pltpu.SemaphoreType.DMA((24,))],
        compiler_params=pltpu.CompilerParams(vmem_limit_bytes=62 * 1024 * 1024),
        name="spread",
    )(starts, nodes)


def collect_kernel(in_ref, starts_ref, nodes_ref, planes, left):
    def unit(u, carry):
        found = []
        for half in range(2):
            for upper in range(2):
                loads = []
                for t in range(8):
                    device = device_of(7 if upper else 0, 8 * half + t)
                    v = in_ref[pl.ds(device * 24 + u, 8, stride=12)]
                    loads.append(turn_pairs(v) if upper else v)
                for ys, v in enumerate(turn_blocks(loads, 16)):
                    found.append((half, 64 * upper + ys, v))
        for half, at, v in found:
            planes[u, half, pl.ds(at, 8, stride=8)] = v
        return carry

    def copies(array):
        target = starts_ref if array == 0 else nodes_ref.at[array - 1]
        return [
            pltpu.make_async_copy(
                planes.at[4 * array + 2 * f + xp, half],
                target.at[f, xp, :, pl.ds(128 * half, 128)],
                left.at[8 * array + 4 * f + 2 * xp + half],
            )
            for f in range(2)
            for xp in range(2)
            for half in range(2)
        ]

    def array_at(k, carry):
        lax.fori_loop(4 * k, 4 * k + 4, unit, 0)
        for n in range(3):

            @pl.when(k == n)
            def _(n=n):
                for copy in copies(n):
                    copy.start()

        return carry

    lax.fori_loop(0, 3, array_at, 0)
    for n in range(3):
        for copy in copies(n):
            copy.wait()


def collect(tiles):
    return pl.pallas_call(
        collect_kernel,
        out_shape=(
            jax.ShapeDtypeStruct((2, 2, 128, 256), F32),
            jax.ShapeDtypeStruct((2, 2, 2, 128, 256), F32),
        ),
        in_specs=[VMEM],
        out_specs=(ANY, ANY),
        scratch_shapes=[pltpu.VMEM((12, 2, 128, 128), F32), pltpu.SemaphoreType.DMA((24,))],
        compiler_params=pltpu.CompilerParams(vmem_limit_bytes=VMEM_LIMIT),
        name="collect",
    )(tiles)


def deal_kernel(scalars, in_ref, *out_refs):
    for b, (first, count) in enumerate(SETS):

        def position(i, carry, b=b, first=first):
            base = lax.rem(scalars[0] + (first + i), SLABS) * SLAB_ROWS
            parts = [(u, ry, rz) for u in range(6) for ry in range(2) for rz in range(2)]
            values = [in_ref[pl.ds(base + ry * 12 + 2 * u + rz, 8, stride=24)] for u, ry, rz in parts]
            for (u, ry, rz), v in zip(parts, values, strict=True):
                out_refs[2 * b + ry][rz, i, u] = v
            return carry

        lax.fori_loop(0, count, position, 0)


def deal(scalars, tiles):
    outs = pl.pallas_call(
        deal_kernel,
        in_specs=[SMEM, VMEM],
        out_specs=(VMEM,) * (2 * len(SETS)),
        out_shape=tuple(jax.ShapeDtypeStruct((2, n, 6, 8, 128), F32) for _, n in SETS for _ in range(2)),
        compiler_params=pltpu.CompilerParams(vmem_limit_bytes=VMEM_LIMIT),
        cost_estimate=pl.CostEstimate(flops=0, bytes_accessed=3000000, transcendentals=0),
        name="deal",
    )(scalars, tiles)
    return [outs[2 * b : 2 * b + 2] for b in range(len(SETS))]


def from_neighbour(payload, di, dj):
    pairs = [(device_of(i + di, j + dj), device_of(i, j)) for i in range(TILES_Y) for j in range(TILES_Z)]
    return lax.ppermute(payload, AXES, pairs)


def rows_beside(low, high):
    return from_neighbour(high, -1, 0), from_neighbour(low, 1, 0)


def columns_beside(columns):
    return from_neighbour(columns[1], 0, -1), from_neighbour(columns[0], 0, 1)


def columns_kernel(low, high, up, down, *refs):
    def position(i, carry):
        values = [
            (ref, u, swap_bits([r[rz, i, u] for r in (up, low, high, down)], [(1, 6), (0, 5)]))
            for rz, ref in enumerate(refs[-2:])
            for u in range(6)
        ]
        for ref, u, arrays in values:
            for k, v in enumerate(arrays):
                ref[k, i, u] = v
        return carry

    lax.fori_loop(0, refs[-1].shape[1], position, 0)


def columns(low, high, up, down, after=(), held=()):
    n = low.shape[1]
    outs = pl.pallas_call(
        lambda *refs: columns_kernel(*refs[:4], *refs[-2:]),
        in_specs=[VMEM] * 4 + [ANY] * (len(after) + len(held)),
        out_specs=(ANY,) * len(held) + (VMEM,) * 2,
        out_shape=tuple(jax.ShapeDtypeStruct(h.shape, F32) for h in held)
        + (jax.ShapeDtypeStruct((4, n, 6, 8, 128), F32),) * 2,
        input_output_aliases={4 + len(after) + k: k for k in range(len(held))},
        compiler_params=pltpu.CompilerParams(vmem_limit_bytes=VMEM_LIMIT),
        cost_estimate=pl.CostEstimate(flops=0, bytes_accessed=n * 800000, transcendentals=0),
        name="columns",
    )(low, high, up, down, *after, *held)
    return outs[-2:], outs[:-2]


def assemble(tile, p, u, first_half, second_half, left, right):
    pieces = [ref[k, p, u] for k in range(4) for ref in (left, first_half, second_half, right)]
    whole = swap_bits(pieces, [(1, 4), (0, 3)])
    return [jnp.where(tile.inside, v, 0.0) for v in whole]


def quarters(arrays):
    lane = lanes()
    merged = []
    for k in range(8):
        merged.append(jnp.where(lane < 64, roll(arrays[k], -40), roll(arrays[k + 8], 24)))
    merged = [
        jnp.where((lane >> 4) % 2 == 0, merged[k], roll(merged[k + 2], 16)) for k in (0, 1, 4, 5)
    ]
    merged = swap_bits(merged, [(1, 5), (0, 3)])
    return [[merged[2 * ry + rz] for rz in range(2)] for ry in range(2)]


def core_rows(arrays):
    lane = lanes()
    merged = [jnp.where(lane < 64, roll(arrays[k], -40), roll(arrays[k + 4], 24)) for k in range(4)]
    merged = [jnp.where((lane >> 4) % 2 == 0, merged[k], roll(merged[k + 1], 16)) for k in (0, 2)]
    return swap_bits(merged, [(0, 5)])


class Tile:
    def __init__(self, scalars):
        lane, row = lanes(), rows()
        y = EDGE * scalars[3] - RIM + 8 * (lane // 32)
        z = EDGE * scalars[4] - RIM + lane % 32
        self.inside = (y >= 0) & (y < 128) & (z >= 0) & (z < 256)
        self.below_top, self.above_bottom = row < 7, row > 0

    def around(self, load, f, xp, ys):
        mid = load(f, xp, ys)
        total = roll(mid, -1) + roll(mid, 1)
        total = total + (load(f, xp, ys + 1) if ys < 7 else roll(load(f, xp, 0), -32))
        total = total + (load(f, xp, ys - 1) if ys > 0 else roll(load(f, xp, 7), 32))
        other = load(f, 1 - xp, ys)
        if xp == 0:
            far = jnp.where(self.above_bottom, roll(other, 1, 0), 0.0)
        else:
            far = jnp.where(self.below_top, roll(other, -1, 0), 0.0)
        return total + (other + far), mid

    def tendency(self, load, xp, ys):
        around_p, p = self.around(load, 0, xp, ys)
        around_v, v = self.around(load, 1, xp, ys)
        reaction = (1.0 - p) * (v * v)
        rate_p = 0.2 * around_p + (reaction - 1.24 * p)
        rate_v = 0.1 * around_v + (reaction - 0.7 * v)
        return (jnp.where(self.inside, rate_p, 0.0), jnp.where(self.inside, rate_v, 0.0)), (p, v)


CELLS = [(xp, ys) for ys in range(8) for xp in range(2)]
FIELD = (2, 2, 8, 8, 128)


def reader(ref, *at):
    return lambda f, xp, ys: ref[at + (f, xp, ys)]


def sweep_kernel(first, begin, count, scalars, *refs):
    halo, (out_ref, start_ref, old, one, two, ahead, rate, base) = refs[:4], refs[-8:]
    tile = Tile(scalars)

    def position(at, carry):
        for array in range(3):
            both = [assemble(tile, begin + at, 2 * array + f, *halo) for f in range(2)]
            for f in range(2):
                for (xp, ys), v in zip(CELLS, both[f], strict=True):
                    old[array, f, xp, ys] = v

        if first == begin == 0:

            @pl.when(at == 0)
            def _():
                start_ref[...] = old[0]

        for xp, ys in CELLS:
            f0, y0 = tile.tendency(reader(old, 0), xp, ys)
            f1, _ = tile.tendency(reader(old, 1), xp, ys)
            f2, _ = tile.tendency(reader(old, 2), xp, ys)
            for f in range(2):
                one[f, xp, ys] = y0[f] + (5 * H / 24) * f0[f] + ((H / 3) * f1[f] - (H / 24) * f2[f])
                base[f, xp, ys] = (H / 6) * (f1[f] + f2[f]) - (5 * H / 6) * f0[f]
                ahead[f, xp, ys] = y0[f] + H * f0[f]
        for xp, ys in CELLS:
            r1, _ = tile.tendency(reader(one), xp, ys)
            for f in range(2):
                correction = base[f, xp, ys] + (H / 2) * r1[f]
                base[f, xp, ys] = correction
                two[f, xp, ys] = ahead[f, xp, ys] + correction
                rate[f, xp, ys] = r1[f]
        for xp, ys in CELLS:
            r2, _ = tile.tendency(reader(two), xp, ys)
            for f in range(2):
                r1 = rate[f, xp, ys]
                one[f, xp, ys] = (H / 3) * r1 - (H / 24) * r2[f]
                ahead[f, xp, ys] = (H / 6) * (r1 + r2[f])
        out_ref[at, 0] = base[...]
        out_ref[at, 1] = one[...]
        out_ref[at, 2] = ahead[...]
        return carry

    lax.fori_loop(0, count, position, 0)


def sweep(scalars, halo, first, begin, count, after=()):
    field = pltpu.VMEM(FIELD, F32)
    return pl.pallas_call(
        functools.partial(sweep_kernel, first, begin, count),
        in_specs=[SMEM] + [VMEM] * 4 + [ANY] * len(after),
        out_specs=(VMEM,) * 2,
        scratch_shapes=[pltpu.VMEM((3,) + FIELD, F32)] + [field] * 5,
        out_shape=(jax.ShapeDtypeStruct((count, 3) + FIELD, F32), jax.ShapeDtypeStruct(FIELD, F32)),
        compiler_params=pltpu.CompilerParams(vmem_limit_bytes=VMEM_LIMIT),
        cost_estimate=pl.CostEstimate(flops=count * 5 * 32 * 1024 * 40, bytes_accessed=count * 1200000, transcendentals=0),
        name=f"sweep_{first + begin}",
    )(scalars, *halo, *after)


def pack_values(loads):
    values = {}
    for array, load in enumerate(loads):
        for f in range(2):
            for xp in range(2):
                for ry, v in enumerate(core_rows([load(f, xp, ys) for ys in range(8)])):
                    values[ry * 12 + array * 4 + f * 2 + xp] = v
    return values


def put(out_ref, scalars, p, values):
    base = lax.rem(scalars[0] + p, SLABS) * SLAB_ROWS
    for r, v in values.items():
        out_ref[pl.ds(base + r, 8, stride=24)] = v


def pack_kernel(first, scalars, raw, *refs):
    out_ref = refs[-1]
    if first > 0:
        out_ref[...] = refs[0][...]

    def position(i, carry):
        put(out_ref, scalars, first + i, pack_values([reader(raw, i, array) for array in range(3)]))
        return carry

    lax.fori_loop(0, raw.shape[0], position, 0)


def pack(scalars, first, raw, earlier=(), after=()):
    return pl.pallas_call(
        functools.partial(pack_kernel, first),
        in_specs=[SMEM, VMEM] + [VMEM] * len(earlier) + [ANY] * len(after),
        out_specs=VMEM,
        out_shape=jax.ShapeDtypeStruct((SLABS * SLAB_ROWS, 128), F32),
        compiler_params=pltpu.CompilerParams(vmem_limit_bytes=VMEM_LIMIT),
        cost_estimate=pl.CostEstimate(flops=6000000, bytes_accessed=3000000, transcendentals=0),
        name=f"pack_{first}",
    )(scalars, raw, *earlier, *after)


def chain_kernel(first, count, scalars, *refs):
    tile = Tile(scalars)
    last = first + count >= SLABS
    z, late, corr, one, two, ahead, next_z, next_late = refs[-8:]
    parts = 2 if last else 1
    swept, refs = refs[:parts], refs[parts:-8]
    take_first = scalars[1] > 0
    if first == 0:
        start_ref, refs = refs[0], refs[1:]
        z[...] = start_ref[...]
    else:
        for k, ref in enumerate((z, late, corr)):
            both = [assemble(tile, 0, 2 * k + f, *refs[:4]) for f in range(2)]
            for f in range(2):
                for (xp, ys), v in zip(CELLS, both[f], strict=True):
                    ref[f, xp, ys] = v
        refs = refs[4:]
    raw = refs[-1] if last else refs[0]

    def step(at, sweeps=None, j=None):
        final = sweeps is None
        p = first + at
        reset = (p == 0) | ((p == 1) & take_first)
        for xp, ys in CELLS:
            fl, l = tile.tendency(reader(late), xp, ys)
            f0, y0 = tile.tendency(reader(z), xp, ys)
            for f in range(2):
                next_late[f, xp, ys] = jnp.where(reset, y0[f], l[f] + H * fl[f] + corr[f, xp, ys])
                g = y0[f] + H * f0[f]
                ahead[f, xp, ys] = g
                if final:
                    one[f, xp, ys] = y0[f] + (H / 2) * f0[f]
                    two[f, xp, ys] = (-H / 2) * f0[f]
                else:
                    next_z[f, xp, ys] = g + sweeps[j, 0, f, xp, ys]
                    one[f, xp, ys] = y0[f] + (5 * H / 24) * f0[f] + sweeps[j, 1, f, xp, ys]
                    two[f, xp, ys] = sweeps[j, 2, f, xp, ys] - (5 * H / 6) * f0[f]
        for xp, ys in CELLS:
            f1, _ = tile.tendency(reader(one), xp, ys)
            for f in range(2):
                c = two[f, xp, ys] + (H / 2) * f1[f]
                corr[f, xp, ys] = c
                two[f, xp, ys] = ahead[f, xp, ys] + c
        late[...] = next_late[...]
        if not final:
            z[...] = next_z[...]
        raw[at, 0] = next_late[...]
        raw[at, 1] = one[...]
        raw[at, 2] = two[...]

    at = 0
    for ref in swept:

        def looped(j, carry, at=at, ref=ref):
            step(at + j, ref, j)
            return carry

        lax.fori_loop(0, ref.shape[0], looped, 0)
        at += ref.shape[0]

    if not last:
        _, low_ref, high_ref = refs
        for k, ref in enumerate((z, late, corr)):
            both = [quarters([ref[f, xp, ys] for xp, ys in CELLS]) for f in range(2)]
            for f in range(2):
                for ry, half_ref in enumerate((low_ref, high_ref)):
                    for rz in range(2):
                        half_ref[rz, 0, 2 * k + f] = both[f][ry][rz]
        return

    step(count)
    for xp, ys in CELLS:
        fl, l = tile.tendency(reader(late), xp, ys)
        for f in range(2):
            raw[count + 1, 0, f, xp, ys] = l[f] + H * fl[f] + corr[f, xp, ys]
    conv_one, conv_two = scalars[1] > 0, scalars[2] > 0
    earlier, out_ref, _ = refs
    out_ref[...] = earlier[...]

    def pack_at(i, carry):
        put(out_ref, scalars, first + i, pack_values([reader(raw, i, array) for array in range(3)]))
        return carry

    lax.fori_loop(0, count, pack_at, 0)

    @pl.when(conv_one)
    def _():
        put(out_ref, scalars, 0, pack_values([reader(raw, count, array) for array in range(3)]))

    @pl.when(conv_two)
    def _():
        at = jnp.where(conv_one, count + 1, count)
        values = pack_values([reader(raw, at, 0)])
        newest = {ry * 12 + array * 4 + k: values[ry * 12 + k] for ry in range(2) for array in range(3) for k in range(4)}
        put(out_ref, scalars, jnp.where(conv_one, 1, 0), newest)


def chain(scalars, first, count, inputs):
    last = first + count >= SLABS
    if last:
        out_shape = jax.ShapeDtypeStruct((SLABS * SLAB_ROWS, 128), F32)
        scratch = [pltpu.VMEM((count + 2, 3) + FIELD, F32)]
    else:
        out_shape = (jax.ShapeDtypeStruct((count, 3) + FIELD, F32),)
        out_shape += (jax.ShapeDtypeStruct((2, 1, 6, 8, 128), F32),) * 2
        scratch = []
    return pl.pallas_call(
        functools.partial(chain_kernel, first, count),
        in_specs=[SMEM] + [VMEM] * len(inputs),
        out_specs=VMEM if last else (VMEM,) * 3,
        scratch_shapes=scratch + [pltpu.VMEM(FIELD, F32)] * 8,
        out_shape=out_shape,
        compiler_params=pltpu.CompilerParams(vmem_limit_bytes=VMEM_LIMIT),
        cost_estimate=pl.CostEstimate(flops=count * 3 * 32 * 1024 * 40, bytes_accessed=count * 500000, transcendentals=0),
        name=f"chain_{first}",
    )(scalars, *inputs)


def body(slab_starts, slab_nodes, first_slab, converged):
    ti, tj = own_tile()
    scalars = jnp.stack([first_slab[0], converged[0], converged[1], ti.astype(jnp.int32), tj.astype(jnp.int32)])
    chunks = spread(slab_starts[0], slab_nodes[0])
    tiles = lax.all_to_all(chunks.reshape(128, 24, 128), AXES, 0, 0, tiled=True).reshape(SLABS * SLAB_ROWS, 128)

    half_a, half_b = deal(scalars, tiles)

    rows = rows_beside(*half_a)
    columns_a, half_b = columns(*half_a, *rows, held=half_b)
    beside = columns_beside(columns_a)
    rows = rows_beside(*half_b)
    columns_b, _ = columns(*half_b, *rows, after=beside)
    halo = [*columns_b, *columns_beside(columns_b)]
    swept, start = sweep(scalars, [*columns_a, *beside], 0, 0, 6, after=columns_b)
    raw, *state = chain(scalars, *BLOCKS[0], [swept, start])

    rows = rows_beside(*state)
    out = pack(scalars, 0, raw, after=state)
    inside, _ = columns(*state, *rows, after=[out])
    beside = columns_beside(inside)
    swept, _ = sweep(scalars, halo, 6, 0, 6, after=inside)
    raw, *state = chain(scalars, *BLOCKS[1], [swept, *inside, *beside])

    rows = rows_beside(*state)
    swept, _ = sweep(scalars, halo, 6, 6, 2, after=state)
    inside, _ = columns(*state, *rows, after=[swept])
    beside = columns_beside(inside)
    more, _ = sweep(scalars, halo, 6, 8, 2, after=inside)
    out = pack(scalars, 6, raw, [out], after=inside)
    out = chain(scalars, *BLOCKS[2], [swept, more, *inside, *beside, out])
    out = lax.all_to_all(out.reshape(128, 24, 128), AXES, 0, 0, tiled=True)
    starts, nodes = collect(out.reshape(128 * 24, 128))
    return starts[None], nodes[None]


def solution(mesh):
    slab_spec = P("tm", None, "space", None, None)
    node_spec = P("tm", None, None, "space", None, None)
    return jax.shard_map(
        body,
        mesh=mesh,
        in_specs=(slab_spec, node_spec, P(), P()),
        out_specs=(slab_spec, node_spec),
        check_vma=False,
    )
```

```python
import functools

import jax
import jax.numpy as jnp
from jax import lax
from jax.experimental import pallas as pl
from jax.experimental.pallas import tpu as pltpu
from jax.sharding import PartitionSpec as P

SLABS = 16
TILES_Y = 8
TILES_Z = 16
EDGE = 16
RIM = 8
BLOCKS = ((0, 6), (6, 6), (12, 4))
SETS = ((0, 6), (6, 10))
H = 0.5
AXES = ("tm", "space")
F32 = jnp.float32
VMEM_LIMIT = 40 * 1024 * 1024
SHAPE = (8, 128)
VMEM = pl.BlockSpec(memory_space=pltpu.VMEM)
SMEM = pl.BlockSpec(memory_space=pltpu.SMEM)
ANY = pl.BlockSpec(memory_space=pl.ANY)
HBM = pl.BlockSpec(memory_space=pltpu.HBM)
SLAB_ROWS = 192


def device_of(i, j):
    i, j = i % TILES_Y, j % TILES_Z
    zb, x = (0, i) if i < 4 else (1, 7 - i)
    cj = j // 2
    core = (j % 2) ^ (cj % 2)
    za, y = (0, cj) if cj < 4 else (1, 7 - cj)
    zl = za ^ zb
    return (y * 4 + za * 2 + core) * 8 + zl * 4 + x


def own_tile():
    tm, space = lax.axis_index("tm"), lax.axis_index("space")
    y, za, core = tm // 4, (tm // 2) % 2, tm % 2
    zl, x = space // 4, space % 4
    zb = za ^ zl
    ti = jnp.where(zb == 0, x, 7 - x)
    cj = jnp.where(za == 0, y, 7 - y)
    return ti, 2 * cj + (core ^ (cj % 2))


def roll(v, by, axis=1):
    by %= v.shape[axis]
    return v if by == 0 else pltpu.roll(v, by, axis)


def lanes():
    return lax.broadcasted_iota(jnp.int32, SHAPE, 1)


def rows():
    return lax.broadcasted_iota(jnp.int32, SHAPE, 0)


def swap_bits(arrays, pairs):
    arrays, lane = list(arrays), lanes()
    for index_bit, lane_bit in pairs:
        step, low = 1 << lane_bit, (lane >> lane_bit) % 2 == 0
        across = lane ^ step
        for a in range(len(arrays)):
            b = a | (1 << index_bit)
            if a != b:
                u, v = arrays[a], arrays[b]
                moved = jnp.where(low, v, u)
                moved = roll(moved, 64) if step == 64 else jnp.take_along_axis(moved, across, axis=1)
                arrays[a] = jnp.where(low, u, moved)
                arrays[b] = jnp.where(low, moved, v)
    return arrays


def turn_blocks(arrays, width):
    n, block = len(arrays), lanes() // width
    arrays = [roll(arrays[-k % n], width * (-k % n)) for k in range(n)]
    step = 1
    while step < n:
        here = block // step % 2 == 0
        arrays = [jnp.where(here, arrays[k], arrays[(k - step) % n]) for k in range(n)]
        step *= 2
    return [roll(v, -width * k) for k, v in enumerate(arrays)]


def turn_pairs(v):
    v = roll(v, 4, 0)
    return jnp.where(rows() // 2 % 2 == 0, roll(v, -2, 0), roll(v, 2, 0))


def spread_kernel(starts_ref, nodes_ref, out_ref, planes, arrived):
    def copies(u):
        source = starts_ref if u < 2 else nodes_ref.at[u // 2 - 1]
        return [
            pltpu.make_async_copy(
                source.at[u % 2, xp, :, pl.ds(128 * half, 128)], planes.at[u, xp, half], arrived.at[4 * u + 2 * xp + half]
            )
            for xp in range(2)
            for half in range(2)
        ]

    for u in range(6):
        for copy in copies(u):
            copy.start()

    def unit(u):
        row = u // 2 * 4 + u % 2 * 2
        for half in range(2):
            found = []
            for upper in range(2):
                loads = [
                    planes[u, xp, half, pl.ds(64 * upper + ys, 8, stride=8)] for ys in range(8) for xp in range(2)
                ]
                for k, v in enumerate(turn_blocks(loads, 8)):
                    tj, rz = 8 * half + k // 2, k % 2
                    at = device_of(7 if upper else 0, tj) * 24 + rz
                    found.append((at, turn_pairs(v) if upper else v))
            for at, v in found:
                out_ref[pl.ds(at + row, 8, stride=12)] = v

    for copy in copies(0) + copies(1):
        copy.wait()

    def pair(k, carry):
        for n in (1, 2):

            @pl.when(k == n)
            def _(n=n):
                for copy in copies(2 * n) + copies(2 * n + 1):
                    copy.wait()

        lax.fori_loop(2 * k, 2 * k + 2, lambda u, c: (unit(u), c)[1], 0)
        return carry

    lax.fori_loop(0, 3, pair, 0)


def spread(starts, nodes):
    return pl.pallas_call(
        spread_kernel,
        in_specs=[HBM, HBM],
        out_specs=VMEM,
        out_shape=jax.ShapeDtypeStruct((128 * 24, 128), F32),
        scratch_shapes=[pltpu.VMEM((6, 2, 2, 128, 128), F32), pltpu.SemaphoreType.DMA((24,))],
        compiler_params=pltpu.CompilerParams(vmem_limit_bytes=62 * 1024 * 1024),
        name="spread",
    )(starts, nodes)


def collect_kernel(in_ref, starts_ref, nodes_ref, planes, left):
    def unit(u, carry):
        found = []
        for half in range(2):
            for upper in range(2):
                loads = []
                for t in range(8):
                    device = device_of(7 if upper else 0, 8 * half + t)
                    v = in_ref[pl.ds(device * 24 + u, 8, stride=12)]
                    loads.append(turn_pairs(v) if upper else v)
                for ys, v in enumerate(turn_blocks(loads, 16)):
                    found.append((half, 64 * upper + ys, v))
        for half, at, v in found:
            planes[u, half, pl.ds(at, 8, stride=8)] = v
        return carry

    def copies(array):
        target = starts_ref if array == 0 else nodes_ref.at[array - 1]
        return [
            pltpu.make_async_copy(
                planes.at[4 * array + 2 * f + xp, half],
                target.at[f, xp, :, pl.ds(128 * half, 128)],
                left.at[8 * array + 4 * f + 2 * xp + half],
            )
            for f in range(2)
            for xp in range(2)
            for half in range(2)
        ]

    def array_at(k, carry):
        lax.fori_loop(4 * k, 4 * k + 4, unit, 0)
        for n in range(3):

            @pl.when(k == n)
            def _(n=n):
                for copy in copies(n):
                    copy.start()

        return carry

    lax.fori_loop(0, 3, array_at, 0)
    for n in range(3):
        for copy in copies(n):
            copy.wait()


def collect(tiles):
    return pl.pallas_call(
        collect_kernel,
        out_shape=(
            jax.ShapeDtypeStruct((2, 2, 128, 256), F32),
            jax.ShapeDtypeStruct((2, 2, 2, 128, 256), F32),
        ),
        in_specs=[VMEM],
        out_specs=(ANY, ANY),
        scratch_shapes=[pltpu.VMEM((12, 2, 128, 128), F32), pltpu.SemaphoreType.DMA((24,))],
        compiler_params=pltpu.CompilerParams(vmem_limit_bytes=VMEM_LIMIT),
        name="collect",
    )(tiles)


def deal_kernel(scalars, in_ref, *out_refs):
    for b, (first, count) in enumerate(SETS):

        def position(i, carry, b=b, first=first):
            base = lax.rem(scalars[0] + (first + i), SLABS) * SLAB_ROWS
            parts = [(u, ry, rz) for u in range(6) for ry in range(2) for rz in range(2)]
            values = [in_ref[pl.ds(base + ry * 12 + 2 * u + rz, 8, stride=24)] for u, ry, rz in parts]
            for (u, ry, rz), v in zip(parts, values, strict=True):
                out_refs[2 * b + ry][rz, i, u] = v
            return carry

        lax.fori_loop(0, count, position, 0)


def deal(scalars, tiles):
    outs = pl.pallas_call(
        deal_kernel,
        in_specs=[SMEM, VMEM],
        out_specs=(VMEM,) * (2 * len(SETS)),
        out_shape=tuple(jax.ShapeDtypeStruct((2, n, 6, 8, 128), F32) for _, n in SETS for _ in range(2)),
        compiler_params=pltpu.CompilerParams(vmem_limit_bytes=VMEM_LIMIT),
        cost_estimate=pl.CostEstimate(flops=0, bytes_accessed=3000000, transcendentals=0),
        name="deal",
    )(scalars, tiles)
    return [outs[2 * b : 2 * b + 2] for b in range(len(SETS))]


def from_neighbour(payload, di, dj):
    pairs = [(device_of(i + di, j + dj), device_of(i, j)) for i in range(TILES_Y) for j in range(TILES_Z)]
    return lax.ppermute(payload, AXES, pairs)


def rows_beside(low, high):
    return from_neighbour(high, -1, 0), from_neighbour(low, 1, 0)


def columns_beside(columns):
    return from_neighbour(columns[1], 0, -1), from_neighbour(columns[0], 0, 1)


def columns_kernel(ranges, low, high, up, down, *refs):
    for b, (first, count) in enumerate(ranges):

        def position(i, carry, first=first, outs=refs[2 * b : 2 * b + 2]):
            values = [
                (ref, u, swap_bits([r[rz, first + i, u] for r in (up, low, high, down)], [(1, 6), (0, 5)]))
                for rz, ref in enumerate(outs)
                for u in range(6)
            ]
            for ref, u, arrays in values:
                for k, v in enumerate(arrays):
                    ref[k, i, u] = v
            return carry

        lax.fori_loop(0, count, position, 0)


def columns(low, high, up, down, after=(), held=(), ranges=None):
    ranges = ranges or [(0, low.shape[1])]
    outs = pl.pallas_call(
        lambda *refs: columns_kernel(ranges, *refs[:4], *refs[-2 * len(ranges) :]),
        in_specs=[VMEM] * 4 + [ANY] * (len(after) + len(held)),
        out_specs=(ANY,) * len(held) + (VMEM,) * (2 * len(ranges)),
        out_shape=tuple(jax.ShapeDtypeStruct(h.shape, F32) for h in held)
        + tuple(jax.ShapeDtypeStruct((4, n, 6, 8, 128), F32) for _, n in ranges for _ in range(2)),
        input_output_aliases={4 + len(after) + k: k for k in range(len(held))},
        compiler_params=pltpu.CompilerParams(vmem_limit_bytes=VMEM_LIMIT),
        cost_estimate=pl.CostEstimate(flops=0, bytes_accessed=low.shape[1] * 800000, transcendentals=0),
        name="columns",
    )(low, high, up, down, *after, *held)
    return outs[len(held) :], outs[: len(held)]


def assemble(tile, p, u, first_half, second_half, left, right):
    pieces = [ref[k, p, u] for k in range(4) for ref in (left, first_half, second_half, right)]
    whole = swap_bits(pieces, [(1, 4), (0, 3)])
    return [jnp.where(tile.inside, v, 0.0) for v in whole]


def quarters(arrays):
    lane = lanes()
    merged = []
    for k in range(8):
        merged.append(jnp.where(lane < 64, roll(arrays[k], -40), roll(arrays[k + 8], 24)))
    merged = [
        jnp.where((lane >> 4) % 2 == 0, merged[k], roll(merged[k + 2], 16)) for k in (0, 1, 4, 5)
    ]
    merged = swap_bits(merged, [(1, 5), (0, 3)])
    return [[merged[2 * ry + rz] for rz in range(2)] for ry in range(2)]


def core_rows(arrays):
    lane = lanes()
    merged = [jnp.where(lane < 64, roll(arrays[k], -40), roll(arrays[k + 4], 24)) for k in range(4)]
    merged = [jnp.where((lane >> 4) % 2 == 0, merged[k], roll(merged[k + 1], 16)) for k in (0, 2)]
    return swap_bits(merged, [(0, 5)])


class Tile:
    def __init__(self, scalars):
        lane, row = lanes(), rows()
        y = EDGE * scalars[3] - RIM + 8 * (lane // 32)
        z = EDGE * scalars[4] - RIM + lane % 32
        self.inside = (y >= 0) & (y < 128) & (z >= 0) & (z < 256)
        self.below_top, self.above_bottom = row < 7, row > 0

    def around(self, load, f, xp, ys):
        mid = load(f, xp, ys)
        total = roll(mid, -1) + roll(mid, 1)
        total = total + (load(f, xp, ys + 1) if ys < 7 else roll(load(f, xp, 0), -32))
        total = total + (load(f, xp, ys - 1) if ys > 0 else roll(load(f, xp, 7), 32))
        other = load(f, 1 - xp, ys)
        if xp == 0:
            far = jnp.where(self.above_bottom, roll(other, 1, 0), 0.0)
        else:
            far = jnp.where(self.below_top, roll(other, -1, 0), 0.0)
        return total + (other + far), mid

    def tendency(self, load, xp, ys):
        around_p, p = self.around(load, 0, xp, ys)
        around_v, v = self.around(load, 1, xp, ys)
        reaction = (1.0 - p) * (v * v)
        rate_p = 0.2 * around_p + (reaction - 1.24 * p)
        rate_v = 0.1 * around_v + (reaction - 0.7 * v)
        return (jnp.where(self.inside, rate_p, 0.0), jnp.where(self.inside, rate_v, 0.0)), (p, v)


CELLS = [(xp, ys) for ys in range(8) for xp in range(2)]
FIELD = (2, 2, 8, 8, 128)


def reader(ref, *at):
    return lambda f, xp, ys: ref[at + (f, xp, ys)]


def sweep_kernel(first, begin, count, skipped, scalars, *refs):
    halo, (out_ref, *start_ref) = refs[:4], refs[4 + skipped : -6]
    old, one, two, ahead, rate, base = refs[-6:]
    tile = Tile(scalars)

    def position(at, carry):
        for array in range(3):
            both = [assemble(tile, begin + at, 2 * array + f, *halo) for f in range(2)]
            for f in range(2):
                for (xp, ys), v in zip(CELLS, both[f], strict=True):
                    old[array, f, xp, ys] = v

        for ref in start_ref:

            @pl.when(at == 0)
            def _(ref=ref):
                ref[...] = old[0]

        for xp, ys in CELLS:
            f0, y0 = tile.tendency(reader(old, 0), xp, ys)
            f1, _ = tile.tendency(reader(old, 1), xp, ys)
            f2, _ = tile.tendency(reader(old, 2), xp, ys)
            for f in range(2):
                one[f, xp, ys] = y0[f] + (5 * H / 24) * f0[f] + ((H / 3) * f1[f] - (H / 24) * f2[f])
                base[f, xp, ys] = (H / 6) * (f1[f] + f2[f]) - (5 * H / 6) * f0[f]
                ahead[f, xp, ys] = y0[f] + H * f0[f]
        for xp, ys in CELLS:
            r1, _ = tile.tendency(reader(one), xp, ys)
            for f in range(2):
                correction = base[f, xp, ys] + (H / 2) * r1[f]
                base[f, xp, ys] = correction
                two[f, xp, ys] = ahead[f, xp, ys] + correction
                rate[f, xp, ys] = r1[f]
        for xp, ys in CELLS:
            r2, _ = tile.tendency(reader(two), xp, ys)
            for f in range(2):
                r1 = rate[f, xp, ys]
                one[f, xp, ys] = (H / 3) * r1 - (H / 24) * r2[f]
                ahead[f, xp, ys] = (H / 6) * (r1 + r2[f])
        out_ref[at, 0] = base[...]
        out_ref[at, 1] = one[...]
        out_ref[at, 2] = ahead[...]
        return carry

    lax.fori_loop(0, count, position, 0)


def sweep(scalars, halo, first, begin, count, after=(), held=()):
    field = pltpu.VMEM(FIELD, F32)
    start = first == begin == 0
    out = pl.pallas_call(
        functools.partial(sweep_kernel, first, begin, count, len(after) + 2 * len(held)),
        in_specs=[SMEM] + [VMEM] * 4 + [ANY] * (len(after) + len(held)),
        out_specs=(ANY,) * len(held) + (VMEM,) * (1 + start),
        scratch_shapes=[pltpu.VMEM((3,) + FIELD, F32)] + [field] * 5,
        out_shape=tuple(jax.ShapeDtypeStruct(h.shape, F32) for h in held)
        + (jax.ShapeDtypeStruct((count, 3) + FIELD, F32),)
        + (jax.ShapeDtypeStruct(FIELD, F32),) * start,
        input_output_aliases={5 + len(after) + k: k for k in range(len(held))},
        compiler_params=pltpu.CompilerParams(vmem_limit_bytes=VMEM_LIMIT),
        cost_estimate=pl.CostEstimate(flops=count * 5 * 32 * 1024 * 40, bytes_accessed=count * 1200000, transcendentals=0),
        name=f"sweep_{first + begin}",
    )(scalars, *halo, *after, *held)
    return out[len(held) :], out[: len(held)]


def pack_values(loads):
    values = {}
    for array, load in enumerate(loads):
        for f in range(2):
            for xp in range(2):
                for ry, v in enumerate(core_rows([load(f, xp, ys) for ys in range(8)])):
                    values[ry * 12 + array * 4 + f * 2 + xp] = v
    return values


def put(out_ref, scalars, p, values):
    base = lax.rem(scalars[0] + p, SLABS) * SLAB_ROWS
    for r, v in values.items():
        out_ref[pl.ds(base + r, 8, stride=24)] = v


def pack_kernel(first, scalars, raw, *refs):
    out_ref = refs[-1]
    if first > 0:
        out_ref[...] = refs[0][...]

    def position(i, carry):
        put(out_ref, scalars, first + i, pack_values([reader(raw, i, array) for array in range(3)]))
        return carry

    lax.fori_loop(0, raw.shape[0], position, 0)


def pack(scalars, first, raw, earlier=(), after=(), held=()):
    out = pl.pallas_call(
        functools.partial(pack_kernel, first),
        in_specs=[SMEM, VMEM] + [VMEM] * len(earlier) + [ANY] * (len(after) + len(held)),
        out_specs=(ANY,) * len(held) + (VMEM,),
        out_shape=tuple(jax.ShapeDtypeStruct(h.shape, F32) for h in held)
        + (jax.ShapeDtypeStruct((SLABS * SLAB_ROWS, 128), F32),),
        input_output_aliases={2 + len(earlier) + len(after) + k: k for k in range(len(held))},
        compiler_params=pltpu.CompilerParams(vmem_limit_bytes=VMEM_LIMIT),
        cost_estimate=pl.CostEstimate(flops=6000000, bytes_accessed=3000000, transcendentals=0),
        name=f"pack_{first}",
    )(scalars, raw, *earlier, *after, *held)
    return out[-1], out[:-1]


def chain_kernel(first, count, parts, scalars, *refs):
    tile = Tile(scalars)
    last = first + count >= SLABS
    z, late, corr, one, two, ahead, next_z, next_late = refs[-8:]
    swept, refs = refs[:parts], refs[parts:-8]
    take_first = scalars[1] > 0
    if first == 0:
        start_ref, refs = refs[0], refs[1:]
        z[...] = start_ref[...]
    else:
        for k, ref in enumerate((z, late, corr)):
            both = [assemble(tile, 0, 2 * k + f, *refs[:4]) for f in range(2)]
            for f in range(2):
                for (xp, ys), v in zip(CELLS, both[f], strict=True):
                    ref[f, xp, ys] = v
        refs = refs[4:]
    raw = refs[-1] if last else refs[0]

    def step(at, sweeps=None, j=None):
        final = sweeps is None
        p = first + at
        reset = (p == 0) | ((p == 1) & take_first)
        for xp, ys in CELLS:
            fl, l = tile.tendency(reader(late), xp, ys)
            f0, y0 = tile.tendency(reader(z), xp, ys)
            for f in range(2):
                next_late[f, xp, ys] = jnp.where(reset, y0[f], l[f] + H * fl[f] + corr[f, xp, ys])
                g = y0[f] + H * f0[f]
                ahead[f, xp, ys] = g
                if final:
                    one[f, xp, ys] = y0[f] + (H / 2) * f0[f]
                    two[f, xp, ys] = (-H / 2) * f0[f]
                else:
                    next_z[f, xp, ys] = g + sweeps[j, 0, f, xp, ys]
                    one[f, xp, ys] = y0[f] + (5 * H / 24) * f0[f] + sweeps[j, 1, f, xp, ys]
                    two[f, xp, ys] = sweeps[j, 2, f, xp, ys] - (5 * H / 6) * f0[f]
        for xp, ys in CELLS:
            f1, _ = tile.tendency(reader(one), xp, ys)
            for f in range(2):
                c = two[f, xp, ys] + (H / 2) * f1[f]
                corr[f, xp, ys] = c
                two[f, xp, ys] = ahead[f, xp, ys] + c
        late[...] = next_late[...]
        if not final:
            z[...] = next_z[...]
        raw[at, 0] = next_late[...]
        raw[at, 1] = one[...]
        raw[at, 2] = two[...]

    at = 0
    for ref in swept:

        def looped(j, carry, at=at, ref=ref):
            step(at + j, ref, j)
            return carry

        lax.fori_loop(0, ref.shape[0], looped, 0)
        at += ref.shape[0]

    if not last:
        _, low_ref, high_ref = refs
        for k, ref in enumerate((z, late, corr)):
            both = [quarters([ref[f, xp, ys] for xp, ys in CELLS]) for f in range(2)]
            for f in range(2):
                for ry, half_ref in enumerate((low_ref, high_ref)):
                    for rz in range(2):
                        half_ref[rz, 0, 2 * k + f] = both[f][ry][rz]
        return

    step(count)
    for xp, ys in CELLS:
        fl, l = tile.tendency(reader(late), xp, ys)
        for f in range(2):
            raw[count + 1, 0, f, xp, ys] = l[f] + H * fl[f] + corr[f, xp, ys]
    conv_one, conv_two = scalars[1] > 0, scalars[2] > 0
    earlier, out_ref, _ = refs
    out_ref[...] = earlier[...]

    def pack_at(i, carry):
        put(out_ref, scalars, first + i, pack_values([reader(raw, i, array) for array in range(3)]))
        return carry

    lax.fori_loop(0, count, pack_at, 0)

    @pl.when(conv_one)
    def _():
        put(out_ref, scalars, 0, pack_values([reader(raw, count, array) for array in range(3)]))

    @pl.when(conv_two)
    def _():
        at = jnp.where(conv_one, count + 1, count)
        values = pack_values([reader(raw, at, 0)])
        newest = {ry * 12 + array * 4 + k: values[ry * 12 + k] for ry in range(2) for array in range(3) for k in range(4)}
        put(out_ref, scalars, jnp.where(conv_one, 1, 0), newest)


def chain(scalars, first, count, swept, inputs):
    last = first + count >= SLABS
    if last:
        out_shape = jax.ShapeDtypeStruct((SLABS * SLAB_ROWS, 128), F32)
        scratch = [pltpu.VMEM((count + 2, 3) + FIELD, F32)]
    else:
        out_shape = (jax.ShapeDtypeStruct((count, 3) + FIELD, F32),)
        out_shape += (jax.ShapeDtypeStruct((2, 1, 6, 8, 128), F32),) * 2
        scratch = []
    return pl.pallas_call(
        functools.partial(chain_kernel, first, count, len(swept)),
        in_specs=[SMEM] + [VMEM] * (len(swept) + len(inputs)),
        out_specs=VMEM if last else (VMEM,) * 3,
        scratch_shapes=scratch + [pltpu.VMEM(FIELD, F32)] * 8,
        out_shape=out_shape,
        compiler_params=pltpu.CompilerParams(vmem_limit_bytes=VMEM_LIMIT),
        cost_estimate=pl.CostEstimate(flops=count * 3 * 32 * 1024 * 40, bytes_accessed=count * 500000, transcendentals=0),
        name=f"chain_{first}",
    )(scalars, *swept, *inputs)


def body(slab_starts, slab_nodes, first_slab, converged):
    ti, tj = own_tile()
    scalars = jnp.stack([first_slab[0], converged[0], converged[1], ti.astype(jnp.int32), tj.astype(jnp.int32)])
    chunks = spread(slab_starts[0], slab_nodes[0])
    tiles = lax.all_to_all(chunks.reshape(128, 24, 128), AXES, 0, 0, tiled=True).reshape(SLABS * SLAB_ROWS, 128)

    half_a, half_b = deal(scalars, tiles)

    rows = rows_beside(*half_a)
    columns_a, half_b = columns(*half_a, *rows, held=half_b)
    beside = columns_beside(columns_a)
    rows = rows_beside(*half_b)
    (low_b, high_b, *columns_c), _ = columns(*half_b, *rows, after=beside, ranges=[(0, 6), (6, 4)])
    halo_b = [low_b, high_b, *columns_beside((low_b, high_b))]
    (swept, start), columns_c = sweep(scalars, [*columns_a, *beside], 0, 0, 6, after=[low_b], held=columns_c)
    halo_c = [*columns_c, *columns_beside(columns_c)]
    raw, low, high = chain(scalars, *BLOCKS[0], [swept], [start])

    up = from_neighbour(high, -1, 0)
    out, (low,) = pack(scalars, 0, raw, after=[high], held=[low])
    down = from_neighbour(low, 1, 0)
    (first,), _ = sweep(scalars, halo_b, 6, 0, 2, after=[low])
    inside, _ = columns(low, high, up, down, after=[first])
    left = from_neighbour(inside[1], 0, -1)
    (second,), (low_half,) = sweep(scalars, halo_b, 6, 2, 3, after=[inside[1]], held=[inside[0]])
    right = from_neighbour(low_half, 0, 1)
    (third,), _ = sweep(scalars, halo_b, 6, 5, 1, after=[low_half])
    raw, low, high = chain(scalars, *BLOCKS[1], [first, second, third], [low_half, inside[1], left, right])

    up = from_neighbour(high, -1, 0)
    (first,), (low,) = sweep(scalars, halo_c, 12, 0, 2, after=[high], held=[low])
    down = from_neighbour(low, 1, 0)
    out, _ = pack(scalars, 6, raw, [out], after=[low])
    inside, _ = columns(low, high, up, down, after=[out])
    left = from_neighbour(inside[1], 0, -1)
    (second,), (low_half,) = sweep(scalars, halo_c, 12, 2, 2, after=[inside[1]], held=[inside[0]])
    right = from_neighbour(low_half, 0, 1)
    out = chain(scalars, *BLOCKS[2], [first, second], [low_half, inside[1], left, right, out])
    out = lax.all_to_all(out.reshape(128, 24, 128), AXES, 0, 0, tiled=True)
    starts, nodes = collect(out.reshape(128 * 24, 128))
    return starts[None], nodes[None]


def solution(mesh):
    slab_spec = P("tm", None, "space", None, None)
    node_spec = P("tm", None, None, "space", None, None)
    return jax.shard_map(
        body,
        mesh=mesh,
        in_specs=(slab_spec, node_spec, P(), P()),
        out_specs=(slab_spec, node_spec),
        check_vma=False,
    )
```

```python
import functools

import jax
import jax.numpy as jnp
from jax import lax
from jax.experimental import pallas as pl
from jax.experimental.pallas import tpu as pltpu
from jax.sharding import PartitionSpec as P

SLABS = 16
TILES_Y = 8
TILES_Z = 16
EDGE = 16
RIM = 8
BLOCKS = ((0, 6), (6, 6), (12, 4))
SETS = ((0, 6), (6, 10))
H = 0.5
AXES = ("tm", "space")
F32 = jnp.float32
VMEM_LIMIT = 40 * 1024 * 1024
SHAPE = (8, 128)
VMEM = pl.BlockSpec(memory_space=pltpu.VMEM)
SMEM = pl.BlockSpec(memory_space=pltpu.SMEM)
ANY = pl.BlockSpec(memory_space=pl.ANY)
HBM = pl.BlockSpec(memory_space=pltpu.HBM)
SLAB_ROWS = 192


def device_of(i, j):
    i, j = i % TILES_Y, j % TILES_Z
    zb, x = (0, i) if i < 4 else (1, 7 - i)
    cj = j // 2
    core = (j % 2) ^ (cj % 2)
    za, y = (0, cj) if cj < 4 else (1, 7 - cj)
    zl = za ^ zb
    return (y * 4 + za * 2 + core) * 8 + zl * 4 + x


def own_tile():
    tm, space = lax.axis_index("tm"), lax.axis_index("space")
    y, za, core = tm // 4, (tm // 2) % 2, tm % 2
    zl, x = space // 4, space % 4
    zb = za ^ zl
    ti = jnp.where(zb == 0, x, 7 - x)
    cj = jnp.where(za == 0, y, 7 - y)
    return ti, 2 * cj + (core ^ (cj % 2))


def roll(v, by, axis=1):
    by %= v.shape[axis]
    return v if by == 0 else pltpu.roll(v, by, axis)


def lanes():
    return lax.broadcasted_iota(jnp.int32, SHAPE, 1)


def rows():
    return lax.broadcasted_iota(jnp.int32, SHAPE, 0)


def swap_bits(arrays, pairs):
    arrays, lane = list(arrays), lanes()
    for index_bit, lane_bit in pairs:
        step, low = 1 << lane_bit, (lane >> lane_bit) % 2 == 0
        across = lane ^ step
        for a in range(len(arrays)):
            b = a | (1 << index_bit)
            if a != b:
                u, v = arrays[a], arrays[b]
                moved = jnp.where(low, v, u)
                moved = roll(moved, 64) if step == 64 else jnp.take_along_axis(moved, across, axis=1)
                arrays[a] = jnp.where(low, u, moved)
                arrays[b] = jnp.where(low, moved, v)
    return arrays


def turn_blocks(arrays, width):
    n, block = len(arrays), lanes() // width
    arrays = [roll(arrays[-k % n], width * (-k % n)) for k in range(n)]
    step = 1
    while step < n:
        here = block // step % 2 == 0
        arrays = [jnp.where(here, arrays[k], arrays[(k - step) % n]) for k in range(n)]
        step *= 2
    return [roll(v, -width * k) for k, v in enumerate(arrays)]


def turn_pairs(v):
    v = roll(v, 4, 0)
    return jnp.where(rows() // 2 % 2 == 0, roll(v, -2, 0), roll(v, 2, 0))


def spread_kernel(starts_ref, nodes_ref, out_ref, planes, arrived):
    def copies(u):
        source = starts_ref if u < 2 else nodes_ref.at[u // 2 - 1]
        return [
            pltpu.make_async_copy(
                source.at[u % 2, xp, :, pl.ds(128 * half, 128)], planes.at[u, xp, half], arrived.at[4 * u + 2 * xp + half]
            )
            for xp in range(2)
            for half in range(2)
        ]

    def arrival(u):
        for xp in range(2):
            for half in range(2):
                here = planes.at[u, xp, half]
                pltpu.make_async_copy(here, here, arrived.at[4 * u + 2 * xp + half]).wait()

    for u in range(6):
        for copy in copies(u):
            copy.start()

    def unit(u):
        row = u // 2 * 4 + u % 2 * 2
        for half in range(2):
            found = []
            for upper in range(2):
                loads = [
                    planes[u, xp, half, pl.ds(64 * upper + ys, 8, stride=8)] for ys in range(8) for xp in range(2)
                ]
                for k, v in enumerate(turn_blocks(loads, 8)):
                    tj, rz = 8 * half + k // 2, k % 2
                    at = device_of(7 if upper else 0, tj) * 24 + rz
                    found.append((at, turn_pairs(v) if upper else v))
            for at, v in found:
                out_ref[pl.ds(at + row, 8, stride=12)] = v

    def units(u, carry):
        arrival(u)
        unit(u)
        return carry

    lax.fori_loop(0, 6, units, 0)


def spread(starts, nodes):
    return pl.pallas_call(
        spread_kernel,
        in_specs=[HBM, HBM],
        out_specs=VMEM,
        out_shape=jax.ShapeDtypeStruct((128 * 24, 128), F32),
        scratch_shapes=[pltpu.VMEM((6, 2, 2, 128, 128), F32), pltpu.SemaphoreType.DMA((24,))],
        compiler_params=pltpu.CompilerParams(vmem_limit_bytes=62 * 1024 * 1024),
        name="spread",
    )(starts, nodes)


def collect_kernel(in_ref, starts_ref, nodes_ref, planes, left):
    def unit(u, carry):
        found = []
        for half in range(2):
            for upper in range(2):
                loads = []
                for t in range(8):
                    device = device_of(7 if upper else 0, 8 * half + t)
                    v = in_ref[pl.ds(device * 24 + u, 8, stride=12)]
                    loads.append(turn_pairs(v) if upper else v)
                for ys, v in enumerate(turn_blocks(loads, 16)):
                    found.append((half, 64 * upper + ys, v))
        for half, at, v in found:
            planes[u, half, pl.ds(at, 8, stride=8)] = v
        return carry

    def copies(array):
        target = starts_ref if array == 0 else nodes_ref.at[array - 1]
        return [
            pltpu.make_async_copy(
                planes.at[4 * array + 2 * f + xp, half],
                target.at[f, xp, :, pl.ds(128 * half, 128)],
                left.at[8 * array + 4 * f + 2 * xp + half],
            )
            for f in range(2)
            for xp in range(2)
            for half in range(2)
        ]

    def array_at(k, carry):
        lax.fori_loop(4 * k, 4 * k + 4, unit, 0)
        for n in range(3):

            @pl.when(k == n)
            def _(n=n):
                for copy in copies(n):
                    copy.start()

        return carry

    lax.fori_loop(0, 3, array_at, 0)
    for n in range(3):
        for copy in copies(n):
            copy.wait()


def collect(tiles):
    return pl.pallas_call(
        collect_kernel,
        out_shape=(
            jax.ShapeDtypeStruct((2, 2, 128, 256), F32),
            jax.ShapeDtypeStruct((2, 2, 2, 128, 256), F32),
        ),
        in_specs=[VMEM],
        out_specs=(ANY, ANY),
        scratch_shapes=[pltpu.VMEM((12, 2, 128, 128), F32), pltpu.SemaphoreType.DMA((24,))],
        compiler_params=pltpu.CompilerParams(vmem_limit_bytes=VMEM_LIMIT),
        name="collect",
    )(tiles)


def deal_kernel(scalars, in_ref, *out_refs):
    for b, (first, count) in enumerate(SETS):

        def position(i, carry, b=b, first=first):
            base = lax.rem(scalars[0] + (first + i), SLABS) * SLAB_ROWS
            parts = [(u, ry, rz) for u in range(6) for ry in range(2) for rz in range(2)]
            values = [in_ref[pl.ds(base + ry * 12 + 2 * u + rz, 8, stride=24)] for u, ry, rz in parts]
            for (u, ry, rz), v in zip(parts, values, strict=True):
                out_refs[2 * b + ry][rz, i, u] = v
            return carry

        lax.fori_loop(0, count, position, 0)


def deal(scalars, tiles):
    outs = pl.pallas_call(
        deal_kernel,
        in_specs=[SMEM, VMEM],
        out_specs=(VMEM,) * (2 * len(SETS)),
        out_shape=tuple(jax.ShapeDtypeStruct((2, n, 6, 8, 128), F32) for _, n in SETS for _ in range(2)),
        compiler_params=pltpu.CompilerParams(vmem_limit_bytes=VMEM_LIMIT),
        cost_estimate=pl.CostEstimate(flops=0, bytes_accessed=3000000, transcendentals=0),
        name="deal",
    )(scalars, tiles)
    return [outs[2 * b : 2 * b + 2] for b in range(len(SETS))]


def from_neighbour(payload, di, dj):
    pairs = [(device_of(i + di, j + dj), device_of(i, j)) for i in range(TILES_Y) for j in range(TILES_Z)]
    return lax.ppermute(payload, AXES, pairs)


def rows_beside(low, high):
    return from_neighbour(high, -1, 0), from_neighbour(low, 1, 0)


def columns_beside(columns):
    return from_neighbour(columns[1], 0, -1), from_neighbour(columns[0], 0, 1)


def columns_kernel(low, high, up, down, *refs):
    def position(i, carry):
        values = [
            (ref, u, swap_bits([r[rz, i, u] for r in (up, low, high, down)], [(1, 6), (0, 5)]))
            for rz, ref in enumerate(refs[-2:])
            for u in range(6)
        ]
        for ref, u, arrays in values:
            for k, v in enumerate(arrays):
                ref[k, i, u] = v
        return carry

    lax.fori_loop(0, refs[-1].shape[1], position, 0)


def columns(low, high, up, down, after=(), held=()):
    n = low.shape[1]
    outs = pl.pallas_call(
        lambda *refs: columns_kernel(*refs[:4], *refs[-2:]),
        in_specs=[VMEM] * 4 + [ANY] * (len(after) + len(held)),
        out_specs=(ANY,) * len(held) + (VMEM,) * 2,
        out_shape=tuple(jax.ShapeDtypeStruct(h.shape, F32) for h in held)
        + (jax.ShapeDtypeStruct((4, n, 6, 8, 128), F32),) * 2,
        input_output_aliases={4 + len(after) + k: k for k in range(len(held))},
        compiler_params=pltpu.CompilerParams(vmem_limit_bytes=VMEM_LIMIT),
        cost_estimate=pl.CostEstimate(flops=0, bytes_accessed=n * 800000, transcendentals=0),
        name="columns",
    )(low, high, up, down, *after, *held)
    return outs[-2:], outs[:-2]


def assemble(tile, p, u, first_half, second_half, left, right):
    pieces = [ref[k, p, u] for k in range(4) for ref in (left, first_half, second_half, right)]
    whole = swap_bits(pieces, [(1, 4), (0, 3)])
    return [jnp.where(tile.inside, v, 0.0) for v in whole]


def quarters(arrays):
    lane = lanes()
    merged = []
    for k in range(8):
        merged.append(jnp.where(lane < 64, roll(arrays[k], -40), roll(arrays[k + 8], 24)))
    merged = [
        jnp.where((lane >> 4) % 2 == 0, merged[k], roll(merged[k + 2], 16)) for k in (0, 1, 4, 5)
    ]
    merged = swap_bits(merged, [(1, 5), (0, 3)])
    return [[merged[2 * ry + rz] for rz in range(2)] for ry in range(2)]


def core_rows(arrays):
    lane = lanes()
    merged = [jnp.where(lane < 64, roll(arrays[k], -40), roll(arrays[k + 4], 24)) for k in range(4)]
    merged = [jnp.where((lane >> 4) % 2 == 0, merged[k], roll(merged[k + 1], 16)) for k in (0, 2)]
    return swap_bits(merged, [(0, 5)])


class Tile:
    def __init__(self, scalars):
        lane, row = lanes(), rows()
        y = EDGE * scalars[3] - RIM + 8 * (lane // 32)
        z = EDGE * scalars[4] - RIM + lane % 32
        self.inside = (y >= 0) & (y < 128) & (z >= 0) & (z < 256)
        self.below_top, self.above_bottom = row < 7, row > 0

    def around(self, load, f, xp, ys):
        mid = load(f, xp, ys)
        total = roll(mid, -1) + roll(mid, 1)
        total = total + (load(f, xp, ys + 1) if ys < 7 else roll(load(f, xp, 0), -32))
        total = total + (load(f, xp, ys - 1) if ys > 0 else roll(load(f, xp, 7), 32))
        other = load(f, 1 - xp, ys)
        if xp == 0:
            far = jnp.where(self.above_bottom, roll(other, 1, 0), 0.0)
        else:
            far = jnp.where(self.below_top, roll(other, -1, 0), 0.0)
        return total + (other + far), mid

    def tendency(self, load, xp, ys):
        around_p, p = self.around(load, 0, xp, ys)
        around_v, v = self.around(load, 1, xp, ys)
        reaction = (1.0 - p) * (v * v)
        rate_p = 0.2 * around_p + (reaction - 1.24 * p)
        rate_v = 0.1 * around_v + (reaction - 0.7 * v)
        return (jnp.where(self.inside, rate_p, 0.0), jnp.where(self.inside, rate_v, 0.0)), (p, v)


CELLS = [(xp, ys) for ys in range(8) for xp in range(2)]
FIELD = (2, 2, 8, 8, 128)


def reader(ref, *at):
    return lambda f, xp, ys: ref[at + (f, xp, ys)]


def sweep_kernel(first, begin, count, scalars, *refs):
    halo, (out_ref, start_ref, old, one, two, ahead, rate, base) = refs[:4], refs[-8:]
    tile = Tile(scalars)

    def position(at, carry):
        for array in range(3):
            both = [assemble(tile, begin + at, 2 * array + f, *halo) for f in range(2)]
            for f in range(2):
                for (xp, ys), v in zip(CELLS, both[f], strict=True):
                    old[array, f, xp, ys] = v

        if first == begin == 0:

            @pl.when(at == 0)
            def _():
                start_ref[...] = old[0]

        for xp, ys in CELLS:
            f0, y0 = tile.tendency(reader(old, 0), xp, ys)
            f1, _ = tile.tendency(reader(old, 1), xp, ys)
            f2, _ = tile.tendency(reader(old, 2), xp, ys)
            for f in range(2):
                one[f, xp, ys] = y0[f] + (5 * H / 24) * f0[f] + ((H / 3) * f1[f] - (H / 24) * f2[f])
                base[f, xp, ys] = (H / 6) * (f1[f] + f2[f]) - (5 * H / 6) * f0[f]
                ahead[f, xp, ys] = y0[f] + H * f0[f]
        for xp, ys in CELLS:
            r1, _ = tile.tendency(reader(one), xp, ys)
            for f in range(2):
                correction = base[f, xp, ys] + (H / 2) * r1[f]
                base[f, xp, ys] = correction
                two[f, xp, ys] = ahead[f, xp, ys] + correction
                rate[f, xp, ys] = r1[f]
        for xp, ys in CELLS:
            r2, _ = tile.tendency(reader(two), xp, ys)
            for f in range(2):
                r1 = rate[f, xp, ys]
                one[f, xp, ys] = (H / 3) * r1 - (H / 24) * r2[f]
                ahead[f, xp, ys] = (H / 6) * (r1 + r2[f])
        out_ref[at, 0] = base[...]
        out_ref[at, 1] = one[...]
        out_ref[at, 2] = ahead[...]
        return carry

    lax.fori_loop(0, count, position, 0)


def sweep(scalars, halo, first, begin, count, after=()):
    field = pltpu.VMEM(FIELD, F32)
    return pl.pallas_call(
        functools.partial(sweep_kernel, first, begin, count),
        in_specs=[SMEM] + [VMEM] * 4 + [ANY] * len(after),
        out_specs=(VMEM,) * 2,
        scratch_shapes=[pltpu.VMEM((3,) + FIELD, F32)] + [field] * 5,
        out_shape=(jax.ShapeDtypeStruct((count, 3) + FIELD, F32), jax.ShapeDtypeStruct(FIELD, F32)),
        compiler_params=pltpu.CompilerParams(vmem_limit_bytes=VMEM_LIMIT),
        cost_estimate=pl.CostEstimate(flops=count * 5 * 32 * 1024 * 40, bytes_accessed=count * 1200000, transcendentals=0),
        name=f"sweep_{first + begin}",
    )(scalars, *halo, *after)


def pack_values(loads):
    values = {}
    for array, load in enumerate(loads):
        for f in range(2):
            for xp in range(2):
                for ry, v in enumerate(core_rows([load(f, xp, ys) for ys in range(8)])):
                    values[ry * 12 + array * 4 + f * 2 + xp] = v
    return values


def put(out_ref, scalars, p, values):
    base = lax.rem(scalars[0] + p, SLABS) * SLAB_ROWS
    for r, v in values.items():
        out_ref[pl.ds(base + r, 8, stride=24)] = v


def pack_kernel(first, scalars, raw, *refs):
    out_ref = refs[-1]
    if first > 0:
        out_ref[...] = refs[0][...]

    def position(i, carry):
        put(out_ref, scalars, first + i, pack_values([reader(raw, i, array) for array in range(3)]))
        return carry

    lax.fori_loop(0, raw.shape[0], position, 0)


def pack(scalars, first, raw, earlier=(), after=()):
    return pl.pallas_call(
        functools.partial(pack_kernel, first),
        in_specs=[SMEM, VMEM] + [VMEM] * len(earlier) + [ANY] * len(after),
        out_specs=VMEM,
        out_shape=jax.ShapeDtypeStruct((SLABS * SLAB_ROWS, 128), F32),
        compiler_params=pltpu.CompilerParams(vmem_limit_bytes=VMEM_LIMIT),
        cost_estimate=pl.CostEstimate(flops=6000000, bytes_accessed=3000000, transcendentals=0),
        name=f"pack_{first}",
    )(scalars, raw, *earlier, *after)


def chain_kernel(first, count, scalars, *refs):
    tile = Tile(scalars)
    last = first + count >= SLABS
    z, late, corr, one, two, ahead, next_z, next_late = refs[-8:]
    parts = 1 if first == BLOCKS[1][0] else 2
    swept, refs = refs[:parts], refs[parts:-8]
    take_first = scalars[1] > 0
    if first == 0:
        start_ref, refs = refs[0], refs[1:]
        z[...] = start_ref[...]
    else:
        for k, ref in enumerate((z, late, corr)):
            both = [assemble(tile, 0, 2 * k + f, *refs[:4]) for f in range(2)]
            for f in range(2):
                for (xp, ys), v in zip(CELLS, both[f], strict=True):
                    ref[f, xp, ys] = v
        refs = refs[4:]
    raw = refs[-1] if last else refs[0]

    def step(at, sweeps=None, j=None):
        final = sweeps is None
        p = first + at
        reset = (p == 0) | ((p == 1) & take_first)
        for xp, ys in CELLS:
            fl, l = tile.tendency(reader(late), xp, ys)
            f0, y0 = tile.tendency(reader(z), xp, ys)
            for f in range(2):
                next_late[f, xp, ys] = jnp.where(reset, y0[f], l[f] + H * fl[f] + corr[f, xp, ys])
                g = y0[f] + H * f0[f]
                ahead[f, xp, ys] = g
                if final:
                    one[f, xp, ys] = y0[f] + (H / 2) * f0[f]
                    two[f, xp, ys] = (-H / 2) * f0[f]
                else:
                    next_z[f, xp, ys] = g + sweeps[j, 0, f, xp, ys]
                    one[f, xp, ys] = y0[f] + (5 * H / 24) * f0[f] + sweeps[j, 1, f, xp, ys]
                    two[f, xp, ys] = sweeps[j, 2, f, xp, ys] - (5 * H / 6) * f0[f]
        for xp, ys in CELLS:
            f1, _ = tile.tendency(reader(one), xp, ys)
            for f in range(2):
                c = two[f, xp, ys] + (H / 2) * f1[f]
                corr[f, xp, ys] = c
                two[f, xp, ys] = ahead[f, xp, ys] + c
        late[...] = next_late[...]
        if not final:
            z[...] = next_z[...]
        raw[at, 0] = next_late[...]
        raw[at, 1] = one[...]
        raw[at, 2] = two[...]

    at = 0
    for ref in swept:

        def looped(j, carry, at=at, ref=ref):
            step(at + j, ref, j)
            return carry

        lax.fori_loop(0, ref.shape[0], looped, 0)
        at += ref.shape[0]

    if not last:
        _, low_ref, high_ref = refs
        for k, ref in enumerate((z, late, corr)):
            both = [quarters([ref[f, xp, ys] for xp, ys in CELLS]) for f in range(2)]
            for f in range(2):
                for ry, half_ref in enumerate((low_ref, high_ref)):
                    for rz in range(2):
                        half_ref[rz, 0, 2 * k + f] = both[f][ry][rz]
        return

    step(count)
    for xp, ys in CELLS:
        fl, l = tile.tendency(reader(late), xp, ys)
        for f in range(2):
            raw[count + 1, 0, f, xp, ys] = l[f] + H * fl[f] + corr[f, xp, ys]
    conv_one, conv_two = scalars[1] > 0, scalars[2] > 0
    earlier, out_ref, _ = refs
    out_ref[...] = earlier[...]

    def pack_at(i, carry):
        put(out_ref, scalars, first + i, pack_values([reader(raw, i, array) for array in range(3)]))
        return carry

    lax.fori_loop(0, count, pack_at, 0)

    @pl.when(conv_one)
    def _():
        put(out_ref, scalars, 0, pack_values([reader(raw, count, array) for array in range(3)]))

    @pl.when(conv_two)
    def _():
        at = jnp.where(conv_one, count + 1, count)
        values = pack_values([reader(raw, at, 0)])
        newest = {ry * 12 + array * 4 + k: values[ry * 12 + k] for ry in range(2) for array in range(3) for k in range(4)}
        put(out_ref, scalars, jnp.where(conv_one, 1, 0), newest)


def chain(scalars, first, count, inputs):
    last = first + count >= SLABS
    if last:
        out_shape = jax.ShapeDtypeStruct((SLABS * SLAB_ROWS, 128), F32)
        scratch = [pltpu.VMEM((count + 2, 3) + FIELD, F32)]
    else:
        out_shape = (jax.ShapeDtypeStruct((count, 3) + FIELD, F32),)
        out_shape += (jax.ShapeDtypeStruct((2, 1, 6, 8, 128), F32),) * 2
        scratch = []
    return pl.pallas_call(
        functools.partial(chain_kernel, first, count),
        in_specs=[SMEM] + [VMEM] * len(inputs),
        out_specs=VMEM if last else (VMEM,) * 3,
        scratch_shapes=scratch + [pltpu.VMEM(FIELD, F32)] * 8,
        out_shape=out_shape,
        compiler_params=pltpu.CompilerParams(vmem_limit_bytes=VMEM_LIMIT),
        cost_estimate=pl.CostEstimate(flops=count * 3 * 32 * 1024 * 40, bytes_accessed=count * 500000, transcendentals=0),
        name=f"chain_{first}",
    )(scalars, *inputs)


def body(slab_starts, slab_nodes, first_slab, converged):
    ti, tj = own_tile()
    scalars = jnp.stack([first_slab[0], converged[0], converged[1], ti.astype(jnp.int32), tj.astype(jnp.int32)])
    chunks = spread(slab_starts[0], slab_nodes[0])
    tiles = lax.all_to_all(chunks.reshape(128, 24, 128), AXES, 0, 0, tiled=True).reshape(SLABS * SLAB_ROWS, 128)

    half_a, half_b = deal(scalars, tiles)

    rows = rows_beside(*half_a)
    columns_a, half_b = columns(*half_a, *rows, held=half_b)
    beside = columns_beside(columns_a)
    rows = rows_beside(*half_b)
    swept, start = sweep(scalars, [*columns_a, *beside], 0, 0, 3)
    columns_b, _ = columns(*half_b, *rows, after=[swept])
    halo = [*columns_b, *columns_beside(columns_b)]
    more, _ = sweep(scalars, [*columns_a, *beside], 0, 3, 3, after=columns_b)
    raw, *state = chain(scalars, *BLOCKS[0], [swept, more, start])

    rows = rows_beside(*state)
    out = pack(scalars, 0, raw, after=state)
    inside, _ = columns(*state, *rows, after=[out])
    beside = columns_beside(inside)
    swept, _ = sweep(scalars, halo, 6, 0, 6, after=inside)
    raw, *state = chain(scalars, *BLOCKS[1], [swept, *inside, *beside])

    rows = rows_beside(*state)
    swept, _ = sweep(scalars, halo, 6, 6, 2, after=state)
    inside, _ = columns(*state, *rows, after=[swept])
    beside = columns_beside(inside)
    more, _ = sweep(scalars, halo, 6, 8, 2, after=inside)
    out = pack(scalars, 6, raw, [out], after=inside)
    out = chain(scalars, *BLOCKS[2], [swept, more, *inside, *beside, out])
    out = lax.all_to_all(out.reshape(128, 24, 128), AXES, 0, 0, tiled=True)
    starts, nodes = collect(out.reshape(128 * 24, 128))
    return starts[None], nodes[None]


def solution(mesh):
    slab_spec = P("tm", None, "space", None, None)
    node_spec = P("tm", None, None, "space", None, None)
    return jax.shard_map(
        body,
        mesh=mesh,
        in_specs=(slab_spec, node_spec, P(), P()),
        out_specs=(slab_spec, node_spec),
        check_vma=False,
    )
```

```python
import functools

import jax
import jax.numpy as jnp
from jax import lax
from jax.experimental import pallas as pl
from jax.experimental.pallas import tpu as pltpu
from jax.sharding import PartitionSpec as P

SLABS = 16
TILES_Y = 8
TILES_Z = 16
EDGE = 16
RIM = 8
BLOCKS = ((0, 6), (6, 6), (12, 4))
SETS = ((0, 6), (6, 10))
H = 0.5
AXES = ("tm", "space")
F32 = jnp.float32
VMEM_LIMIT = 40 * 1024 * 1024
SHAPE = (8, 128)
VMEM = pl.BlockSpec(memory_space=pltpu.VMEM)
SMEM = pl.BlockSpec(memory_space=pltpu.SMEM)
ANY = pl.BlockSpec(memory_space=pl.ANY)
HBM = pl.BlockSpec(memory_space=pltpu.HBM)
SLAB_ROWS = 192


def device_of(i, j):
    i, j = i % TILES_Y, j % TILES_Z
    zb, x = (0, i) if i < 4 else (1, 7 - i)
    cj = j // 2
    core = (j % 2) ^ (cj % 2)
    za, y = (0, cj) if cj < 4 else (1, 7 - cj)
    zl = za ^ zb
    return (y * 4 + za * 2 + core) * 8 + zl * 4 + x


def own_tile():
    tm, space = lax.axis_index("tm"), lax.axis_index("space")
    y, za, core = tm // 4, (tm // 2) % 2, tm % 2
    zl, x = space // 4, space % 4
    zb = za ^ zl
    ti = jnp.where(zb == 0, x, 7 - x)
    cj = jnp.where(za == 0, y, 7 - y)
    return ti, 2 * cj + (core ^ (cj % 2))


def roll(v, by, axis=1):
    by %= v.shape[axis]
    return v if by == 0 else pltpu.roll(v, by, axis)


def lanes():
    return lax.broadcasted_iota(jnp.int32, SHAPE, 1)


def rows():
    return lax.broadcasted_iota(jnp.int32, SHAPE, 0)


def swap_bits(arrays, pairs):
    arrays, lane = list(arrays), lanes()
    for index_bit, lane_bit in pairs:
        step, low = 1 << lane_bit, (lane >> lane_bit) % 2 == 0
        across = lane ^ step
        for a in range(len(arrays)):
            b = a | (1 << index_bit)
            if a != b:
                u, v = arrays[a], arrays[b]
                moved = jnp.where(low, v, u)
                moved = roll(moved, 64) if step == 64 else jnp.take_along_axis(moved, across, axis=1)
                arrays[a] = jnp.where(low, u, moved)
                arrays[b] = jnp.where(low, moved, v)
    return arrays


def turn_blocks(arrays, width):
    n, block = len(arrays), lanes() // width
    arrays = [roll(arrays[-k % n], width * (-k % n)) for k in range(n)]
    step = 1
    while step < n:
        here = block // step % 2 == 0
        arrays = [jnp.where(here, arrays[k], arrays[(k - step) % n]) for k in range(n)]
        step *= 2
    return [roll(v, -width * k) for k, v in enumerate(arrays)]


def turn_pairs(v):
    v = roll(v, 4, 0)
    return jnp.where(rows() // 2 % 2 == 0, roll(v, -2, 0), roll(v, 2, 0))


def spread_kernel(starts_ref, nodes_ref, out_ref, planes, arrived):
    def copies(u):
        source = starts_ref if u < 2 else nodes_ref.at[u // 2 - 1]
        return [
            pltpu.make_async_copy(
                source.at[u % 2, xp, :, pl.ds(128 * half, 128)], planes.at[u, xp, half], arrived.at[4 * u + 2 * xp + half]
            )
            for xp in range(2)
            for half in range(2)
        ]

    def arrival(u):
        for xp in range(2):
            for half in range(2):
                here = planes.at[u, xp, half]
                pltpu.make_async_copy(here, here, arrived.at[4 * u + 2 * xp + half]).wait()

    for u in range(6):
        for copy in copies(u):
            copy.start()

    def unit(u):
        row = u // 2 * 4 + u % 2 * 2
        for half in range(2):
            found = []
            for upper in range(2):
                loads = [
                    planes[u, xp, half, pl.ds(64 * upper + ys, 8, stride=8)] for ys in range(8) for xp in range(2)
                ]
                for k, v in enumerate(turn_blocks(loads, 8)):
                    tj, rz = 8 * half + k // 2, k % 2
                    at = device_of(7 if upper else 0, tj) * 24 + rz
                    found.append((at, turn_pairs(v) if upper else v))
            for at, v in found:
                out_ref[pl.ds(at + row, 8, stride=12)] = v

    def units(u, carry):
        arrival(u)
        unit(u)
        return carry

    lax.fori_loop(0, 6, units, 0)


def spread(starts, nodes):
    return pl.pallas_call(
        spread_kernel,
        in_specs=[HBM, HBM],
        out_specs=VMEM,
        out_shape=jax.ShapeDtypeStruct((128 * 24, 128), F32),
        scratch_shapes=[pltpu.VMEM((6, 2, 2, 128, 128), F32), pltpu.SemaphoreType.DMA((24,))],
        compiler_params=pltpu.CompilerParams(vmem_limit_bytes=62 * 1024 * 1024),
        name="spread",
    )(starts, nodes)


def collect_kernel(in_ref, starts_ref, nodes_ref, planes, left):
    def unit(u, carry):
        found = []
        for half in range(2):
            for upper in range(2):
                loads = []
                for t in range(8):
                    device = device_of(7 if upper else 0, 8 * half + t)
                    v = in_ref[pl.ds(device * 24 + u, 8, stride=12)]
                    loads.append(turn_pairs(v) if upper else v)
                for ys, v in enumerate(turn_blocks(loads, 16)):
                    found.append((half, 64 * upper + ys, v))
        for half, at, v in found:
            planes[u, half, pl.ds(at, 8, stride=8)] = v
        return carry

    def copies(array):
        target = starts_ref if array == 0 else nodes_ref.at[array - 1]
        return [
            pltpu.make_async_copy(
                planes.at[4 * array + 2 * f + xp, half],
                target.at[f, xp, :, pl.ds(128 * half, 128)],
                left.at[8 * array + 4 * f + 2 * xp + half],
            )
            for f in range(2)
            for xp in range(2)
            for half in range(2)
        ]

    def array_at(k, carry):
        lax.fori_loop(4 * k, 4 * k + 4, unit, 0)
        for n in range(3):

            @pl.when(k == n)
            def _(n=n):
                for copy in copies(n):
                    copy.start()

        return carry

    lax.fori_loop(0, 3, array_at, 0)
    for n in range(3):
        for copy in copies(n):
            copy.wait()


def collect(tiles):
    return pl.pallas_call(
        collect_kernel,
        out_shape=(
            jax.ShapeDtypeStruct((2, 2, 128, 256), F32),
            jax.ShapeDtypeStruct((2, 2, 2, 128, 256), F32),
        ),
        in_specs=[VMEM],
        out_specs=(ANY, ANY),
        scratch_shapes=[pltpu.VMEM((12, 2, 128, 128), F32), pltpu.SemaphoreType.DMA((24,))],
        compiler_params=pltpu.CompilerParams(vmem_limit_bytes=VMEM_LIMIT),
        name="collect",
    )(tiles)


def deal_kernel(scalars, in_ref, *out_refs):
    for b, (first, count) in enumerate(SETS):

        def position(i, carry, b=b, first=first):
            base = lax.rem(scalars[0] + (first + i), SLABS) * SLAB_ROWS
            parts = [(u, ry, rz) for u in range(6) for ry in range(2) for rz in range(2)]
            values = [in_ref[pl.ds(base + ry * 12 + 2 * u + rz, 8, stride=24)] for u, ry, rz in parts]
            for (u, ry, rz), v in zip(parts, values, strict=True):
                out_refs[2 * b + ry][rz, i, u] = v
            return carry

        lax.fori_loop(0, count, position, 0)


def deal(scalars, tiles):
    outs = pl.pallas_call(
        deal_kernel,
        in_specs=[SMEM, VMEM],
        out_specs=(VMEM,) * (2 * len(SETS)),
        out_shape=tuple(jax.ShapeDtypeStruct((2, n, 6, 8, 128), F32) for _, n in SETS for _ in range(2)),
        compiler_params=pltpu.CompilerParams(vmem_limit_bytes=VMEM_LIMIT),
        cost_estimate=pl.CostEstimate(flops=0, bytes_accessed=3000000, transcendentals=0),
        name="deal",
    )(scalars, tiles)
    return [outs[2 * b : 2 * b + 2] for b in range(len(SETS))]


def from_neighbour(payload, di, dj):
    pairs = [(device_of(i + di, j + dj), device_of(i, j)) for i in range(TILES_Y) for j in range(TILES_Z)]
    return lax.ppermute(payload, AXES, pairs)


def rows_beside(low, high):
    return from_neighbour(high, -1, 0), from_neighbour(low, 1, 0)


def columns_beside(columns):
    return from_neighbour(columns[1], 0, -1), from_neighbour(columns[0], 0, 1)


def columns_kernel(low, high, up, down, *refs):
    def position(i, carry):
        values = [
            (ref, u, swap_bits([r[rz, i, u] for r in (up, low, high, down)], [(1, 6), (0, 5)]))
            for rz, ref in enumerate(refs[-2:])
            for u in range(6)
        ]
        for ref, u, arrays in values:
            for k, v in enumerate(arrays):
                ref[k, i, u] = v
        return carry

    lax.fori_loop(0, refs[-1].shape[1], position, 0)


def columns(low, high, up, down, after=(), held=()):
    n = low.shape[1]
    outs = pl.pallas_call(
        lambda *refs: columns_kernel(*refs[:4], *refs[-2:]),
        in_specs=[VMEM] * 4 + [ANY] * (len(after) + len(held)),
        out_specs=(ANY,) * len(held) + (VMEM,) * 2,
        out_shape=tuple(jax.ShapeDtypeStruct(h.shape, F32) for h in held)
        + (jax.ShapeDtypeStruct((4, n, 6, 8, 128), F32),) * 2,
        input_output_aliases={4 + len(after) + k: k for k in range(len(held))},
        compiler_params=pltpu.CompilerParams(vmem_limit_bytes=VMEM_LIMIT),
        cost_estimate=pl.CostEstimate(flops=0, bytes_accessed=n * 800000, transcendentals=0),
        name="columns",
    )(low, high, up, down, *after, *held)
    return outs[-2:], outs[:-2]


def assemble(tile, p, u, first_half, second_half, left, right):
    pieces = [ref[k, p, u] for k in range(4) for ref in (left, first_half, second_half, right)]
    whole = swap_bits(pieces, [(1, 4), (0, 3)])
    return [jnp.where(tile.inside, v, 0.0) for v in whole]


def quarters(arrays):
    lane = lanes()
    merged = []
    for k in range(8):
        merged.append(jnp.where(lane < 64, roll(arrays[k], -40), roll(arrays[k + 8], 24)))
    merged = [
        jnp.where((lane >> 4) % 2 == 0, merged[k], roll(merged[k + 2], 16)) for k in (0, 1, 4, 5)
    ]
    merged = swap_bits(merged, [(1, 5), (0, 3)])
    return [[merged[2 * ry + rz] for rz in range(2)] for ry in range(2)]


def core_rows(arrays):
    lane = lanes()
    merged = [jnp.where(lane < 64, roll(arrays[k], -40), roll(arrays[k + 4], 24)) for k in range(4)]
    merged = [jnp.where((lane >> 4) % 2 == 0, merged[k], roll(merged[k + 1], 16)) for k in (0, 2)]
    return swap_bits(merged, [(0, 5)])


class Tile:
    def __init__(self, scalars):
        lane, row = lanes(), rows()
        y = EDGE * scalars[3] - RIM + 8 * (lane // 32)
        z = EDGE * scalars[4] - RIM + lane % 32
        self.inside = (y >= 0) & (y < 128) & (z >= 0) & (z < 256)
        self.below_top, self.above_bottom = row < 7, row > 0

    def around(self, load, f, xp, ys):
        mid = load(f, xp, ys)
        total = roll(mid, -1) + roll(mid, 1)
        total = total + (load(f, xp, ys + 1) if ys < 7 else roll(load(f, xp, 0), -32))
        total = total + (load(f, xp, ys - 1) if ys > 0 else roll(load(f, xp, 7), 32))
        other = load(f, 1 - xp, ys)
        if xp == 0:
            far = jnp.where(self.above_bottom, roll(other, 1, 0), 0.0)
        else:
            far = jnp.where(self.below_top, roll(other, -1, 0), 0.0)
        return total + (other + far), mid

    def tendency(self, load, xp, ys):
        around_p, p = self.around(load, 0, xp, ys)
        around_v, v = self.around(load, 1, xp, ys)
        reaction = (1.0 - p) * (v * v)
        rate_p = 0.2 * around_p + (reaction - 1.24 * p)
        rate_v = 0.1 * around_v + (reaction - 0.7 * v)
        return (rate_p, rate_v), (p, v)

    def within(self, v):
        return jnp.where(self.inside, v, 0.0)


CELLS = [(xp, ys) for ys in range(8) for xp in range(2)]
FIELD = (2, 2, 8, 8, 128)


def reader(ref, *at):
    return lambda f, xp, ys: ref[at + (f, xp, ys)]


def sweep_kernel(first, begin, count, scalars, *refs):
    halo, (out_ref, start_ref, old, one, two, ahead, rate, base) = refs[:4], refs[-8:]
    tile = Tile(scalars)

    def position(at, carry):
        for array in range(3):
            both = [assemble(tile, begin + at, 2 * array + f, *halo) for f in range(2)]
            for f in range(2):
                for (xp, ys), v in zip(CELLS, both[f], strict=True):
                    old[array, f, xp, ys] = v

        if first == begin == 0:

            @pl.when(at == 0)
            def _():
                start_ref[...] = old[0]

        for xp, ys in CELLS:
            f0, y0 = tile.tendency(reader(old, 0), xp, ys)
            f1, _ = tile.tendency(reader(old, 1), xp, ys)
            f2, _ = tile.tendency(reader(old, 2), xp, ys)
            for f in range(2):
                one[f, xp, ys] = tile.within(y0[f] + (5 * H / 24) * f0[f] + ((H / 3) * f1[f] - (H / 24) * f2[f]))
                base[f, xp, ys] = (H / 6) * (f1[f] + f2[f]) - (5 * H / 6) * f0[f]
                ahead[f, xp, ys] = y0[f] + H * f0[f]
        for xp, ys in CELLS:
            r1, _ = tile.tendency(reader(one), xp, ys)
            for f in range(2):
                correction = base[f, xp, ys] + (H / 2) * r1[f]
                base[f, xp, ys] = correction
                two[f, xp, ys] = tile.within(ahead[f, xp, ys] + correction)
                rate[f, xp, ys] = r1[f]
        for xp, ys in CELLS:
            r2, _ = tile.tendency(reader(two), xp, ys)
            for f in range(2):
                r1 = rate[f, xp, ys]
                one[f, xp, ys] = (H / 3) * r1 - (H / 24) * r2[f]
                ahead[f, xp, ys] = (H / 6) * (r1 + r2[f])
        out_ref[at, 0] = base[...]
        out_ref[at, 1] = one[...]
        out_ref[at, 2] = ahead[...]
        return carry

    lax.fori_loop(0, count, position, 0)


def sweep(scalars, halo, first, begin, count, after=()):
    field = pltpu.VMEM(FIELD, F32)
    return pl.pallas_call(
        functools.partial(sweep_kernel, first, begin, count),
        in_specs=[SMEM] + [VMEM] * 4 + [ANY] * len(after),
        out_specs=(VMEM,) * 2,
        scratch_shapes=[pltpu.VMEM((3,) + FIELD, F32)] + [field] * 5,
        out_shape=(jax.ShapeDtypeStruct((count, 3) + FIELD, F32), jax.ShapeDtypeStruct(FIELD, F32)),
        compiler_params=pltpu.CompilerParams(vmem_limit_bytes=VMEM_LIMIT),
        cost_estimate=pl.CostEstimate(flops=count * 5 * 32 * 1024 * 40, bytes_accessed=count * 1200000, transcendentals=0),
        name=f"sweep_{first + begin}",
    )(scalars, *halo, *after)


def pack_values(loads):
    values = {}
    for array, load in enumerate(loads):
        for f in range(2):
            for xp in range(2):
                for ry, v in enumerate(core_rows([load(f, xp, ys) for ys in range(8)])):
                    values[ry * 12 + array * 4 + f * 2 + xp] = v
    return values


def put(out_ref, scalars, p, values):
    base = lax.rem(scalars[0] + p, SLABS) * SLAB_ROWS
    for r, v in values.items():
        out_ref[pl.ds(base + r, 8, stride=24)] = v


def pack_kernel(first, scalars, raw, *refs):
    out_ref = refs[-1]
    if first > 0:
        out_ref[...] = refs[0][...]

    def position(i, carry):
        put(out_ref, scalars, first + i, pack_values([reader(raw, i, array) for array in range(3)]))
        return carry

    lax.fori_loop(0, raw.shape[0], position, 0)


def pack(scalars, first, raw, earlier=(), after=()):
    return pl.pallas_call(
        functools.partial(pack_kernel, first),
        in_specs=[SMEM, VMEM] + [VMEM] * len(earlier) + [ANY] * len(after),
        out_specs=VMEM,
        out_shape=jax.ShapeDtypeStruct((SLABS * SLAB_ROWS, 128), F32),
        compiler_params=pltpu.CompilerParams(vmem_limit_bytes=VMEM_LIMIT),
        cost_estimate=pl.CostEstimate(flops=6000000, bytes_accessed=3000000, transcendentals=0),
        name=f"pack_{first}",
    )(scalars, raw, *earlier, *after)


def chain_kernel(first, count, scalars, *refs):
    tile = Tile(scalars)
    last = first + count >= SLABS
    z, late, corr, one, two, ahead, next_z, next_late = refs[-8:]
    parts = 1 if first == BLOCKS[1][0] else 2
    swept, refs = refs[:parts], refs[parts:-8]
    take_first = scalars[1] > 0
    if first == 0:
        start_ref, refs = refs[0], refs[1:]
        z[...] = start_ref[...]
    else:
        for k, ref in enumerate((z, late, corr)):
            both = [assemble(tile, 0, 2 * k + f, *refs[:4]) for f in range(2)]
            for f in range(2):
                for (xp, ys), v in zip(CELLS, both[f], strict=True):
                    ref[f, xp, ys] = v
        refs = refs[4:]
    raw = refs[-1] if last else refs[0]

    def step(at, sweeps=None, j=None):
        final = sweeps is None
        p = first + at
        reset = (p == 0) | ((p == 1) & take_first)
        for xp, ys in CELLS:
            fl, l = tile.tendency(reader(late), xp, ys)
            f0, y0 = tile.tendency(reader(z), xp, ys)
            for f in range(2):
                next_late[f, xp, ys] = jnp.where(reset, y0[f], tile.within(l[f] + H * fl[f] + corr[f, xp, ys]))
                g = y0[f] + H * f0[f]
                ahead[f, xp, ys] = g
                if final:
                    one[f, xp, ys] = tile.within(y0[f] + (H / 2) * f0[f])
                    two[f, xp, ys] = (-H / 2) * f0[f]
                else:
                    next_z[f, xp, ys] = tile.within(g + sweeps[j, 0, f, xp, ys])
                    one[f, xp, ys] = tile.within(y0[f] + (5 * H / 24) * f0[f] + sweeps[j, 1, f, xp, ys])
                    two[f, xp, ys] = sweeps[j, 2, f, xp, ys] - (5 * H / 6) * f0[f]
        for xp, ys in CELLS:
            f1, _ = tile.tendency(reader(one), xp, ys)
            for f in range(2):
                c = two[f, xp, ys] + (H / 2) * f1[f]
                corr[f, xp, ys] = c
                two[f, xp, ys] = ahead[f, xp, ys] + c
        late[...] = next_late[...]
        if not final:
            z[...] = next_z[...]
        raw[at, 0] = next_late[...]
        raw[at, 1] = one[...]
        raw[at, 2] = two[...]

    at = 0
    for ref in swept:

        def looped(j, carry, at=at, ref=ref):
            step(at + j, ref, j)
            return carry

        lax.fori_loop(0, ref.shape[0], looped, 0)
        at += ref.shape[0]

    if not last:
        _, low_ref, high_ref = refs
        for k, ref in enumerate((z, late, corr)):
            both = [quarters([ref[f, xp, ys] for xp, ys in CELLS]) for f in range(2)]
            for f in range(2):
                for ry, half_ref in enumerate((low_ref, high_ref)):
                    for rz in range(2):
                        half_ref[rz, 0, 2 * k + f] = both[f][ry][rz]
        return

    step(count)
    for xp, ys in CELLS:
        fl, l = tile.tendency(reader(late), xp, ys)
        for f in range(2):
            raw[count + 1, 0, f, xp, ys] = l[f] + H * fl[f] + corr[f, xp, ys]
    conv_one, conv_two = scalars[1] > 0, scalars[2] > 0
    earlier, out_ref, _ = refs
    out_ref[...] = earlier[...]

    def pack_at(i, carry):
        put(out_ref, scalars, first + i, pack_values([reader(raw, i, array) for array in range(3)]))
        return carry

    lax.fori_loop(0, count, pack_at, 0)

    @pl.when(conv_one)
    def _():
        put(out_ref, scalars, 0, pack_values([reader(raw, count, array) for array in range(3)]))

    @pl.when(conv_two)
    def _():
        at = jnp.where(conv_one, count + 1, count)
        values = pack_values([reader(raw, at, 0)])
        newest = {ry * 12 + array * 4 + k: values[ry * 12 + k] for ry in range(2) for array in range(3) for k in range(4)}
        put(out_ref, scalars, jnp.where(conv_one, 1, 0), newest)


def chain(scalars, first, count, inputs):
    last = first + count >= SLABS
    if last:
        out_shape = jax.ShapeDtypeStruct((SLABS * SLAB_ROWS, 128), F32)
        scratch = [pltpu.VMEM((count + 2, 3) + FIELD, F32)]
    else:
        out_shape = (jax.ShapeDtypeStruct((count, 3) + FIELD, F32),)
        out_shape += (jax.ShapeDtypeStruct((2, 1, 6, 8, 128), F32),) * 2
        scratch = []
    return pl.pallas_call(
        functools.partial(chain_kernel, first, count),
        in_specs=[SMEM] + [VMEM] * len(inputs),
        out_specs=VMEM if last else (VMEM,) * 3,
        scratch_shapes=scratch + [pltpu.VMEM(FIELD, F32)] * 8,
        out_shape=out_shape,
        compiler_params=pltpu.CompilerParams(vmem_limit_bytes=VMEM_LIMIT),
        cost_estimate=pl.CostEstimate(flops=count * 3 * 32 * 1024 * 40, bytes_accessed=count * 500000, transcendentals=0),
        name=f"chain_{first}",
    )(scalars, *inputs)


def body(slab_starts, slab_nodes, first_slab, converged):
    ti, tj = own_tile()
    scalars = jnp.stack([first_slab[0], converged[0], converged[1], ti.astype(jnp.int32), tj.astype(jnp.int32)])
    chunks = spread(slab_starts[0], slab_nodes[0])
    tiles = lax.all_to_all(chunks.reshape(128, 24, 128), AXES, 0, 0, tiled=True).reshape(SLABS * SLAB_ROWS, 128)

    half_a, half_b = deal(scalars, tiles)

    rows = rows_beside(*half_a)
    columns_a, half_b = columns(*half_a, *rows, held=half_b)
    beside = columns_beside(columns_a)
    rows = rows_beside(*half_b)
    swept, start = sweep(scalars, [*columns_a, *beside], 0, 0, 3)
    columns_b, _ = columns(*half_b, *rows, after=[swept])
    halo = [*columns_b, *columns_beside(columns_b)]
    more, _ = sweep(scalars, [*columns_a, *beside], 0, 3, 3, after=columns_b)
    raw, *state = chain(scalars, *BLOCKS[0], [swept, more, start])

    rows = rows_beside(*state)
    out = pack(scalars, 0, raw, after=state)
    inside, _ = columns(*state, *rows, after=[out])
    beside = columns_beside(inside)
    swept, _ = sweep(scalars, halo, 6, 0, 6, after=inside)
    raw, *state = chain(scalars, *BLOCKS[1], [swept, *inside, *beside])

    rows = rows_beside(*state)
    swept, _ = sweep(scalars, halo, 6, 6, 2, after=state)
    inside, _ = columns(*state, *rows, after=[swept])
    beside = columns_beside(inside)
    more, _ = sweep(scalars, halo, 6, 8, 2, after=inside)
    out = pack(scalars, 6, raw, [out], after=inside)
    out = chain(scalars, *BLOCKS[2], [swept, more, *inside, *beside, out])
    out = lax.all_to_all(out.reshape(128, 24, 128), AXES, 0, 0, tiled=True)
    starts, nodes = collect(out.reshape(128 * 24, 128))
    return starts[None], nodes[None]


def solution(mesh):
    slab_spec = P("tm", None, "space", None, None)
    node_spec = P("tm", None, None, "space", None, None)
    return jax.shard_map(
        body,
        mesh=mesh,
        in_specs=(slab_spec, node_spec, P(), P()),
        out_specs=(slab_spec, node_spec),
        check_vma=False,
    )
```
